256 devices in a mesh: tok: 2 (over core), row: 8 (over x, z_lo), col: 16 (over z_hi, y).
Axes of the slice: x: 4, y: 4, z: 8 (z_hi: 4, z_lo: 2; z = z_hi * 2 + z_lo), core: 2. Of those that a mesh axis runs over, the one named last changes fastest.
Arguments:
- tokens: bfloat16 [1024, 8192], P('tok', 'col'), may hold values from -6 to 6
- gate_weight: bfloat16 [8192, 16384], P(None, ('row', 'col')), may hold values from -0.0625 to 0.0625
- up_weight: bfloat16 [8192, 16384], P(None, ('row', 'col')), may hold values from -0.0625 to 0.0625
Outputs:
- gram: float32 [8, 16384, 16, 128], P('tok', 'row', 'col')
- panel: float32 [16384, 256], P(('row', 'col'), 'tok')
The draws below stay inside these ranges and needn't reach their ends.
All inputs are finite; a program needn't handle non-finite values.
Results may differ from the reference program's by a relative error of at most 0.0046.
Values may be sent and summed in bfloat16 or wider, within the bound.
A program may use at most 64 MiB of HBM per device.

```python
import jax
import jax.numpy as jnp
from jax import lax

D = 8192
FF = 16384
PANEL = 256
TOKENS = 1024
FB = 128
N_ROW = 8
N_COL = 16


def block_levels(stream_key, shape, pieces, low, largest):
    factor_of, own = 1.0, jax.random.fold_in(stream_key, 6)
    for axis_at, parts in pieces:
        steps = jnp.exp(jax.random.uniform(jax.random.fold_in(own, axis_at), (parts,), jnp.float32, low / len(pieces), largest / len(pieces)))
        factor_of = factor_of * jnp.repeat(steps, shape[axis_at] // parts).reshape([-1 if axis == axis_at else 1 for axis in range(len(shape))])
    return factor_of


def bell_draw(key, dims, spread, most, pieces=(), kind=jnp.bfloat16):
    values = jax.random.normal(key, dims, jnp.float32) * spread
    if len(pieces) > 0:
        values = block_levels(key, dims, pieces, -0.22, 0.18) * values
    return jnp.clip(values, min=-most, max=most).astype(kind)


def setup_inputs(seed: int = 0) -> dict:
    key_of = jax.random.split(jax.random.key(seed), 4)
    tokens = bell_draw(key_of[0], (TOKENS, D), 1.0, 6.0, ((0, 2), (1, 16)))
    gate_weight = bell_draw(key_of[1], (D, FF), D ** -0.5, 0.0625, ((1, 128),))
    up_weight = bell_draw(key_of[2], (D, FF), D ** -0.5, 0.0625, ((1, 128),))
    return {"tokens": tokens, "gate_weight": gate_weight, "up_weight": up_weight}


def reference(tokens, gate_weight, up_weight):
    gate = jnp.dot(tokens.astype(jnp.float32), gate_weight.astype(jnp.float32), preferred_element_type=jnp.float32)
    up = jnp.dot(tokens.astype(jnp.float32), up_weight.astype(jnp.float32), preferred_element_type=jnp.float32)
    hidden = (jax.nn.silu(gate) * up).astype(jnp.bfloat16)
    whole = jnp.dot(hidden.T.astype(jnp.float32), hidden.astype(jnp.float32), preferred_element_type=jnp.float32)
    factor = jnp.linalg.cholesky(whole[:PANEL, :PANEL])
    panel = lax.linalg.triangular_solve(factor, whole[:, :PANEL], left_side=False, lower=True, transpose_a=True)
    grouped = whole.reshape(FF, N_ROW, N_COL, FB).transpose(1, 0, 2, 3)
    return (grouped, panel)
```

```python
import functools

import jax
import jax.numpy as jnp
from jax import lax
from jax.experimental import pallas as pl
from jax.experimental.pallas import tpu as pltpu
from jax.sharding import PartitionSpec as P

PANEL = 256
HIGH = lax.Precision.HIGHEST
MESH = pl.DeviceIdType.MESH
OFFSETS = (0, -1, 1, 2)
NT = (((1,), (1,)), ((), ()))
F32 = jnp.float32

ROWS = 512
QUARTER = 64
FIRST_Y = (256, 96)
FIRST_Z = (352, 160)
PIECES = 4
BATCHES = (2, 2, 2, 2, 2, 2, 1, 1, 1)
RATE, HOP, ISSUE, AHEAD = 49.0, 2.0, 0.12, 0.5


class Move:
    def __init__(self, link, size, needs, source=None, target=None, rows=None, target_rows=None, role=None):
        self.link, self.size, self.needs = link, size, needs
        self.source, self.target, self.rows, self.target_rows, self.role = source, target, rows, target_rows, role


def part(rows, which):
    first = (rows[2] // 2 + 15) // 16 * 16
    return (rows[0], rows[1] + first, rows[2] - first) if which == "b" else (rows[0], rows[1], first)


def token_moves():
    moves, arrivals = {}, {}

    def add(name, link, needs0, needs1, source, target, rows, target_rows=None):
        moves[name] = Move(link, rows[2], (tuple(needs0), tuple(needs1)), source, target, rows, target_rows or rows)

    def along_z(tag, rows, j, have):
        up, far_up, down, far_down = [tag + k for k in ("u1", "u2", "d1", "d2")]
        at = {h: (h, j) for h in OFFSETS}
        add(up, "u", [up], have, (at[-1], at[0]), at[-1], rows)
        add(far_up, "u", [far_up], [up], (at[2], at[-1]), at[2], part(rows, "a"))
        add(down, "d", have, [down], (at[0], at[1]), at[1], rows)
        add(far_down, "d", [down], [far_down], (at[1], at[2]), at[2], part(rows, "b"))
        return {0: list(have), -1: [up], 1: [down], 2: [far_up, far_down]}

    def along_y(tag, rows, h, have):
        right, left, far_right, far_left = [tag + k for k in ("y+1", "y-1", "y+2", "y-2")]
        at = {j: (h, j) for j in OFFSETS}
        add(right, "y+", have, have, (at[0],) * 2, at[-1], rows)
        add(left, "y-", have, have, (at[0],) * 2, at[1], rows)
        add(far_right, "y+", [right], [right], (at[-1],) * 2, at[2], part(rows, "a"))
        add(far_left, "y-", [left], [left], (at[1],) * 2, at[2], part(rows, "b"))
        return {0: list(have), -1: [right], 1: [left], 2: [far_right, far_left]}

    for tag, rows in (("q", (0, 0, QUARTER)), ("f", (None,) + FIRST_Y)):
        near = along_y(tag, rows, 0, [])
        for j in OFFSETS:
            for h, names in along_z(tag + "%d" % j, rows, j, near[j]).items():
                arrivals[tag, h, j] = names
    near = along_z("s", (None,) + FIRST_Z, 0, [])
    for h in OFFSETS:
        for j, names in along_y("s%d" % h, (None,) + FIRST_Z, h, near[h]).items():
            arrivals["s", h, j] = names
    ready = {}
    own, before, after, across = [(d, 0, QUARTER) for d in (0, -1, 1, 2)]
    for spot in [(h, j) for h in OFFSETS for j in OFFSETS][1:]:
        have = arrivals[("q",) + spot]
        right, left, far_right, far_left = ["x%d,%d" % spot + k for k in ("x+1", "x-1", "x+2", "x-2")]
        add(right, "x+", have, have, (spot,) * 2, spot, own, before)
        add(left, "x-", have, have, (spot,) * 2, spot, own, after)
        add(far_right, "x+", [right], [right], (spot,) * 2, spot, part(before, "a"), part(across, "a"))
        add(far_left, "x-", [left], [left], (spot,) * 2, spot, part(after, "b"), part(across, "b"))
        ready[spot] = [n for kind in "qfs" for n in arrivals[(kind,) + spot]] + [right, left, far_right, far_left]
    return moves, ready


def hidden_moves():
    moves, piece, block = {}, 128 // PIECES, 128
    every = range(PIECES)

    def add(name, link, size, needs, role):
        moves[name] = Move(link, size, (tuple(needs),) * 2, role=role)

    for p in every:
        add("zl%d" % p, "zl", piece, [], ("cols", (0, "mine"), (0, "other"), "zl", p))
        for sign, d in (("+", 1), ("-", -1)):
            add("xo%s%d" % (sign, p), "x" + sign, piece, [], ("cols", (0, "mine"), (-d, "mine"), "x" + sign, p))
            add("xp%s%d" % (sign, p), "x" + sign, piece, ["zl%d" % p], ("cols", (0, "other"), (-d, "other"), "x" + sign, p))
        add("xr+%d" % p, "x+", piece, ["xo+%d" % p, "xp+%d" % p], ("cols", (-1, 0), (2, 0), "x+", p))
    add("xr-", "x-", block, ["x%s-%d" % (k, p) for k in "op" for p in every], ("cols", (1, 1), (2, 1), "x-", None))
    gone = {0: ([], []), -1: (["za+"], ["zb+"]), 1: (["za-"], ["zb-"]), 2: (["zr+"], ["zr-"])}
    for relayed, (sign, d) in enumerate((("+", 1), ("-", -1))):
        link = "u" if d == 1 else "d"
        for which, half in enumerate("ab"):
            add("z" + half + sign, link, block, [], ("rows", (0, 0), (-d, 0), "z" + sign, which))
            for h in OFFSETS:
                add("y%d" % h + half + sign, "y" + sign, block // 2, gone[h][which], ("rows", (h, 0), (h, -d), "y" + sign, which))
        add("zr" + sign, link, block, ["z" + "ab"[relayed] + sign], ("rows", (-d, 0), (2, 0), "z" + sign, relayed))
        for h in OFFSETS:
            need = ["y%d" % h + "ab"[relayed] + sign]
            add("y%dr" % h + sign, "y" + sign, block // 2, need, ("rows", (h, -d), (h, 2), "y" + sign, relayed))
    for p in every:
        first = [name % p for name in ("zl%d", "xo+%d", "xo-%d", "xp+%d", "xp-%d", "xr+%d")]
        for hop in (1, 2, 3):
            add("c%d%d" % (hop, p), "c%d" % hop, piece, first if hop == 1 else ["c%d%d" % (hop - 1, p)], ("chain", hop, p))
        add("l%d" % p, "l", piece, ["c3%d" % p], ("spread", p))
        add("m%d" % p, "m", piece, ["l%d" % p], ("relay", p))
    row_groups = {h: gone[h][0] + gone[h][1] + ["y%d" % h + k + sign for k in "abr" for sign in "+-"] for h in OFFSETS}
    pairs = {0: ["zl%d" % p for p in every], 2: ["xr-"] + ["xr+%d" % p for p in every]}
    for sign, d in (("+", -1), ("-", 1)):
        pairs[d] = ["x%s%s%d" % (k, sign, p) for k in "op" for p in every]
    return moves, row_groups, pairs


def schedule(moves):
    followers = {name: set() for name in moves}
    for name, move in moves.items():
        for parity in (0, 1):
            for need in move.needs[parity]:
                followers[need].add((name, parity))

    def there(name, parity):
        return 1 - parity if moves[name].role is None and moves[name].link in "ud" else parity

    @functools.lru_cache(None)
    def rest(name, parity):
        after = [moves[m].size / RATE + HOP + rest(m, there(m, q)) for m, q in followers[name] if q == parity]
        return max(after, default=0.0)

    landed, begun, free = ({}, {}), ({}, {}), {}
    waiting = {(name, parity) for name in moves for parity in (0, 1)}
    while waiting:
        best = None
        for name, parity in waiting:
            move, have = moves[name], landed[parity]
            when = max(free.get((move.link, parity), 0.0), free.get(parity, 0.0))
            for need in move.needs[parity]:
                if need not in have:
                    break
                when = max(when, have[need])
            else:
                key = (when, -(rest(name, there(name, parity)) + move.size / RATE), name, parity)
                if best is None or key < best:
                    best = key
        when, _, name, parity = best
        done = when + moves[name].size / RATE
        free[moves[name].link, parity] = done
        free[parity] = when + ISSUE
        begun[parity][name] = when
        landed[there(name, parity)][name] = done + HOP
        waiting.discard((name, parity))
    return begun, landed


def eliminate(u, piece):
    wide = lax.broadcasted_iota(jnp.int32, (8, 384), 0)
    base = 64 * (piece // 2)
    groups = [u[base + 8 * g:base + 8 * g + 8, :] for g in range(8)]
    for p in range(4 * (piece % 2), 4 * (piece % 2) + 4):
        cols = {
            (g, k): jnp.broadcast_to(groups[g][:, base + 8 * p + k:base + 8 * p + k + 1], (8, 128))
            for g in range(p, 8) for k in range(8)
        }
        for k in range(8):
            inv = lax.rsqrt(jnp.broadcast_to(cols[p, k][k:k + 1, :], (8, 128)))
            inv2 = inv * inv
            ratio = [cols[g, k] * inv2 for g in range(p, 8)]
            for j in range(k + 1, 8):
                pivot = jnp.broadcast_to(cols[p, k][j:j + 1, :], (8, 128))
                for g in range(p, 8):
                    cols[g, j] = cols[g, j] - ratio[g - p] * pivot
            line = jnp.broadcast_to(groups[p][k:k + 1, :], (8, 384))
            scaled = groups[p] * jnp.concatenate([inv] * 3, axis=1)
            lower = jnp.concatenate([ratio[0]] * 3, axis=1)
            groups[p] = jnp.where(wide == k, scaled, jnp.where(wide > k, groups[p] - lower * line, groups[p]))
            for g in range(p, 8):
                cols[g, k] = cols[g, k] * inv
        for g in range(p + 1, 8):
            acc = groups[g]
            for k in range(8):
                acc = acc - jnp.concatenate([cols[g, k]] * 3, axis=1) * jnp.broadcast_to(groups[p][k:k + 1, :], (8, 384))
            groups[g] = acc
    for g in range(4 * (piece % 2), 8):
        u[base + 8 * g:base + 8 * g + 8, :] = groups[g]
    if piece % 2 and piece < 7:
        block = u[base:base + 64, :]
        first = 0 if base == 0 else 128
        update = jnp.dot(block[:, first:256].T, block, precision=HIGH, preferred_element_type=F32)
        rest = base + 64
        u[rest:256, :] = u[rest:256, :] - update[rest - first:256 - first, :]


def gather_kernel(
    tokens_hbm, gate_hbm, up_hbm, rows_out, cols_out, lead_out, own_out,
    held, weights, total, rows, cols, leads,
    load_sem, send_sem, recv_sem, send2, recv2, side_send, side_recv, lead_send, lead_recv, local_sem,
):
    tok, row, col = lax.axis_index("tok"), lax.axis_index("row"), lax.axis_index("col")
    x, z_lo, z_hi, y = lax.div(row, 2), lax.rem(row, 2), lax.div(col, 4), lax.rem(col, 4)

    def around(at):
        return {0: at, 1: lax.rem(at + 1, 4), 2: lax.rem(at + 2, 4), -1: lax.rem(at + 3, 4)}

    xs, zs, ys = around(x), around(z_hi), around(y)
    places = {(h, j): zs[h] * 4 + ys[j] for h in OFFSETS for j in OFFSETS}
    quarters = {d: xs[d] * QUARTER for d in OFFSETS}
    groups = {(d, z): xs[d] * 2 + z for d in OFFSETS for z in (0, 1)}
    firsts = {h: zs[h] * 4 for h in OFFSETS}
    spots = {d: lax.rem(xs[d], 2) * 2 for d in OFFSETS}
    keeps = {d: lax.div(xs[d], 2) == tok for d in OFFSETS}
    partner_row = x * 2 + 1 - z_lo

    devices = {"zl": (tok, partner_row, col)}
    for sign, d in (("+", 1), ("-", -1)):
        devices["x" + sign] = (tok, xs[d] * 2 + z_lo, col)
        devices["y" + sign] = (tok, row, places[0, d])
        devices["z" + sign] = (tok, row, places[d, 0])
    sibling = (1 - tok, row, col)
    step = {
        ("u", 0): devices["zl"], ("u", 1): (tok, partner_row, places[1, 0]),
        ("d", 0): (tok, partner_row, places[-1, 0]), ("d", 1): devices["zl"],
    }
    low = y < 2
    at_z = {k: jnp.logical_and(low, z_hi == k) for k in range(4)}
    past_first = jnp.logical_and(low, z_hi > 0)
    at_y = {k: y == k for k in range(4)}

    first = pltpu.make_async_copy(tokens_hbm, held.at[col], load_sem.at[2])
    first.start()
    loads = [
        pltpu.make_async_copy(gate_hbm, weights.at[:, 0:128], load_sem.at[0]),
        pltpu.make_async_copy(up_hbm, weights.at[:, 128:256], load_sem.at[1]),
    ]
    for load in loads:
        load.start()

    barrier = pltpu.get_barrier_semaphore()
    far = (tok, partner_row, places[1, 0] * z_lo + places[-1, 0] * (1 - z_lo))
    near = [devices[k] for k in ("x+", "x-", "y+", "y-", "z+", "z-", "zl")] + [far, sibling]
    for device in near:
        pl.semaphore_signal(barrier, inc=1, device_id=device, device_id_type=MESH)
    pl.semaphore_wait(barrier, len(near))
    first.wait()

    tokens, ready = token_moves()
    hiddens, row_groups, pairs = hidden_moves()
    number = {name: at for at, name in enumerate(tokens)}
    number.update({name: at for at, name in enumerate(n for n in hiddens if hiddens[n].role[0] in ("rows", "cols"))})

    def span(at_rows):
        if at_rows[0] is None:
            return pl.ds(at_rows[1], at_rows[2])
        return pl.ds(pl.multiple_of(quarters[at_rows[0]] + at_rows[1], 16), at_rows[2])

    def remote(semaphores, index, source, target, device):
        return pltpu.make_async_remote_copy(
            src_ref=source, dst_ref=target, send_sem=semaphores[0].at[index], recv_sem=semaphores[1].at[index],
            device_id=device, device_id_type=MESH,
        )

    def held_ref(spot, at_rows):
        return held.at[places[spot], span(at_rows), :]

    def block_ref(move, at, parity):
        kind, which = move.role[0], move.role[4]
        if kind == "rows":
            return rows.at[places[at]] if which is None else rows.at[places[at], pl.ds(64 * which, 64), :]
        z = {"mine": parity, "other": 1 - parity}.get(at[1], at[1])
        if which is None:
            return cols.at[groups[at[0], z]]
        size = 128 // PIECES
        return cols.at[groups[at[0], z], pl.ds(size * which, size), :]

    def outgoing(move, name, parity):
        if move.role is not None:
            place = block_ref(move, move.role[1], parity)
            return remote((send2, recv2), number[name], place, place, devices[move.role[3]])
        place = held_ref(move.source[parity], move.rows)
        device = step[move.link, parity] if move.link in "ud" else devices[move.link]
        return remote((send_sem, recv_sem), number[name], place, place, device)

    def incoming(move, name, parity):
        if move.role is not None:
            place = block_ref(move, move.role[2], parity)
            return remote((send2, recv2), number[name], place, place, sibling)
        place = held_ref(move.target, move.target_rows)
        return remote((send_sem, recv_sem), number[name], place, place, sibling)

    def lead(b, p):
        size = 128 // PIECES
        return leads.at[b, pl.ds(size * p, size), :]

    def lead_copy(kind, b, p, device, from_cols=False):
        size = 128 // PIECES
        return pltpu.make_async_remote_copy(
            src_ref=cols.at[0, pl.ds(size * p, size), :] if from_cols else lead(b, p), dst_ref=lead(b, p),
            send_sem=lead_send.at[kind * PIECES + p],
            recv_sem=lead_recv.at[b * PIECES + p],
            device_id=device, device_id_type=MESH,
        )

    def lead_arrive(b, p):
        lead_copy(0, b, p, sibling).wait_recv()

    def chain_role(hop, parity):
        if hop == 1:
            return at_z[0], step["u" if parity == 1 else "d", parity]
        upward = (hop == 2) == (parity == 0)
        return at_z[1 if upward else 3], step["u" if upward else "d", parity]

    relays = ((3, 0, "y-"), (2, 1, "y+"))

    def lead_start(role, parity):
        if role[0] == "chain":
            hop, p = role[1:]
            here, device = chain_role(hop, parity)

            @pl.when(here)
            def _():
                if hop > 1:
                    lead_arrive(y, p)
                lead_copy(0, y, p, device, hop == 1).start()
        elif role[0] == "spread":
            p = role[1]

            @pl.when(at_z[0])
            def _():
                lead_copy(1, y, p, devices["y+"], True).start()
                lead_copy(2, y, p, devices["y-"], True).start()

            @pl.when(at_z[2])
            def _():
                lead_arrive(y, p)

            @pl.when(past_first)
            def _():
                lead_copy(1, y, p, devices["y+"]).start()
                lead_copy(2, y, p, devices["y-"]).start()
        else:
            p = role[1]
            for k, b, way in relays:
                @pl.when(at_y[k])
                def _():
                    lead_arrive(b, p)
                    lead_copy(3, b, p, devices[way]).start()

    def lead_end(parity):
        for p in range(PIECES):
            for hop in (1, 2, 3):
                here, device = chain_role(hop, parity)

                @pl.when(here)
                def _():
                    lead_copy(0, y, p, device).wait_send()

            @pl.when(low)
            def _():
                lead_copy(1, y, p, devices["y+"]).wait_send()
                lead_copy(2, y, p, devices["y-"]).wait_send()

            for k, b, way in relays:
                @pl.when(at_y[k])
                def _():
                    lead_copy(3, b, p, devices[way]).wait_send()

    def side(index, source, target):
        return pltpu.make_async_remote_copy(
            src_ref=source, dst_ref=target, send_sem=side_send.at[index], recv_sem=side_recv.at[index],
            device_id=sibling, device_id_type=MESH,
        )

    def keep(index, source, target):
        return pltpu.make_async_copy(source, target, local_sem.at[index])

    shared = {}
    for k, h in enumerate(OFFSETS):
        shared["r", h] = (row_groups[h], k)
        shared["c", h] = (pairs[h], 4 + k)

    def side_refs(kind, d):
        if kind == "r":
            at = pl.ds(firsts[d], 4)
            return rows.at[at], (lambda t: rows_out.at[t, at])
        if kind == "c":
            return cols.at[pl.ds(groups[d, 0], 2)], (lambda t: cols_out.at[t, pl.ds(spots[d], 2)])
        if kind == "l":
            return leads, (lambda t: lead_out.at[t])
        return rows.at[col], (lambda t: own_out.at[t])

    def side_start(kind, d, index):
        source, target = side_refs(kind, d)
        if kind != "c":
            side(index, source, target(tok)).start()
            keep(index, source, target(tok)).start()
            return

        @pl.when(keeps[d])
        def _():
            keep(index, source, target(tok)).start()

        @pl.when(jnp.logical_not(keeps[d]))
        def _():
            side(index, source, target(tok)).start()

    def side_end(kind, d, index):
        source, target = side_refs(kind, d)
        if kind != "c":
            side(index, target(1 - tok), target(1 - tok)).wait_recv()
            side(index, source, target(tok)).wait_send()
            keep(index, source, target(tok)).wait()
            return

        @pl.when(keeps[d])
        def _():
            keep(index, source, target(tok)).wait()
            side(index, target(1 - tok), target(1 - tok)).wait_recv()

        @pl.when(jnp.logical_not(keeps[d]))
        def _():
            side(index, source, target(tok)).wait_send()

    def both(act):
        for parity in (0, 1):
            pl.when(z_lo == parity)(functools.partial(act, parity))

    def in_order(begun):
        return [sorted((begun[parity][name], name) for name in begun[parity]) for parity in (0, 1)]

    begun, landed = schedule(tokens)
    order = in_order(begun)
    seen, at = (set(), set()), [0, 0]

    def arrive(moves, name, parity):
        if name not in seen[parity]:
            seen[parity].add(name)
            if name in number:
                incoming(moves[name], name, parity).wait_recv()

    def stretch(until, batch, parity):
        while at[parity] < len(order[parity]) and order[parity][at[parity]][0] <= until:
            name = order[parity][at[parity]][1]
            at[parity] += 1
            for need in tokens[name].needs[parity]:
                arrive(tokens, need, parity)
            outgoing(tokens[name], name, parity).start()
        for chunk in batch:
            for need in ready[chunk]:
                arrive(tokens, need, parity)

    finished = {c: max(landed[p][name] for p in (0, 1) for name in ready[c]) for c in ready}
    queue = sorted(ready, key=lambda c: (finished[c], c))
    start = 0
    for k, size in enumerate(BATCHES):
        batch = queue[start:start + size]
        start += size
        until = max(finished[c] for c in batch) + AHEAD if start < len(queue) else 1e9
        both(functools.partial(stretch, until, batch))
        if k == 0:
            for load in loads:
                load.wait()
            total[...] = jnp.zeros_like(total)
        for here in ([col] if k == 0 else []) + [places[chunk] for chunk in batch]:
            total[...] += jnp.dot(held[here], weights[pl.ds(pl.multiple_of(here * 512, 512), 512), :], preferred_element_type=F32)

    def tokens_end(parity):
        for name in tokens:
            arrive(tokens, name, parity)

    both(tokens_end)
    gate = total[:, 0:128]
    hidden = gate / (1.0 + jnp.exp(-gate)) * total[:, 128:256]
    hidden = hidden.T.astype(jnp.bfloat16)
    rows[col] = hidden
    cols[row] = hidden

    begun, landed = schedule(hiddens)
    order = in_order(begun)
    left = (dict(shared), dict(shared))

    def hidden_stage(parity):
        waited = False
        for _, name in order[parity]:
            move = hiddens[name]
            if move.needs[parity] and not waited:
                waited = True
                side_start("o", 0, 8)
                for sent in tokens:
                    outgoing(tokens[sent], sent, parity).wait_send()
            for need in move.needs[parity]:
                arrive(hiddens, need, parity)
            if move.role[0] in ("rows", "cols"):
                outgoing(move, name, parity).start()
            else:
                lead_start(move.role, parity)
            for key in list(left[parity]):
                names, index = left[parity][key]
                if seen[parity].issuperset(names):
                    del left[parity][key]
                    side_start(*key, index)
        for key in list(left[parity]):
            names, index = left[parity].pop(key)
            for name in names:
                arrive(hiddens, name, parity)
            side_start(*key, index)
        for name in hiddens:
            arrive(hiddens, name, parity)

    both(hidden_stage)
    held_lead = pltpu.make_async_copy(cols.at[0], leads.at[lax.rem(y, 2)], local_sem.at[10])

    @pl.when(at_z[0])
    def _():
        held_lead.start()

    for p in range(PIECES):
        for k, b in ((0, 1), (1, 0), (2, 0), (3, 1)):
            @pl.when(at_y[k])
            def _():
                lead_arrive(b, p)

    @pl.when(at_z[0])
    def _():
        held_lead.wait()

    side_start("l", 0, 9)

    def hidden_end(parity):
        lead_end(parity)
        for name in hiddens:
            if name in number:
                outgoing(hiddens[name], name, parity).wait_send()

    both(hidden_end)
    for kind, d in shared:
        side_end(kind, d, shared[kind, d][1])
    side_end("o", 0, 8)
    side_end("l", 0, 9)


def gather(tokens, gate_weight, up_weight):
    depth, width = gate_weight.shape
    half = tokens.shape[0]
    bf16 = jnp.bfloat16
    hbm = pl.BlockSpec(memory_space=pl.ANY)
    return pl.pallas_call(
        gather_kernel,
        out_shape=(
            jax.ShapeDtypeStruct((2, 16, width, half), bf16),
            jax.ShapeDtypeStruct((2, 4, width, half), bf16),
            jax.ShapeDtypeStruct((2, 2, width, half), bf16),
            jax.ShapeDtypeStruct((2, width, half), bf16),
        ),
        in_specs=[hbm, hbm, hbm],
        out_specs=(hbm,) * 4,
        scratch_shapes=[
            pltpu.VMEM((16, half, 512), bf16),
            pltpu.VMEM((depth, 2 * width), bf16),
            pltpu.VMEM((half, 2 * width), F32),
            pltpu.VMEM((16, width, half), bf16),
            pltpu.VMEM((8, width, half), bf16),
            pltpu.VMEM((2, width, half), bf16),
            pltpu.SemaphoreType.DMA((3,)),
            pltpu.SemaphoreType.DMA((120,)),
            pltpu.SemaphoreType.DMA((120,)),
            pltpu.SemaphoreType.DMA((55,)),
            pltpu.SemaphoreType.DMA((55,)),
            pltpu.SemaphoreType.DMA((10,)),
            pltpu.SemaphoreType.DMA((10,)),
            pltpu.SemaphoreType.DMA((4 * PIECES,)),
            pltpu.SemaphoreType.DMA((2 * PIECES,)),
            pltpu.SemaphoreType.DMA((11,)),
        ],
        compiler_params=pltpu.CompilerParams(
            collective_id=0, has_side_effects=True, vmem_limit_bytes=60 * 2**20
        ),
        cost_estimate=pl.CostEstimate(flops=2 * half * depth * 2 * width, bytes_accessed=12 * 2**20, transcendentals=half * width),
    )(tokens, gate_weight, up_weight)


def gram_kernel(rows_ref, cols_ref, lead_ref, own_ref, gram_ref, panel_ref, u, out):
    step = pl.program_id(0)

    def tile():
        both = rows_ref[...].reshape(2, 256, 512)
        right = cols_ref[...].reshape(2, 512, 512)
        product = lax.dot_general(both[0], right[0], NT, preferred_element_type=F32)
        product += lax.dot_general(both[1], right[1], NT, preferred_element_type=F32)
        for a in range(4):
            gram_ref[a] = product[:, 128 * a:128 * a + 128]

    @pl.when(step == 0)
    def _():
        lead = lead_ref[...].reshape(2, 256, 512)
        u[:, 0:256] = lax.dot_general(lead[0], lead[0], NT, preferred_element_type=F32) + lax.dot_general(lead[1], lead[1], NT, preferred_element_type=F32)
        u[:, 256:384] = lax.dot_general(lead[0], own_ref[0], NT, preferred_element_type=F32) + lax.dot_general(lead[1], own_ref[1], NT, preferred_element_type=F32)

    for part_at in range(8):
        @pl.when(step == part_at)
        def _():
            tile()
            eliminate(u, part_at)

    @pl.when(step == 7)
    def _():
        panel_ref[...] = u[pl.ds(pl.multiple_of(lax.axis_index("tok") * 128, 128), 128), 256:384].T


def gram_and_panel(rows, cols, lead, own):
    width, half = rows.shape[2:]
    return pl.pallas_call(
        gram_kernel,
        grid=(8,),
        out_shape=(
            jax.ShapeDtypeStruct((4, 16 * width, width), F32),
            jax.ShapeDtypeStruct((width, width), F32),
        ),
        in_specs=[
            pl.BlockSpec((2, 2, width, half), lambda s: (0, s, 0, 0)),
            pl.BlockSpec((2, 4, width, half), lambda s: (0, 0, 0, 0)),
            pl.BlockSpec((2, 2, width, half), lambda s: (0, 0, 0, 0)),
            pl.BlockSpec((2, width, half), lambda s: (0, 0, 0)),
        ],
        out_specs=(
            pl.BlockSpec((4, 2 * width, width), lambda s: (0, s, 0)),
            pl.BlockSpec((width, width), lambda s: (0, 0)),
        ),
        scratch_shapes=[pltpu.VMEM((PANEL, 384), F32), pltpu.VMEM((8, 128), F32)],
        compiler_params=pltpu.CompilerParams(vmem_limit_bytes=60 * 2**20),
        cost_estimate=pl.CostEstimate(flops=2 * 2048 * 512 * 1024, bytes_accessed=10 * 2**20, transcendentals=0),
    )(rows, cols, lead, own)


def local(tokens, gate_weight, up_weight):
    gram, panel = gram_and_panel(*gather(tokens, gate_weight, up_weight))
    return (gram.reshape(4, 2048, 1, 128), panel)


def solution(mesh):
    placed = (P("tok", "col"), P(None, ("row", "col")), P(None, ("row", "col")))
    return jax.shard_map(
        local,
        mesh=mesh,
        in_specs=placed,
        out_specs=(P("tok", "row", "col", None), P(("row", "col"), "tok")),
        check_vma=False,
    )
```

```python
import functools

import jax
import jax.numpy as jnp
from jax import lax
from jax.experimental import pallas as pl
from jax.experimental.pallas import tpu as pltpu
from jax.sharding import PartitionSpec as P

PANEL = 256
HIGH = lax.Precision.HIGHEST
MESH = pl.DeviceIdType.MESH
OFFSETS = (0, -1, 1, 2)
NT = (((1,), (1,)), ((), ()))
F32 = jnp.float32

ROWS = 512
QUARTER = 64
FIRST_Y = (256, 96)
FIRST_Z = (352, 160)
PIECES = 4
BATCHES = (2, 2, 2, 2, 2, 2, 1, 1, 1)
RATE, HOP, ISSUE, AHEAD = 49.0, 2.0, 0.12, 0.5


class Move:
    def __init__(self, link, size, needs, source=None, target=None, rows=None, target_rows=None, role=None):
        self.link, self.size, self.needs = link, size, needs
        self.source, self.target, self.rows, self.target_rows, self.role = source, target, rows, target_rows, role


def part(rows, which):
    first = (rows[2] // 2 + 15) // 16 * 16
    return (rows[0], rows[1] + first, rows[2] - first) if which == "b" else (rows[0], rows[1], first)


def token_moves():
    moves, arrivals = {}, {}

    def add(name, link, needs0, needs1, source, target, rows, target_rows=None):
        moves[name] = Move(link, rows[2], (tuple(needs0), tuple(needs1)), source, target, rows, target_rows or rows)

    def along_z(tag, rows, j, have):
        up, far_up, down, far_down = [tag + k for k in ("u1", "u2", "d1", "d2")]
        at = {h: (h, j) for h in OFFSETS}
        add(up, "u", [up], have, (at[-1], at[0]), at[-1], rows)
        add(far_up, "u", [far_up], [up], (at[2], at[-1]), at[2], part(rows, "a"))
        add(down, "d", have, [down], (at[0], at[1]), at[1], rows)
        add(far_down, "d", [down], [far_down], (at[1], at[2]), at[2], part(rows, "b"))
        return {0: list(have), -1: [up], 1: [down], 2: [far_up, far_down]}

    def along_y(tag, rows, h, have):
        right, left, far_right, far_left = [tag + k for k in ("y+1", "y-1", "y+2", "y-2")]
        at = {j: (h, j) for j in OFFSETS}
        add(right, "y+", have, have, (at[0],) * 2, at[-1], rows)
        add(left, "y-", have, have, (at[0],) * 2, at[1], rows)
        add(far_right, "y+", [right], [right], (at[-1],) * 2, at[2], part(rows, "a"))
        add(far_left, "y-", [left], [left], (at[1],) * 2, at[2], part(rows, "b"))
        return {0: list(have), -1: [right], 1: [left], 2: [far_right, far_left]}

    for tag, rows in (("q", (0, 0, QUARTER)), ("f", (None,) + FIRST_Y)):
        near = along_y(tag, rows, 0, [])
        for j in OFFSETS:
            for h, names in along_z(tag + "%d" % j, rows, j, near[j]).items():
                arrivals[tag, h, j] = names
    near = along_z("s", (None,) + FIRST_Z, 0, [])
    for h in OFFSETS:
        for j, names in along_y("s%d" % h, (None,) + FIRST_Z, h, near[h]).items():
            arrivals["s", h, j] = names
    ready = {}
    own, before, after, across = [(d, 0, QUARTER) for d in (0, -1, 1, 2)]
    for spot in [(h, j) for h in OFFSETS for j in OFFSETS][1:]:
        have = arrivals[("q",) + spot]
        right, left, far_right, far_left = ["x%d,%d" % spot + k for k in ("x+1", "x-1", "x+2", "x-2")]
        add(right, "x+", have, have, (spot,) * 2, spot, own, before)
        add(left, "x-", have, have, (spot,) * 2, spot, own, after)
        add(far_right, "x+", [right], [right], (spot,) * 2, spot, part(before, "a"), part(across, "a"))
        add(far_left, "x-", [left], [left], (spot,) * 2, spot, part(after, "b"), part(across, "b"))
        ready[spot] = [n for kind in "qfs" for n in arrivals[(kind,) + spot]] + [right, left, far_right, far_left]
    return moves, ready


def hidden_moves():
    moves, piece, block = {}, 128 // PIECES, 128
    every = range(PIECES)

    def add(name, link, size, needs, role):
        moves[name] = Move(link, size, (tuple(needs),) * 2, role=role)

    for p in every:
        add("zl%d" % p, "zl", piece, [], ("cols", (0, "mine"), (0, "other"), "zl", p))
        for sign, d in (("+", 1), ("-", -1)):
            add("xo%s%d" % (sign, p), "x" + sign, piece, [], ("cols", (0, "mine"), (-d, "mine"), "x" + sign, p))
            add("xp%s%d" % (sign, p), "x" + sign, piece, ["zl%d" % p], ("cols", (0, "other"), (-d, "other"), "x" + sign, p))
        add("xr+%d" % p, "x+", piece, ["xo+%d" % p, "xp+%d" % p], ("cols", (-1, 0), (2, 0), "x+", p))
    add("xr-", "x-", block, ["x%s-%d" % (k, p) for k in "op" for p in every], ("cols", (1, 1), (2, 1), "x-", None))
    gone = {0: ([], []), -1: (["za+"], ["zb+"]), 1: (["za-"], ["zb-"]), 2: (["zr+"], ["zr-"])}
    for relayed, (sign, d) in enumerate((("+", 1), ("-", -1))):
        link = "u" if d == 1 else "d"
        for which, half in enumerate("ab"):
            add("z" + half + sign, link, block, [], ("rows", (0, 0), (-d, 0), "z" + sign, which))
            for h in OFFSETS:
                add("y%d" % h + half + sign, "y" + sign, block // 2, gone[h][which], ("rows", (h, 0), (h, -d), "y" + sign, which))
        add("zr" + sign, link, block, ["z" + "ab"[relayed] + sign], ("rows", (-d, 0), (2, 0), "z" + sign, relayed))
        for h in OFFSETS:
            need = ["y%d" % h + "ab"[relayed] + sign]
            add("y%dr" % h + sign, "y" + sign, block // 2, need, ("rows", (h, -d), (h, 2), "y" + sign, relayed))
    for p in every:
        first = [name % p for name in ("zl%d", "xo+%d", "xo-%d", "xp+%d", "xp-%d", "xr+%d")]
        for hop in (1, 2, 3):
            add("c%d%d" % (hop, p), "c%d" % hop, piece, first if hop == 1 else ["c%d%d" % (hop - 1, p)], ("chain", hop, p))
        add("l%d" % p, "l", piece, ["c3%d" % p], ("spread", p))
        add("m%d" % p, "m", piece, ["l%d" % p], ("relay", p))
    row_groups = {h: gone[h][0] + gone[h][1] + ["y%d" % h + k + sign for k in "abr" for sign in "+-"] for h in OFFSETS}
    pairs = {0: ["zl%d" % p for p in every], 2: ["xr-"] + ["xr+%d" % p for p in every]}
    for sign, d in (("+", -1), ("-", 1)):
        pairs[d] = ["x%s%s%d" % (k, sign, p) for k in "op" for p in every]
    return moves, row_groups, pairs


def schedule(moves):
    followers = {name: set() for name in moves}
    for name, move in moves.items():
        for parity in (0, 1):
            for need in move.needs[parity]:
                followers[need].add((name, parity))

    def there(name, parity):
        return 1 - parity if moves[name].role is None and moves[name].link in "ud" else parity

    @functools.lru_cache(None)
    def rest(name, parity):
        after = [moves[m].size / RATE + HOP + rest(m, there(m, q)) for m, q in followers[name] if q == parity]
        return max(after, default=0.0)

    landed, begun, free = ({}, {}), ({}, {}), {}
    waiting = {(name, parity) for name in moves for parity in (0, 1)}
    while waiting:
        best = None
        for name, parity in waiting:
            move, have = moves[name], landed[parity]
            when = max(free.get((move.link, parity), 0.0), free.get(parity, 0.0))
            for need in move.needs[parity]:
                if need not in have:
                    break
                when = max(when, have[need])
            else:
                key = (when, -(rest(name, there(name, parity)) + move.size / RATE), name, parity)
                if best is None or key < best:
                    best = key
        when, _, name, parity = best
        done = when + moves[name].size / RATE
        free[moves[name].link, parity] = done
        free[parity] = when + ISSUE
        begun[parity][name] = when
        landed[there(name, parity)][name] = done + HOP
        waiting.discard((name, parity))
    return begun, landed


def balance(u):
    rows = lax.broadcasted_iota(jnp.int32, (PANEL, PANEL), 0)
    lanes = lax.broadcasted_iota(jnp.int32, (PANEL, PANEL), 1)
    corner = u[:, 0:PANEL]
    only = jnp.where(rows == lanes, corner, 0.0)
    down, across = lax.rsqrt(jnp.sum(only, axis=1, keepdims=True)), lax.rsqrt(jnp.sum(only, axis=0, keepdims=True))
    u[:, 0:PANEL] = corner * down * across
    u[:, PANEL:] = u[:, PANEL:] * down


def eliminate(u, piece):
    wide = lax.broadcasted_iota(jnp.int32, (8, 384), 0)
    base = 64 * (piece // 2)
    groups = [u[base + 8 * g:base + 8 * g + 8, :] for g in range(8)]

    def spread(row, at):
        return jnp.broadcast_to(row[at:at + 1, :], (8, row.shape[1]))

    def thrice(tile):
        return jnp.concatenate([tile] * 3, axis=1)

    for p in range(4 * (piece % 2), 4 * (piece % 2) + 4):
        cols = {
            (g, k): jnp.broadcast_to(groups[g][:, base + 8 * p + k:base + 8 * p + k + 1], (8, 128))
            for g in range(p, 8) for k in range(8)
        }
        for k in range(0, 8, 2):
            a, b, c = spread(cols[p, k], k), spread(cols[p, k + 1], k), spread(cols[p, k + 1], k + 1)
            over = 1.0 / (a * c - b * b)
            left, right = [], []
            for g in range(p, 8):
                left.append((c * cols[g, k] - b * cols[g, k + 1]) * over)
                right.append((a * cols[g, k + 1] - b * cols[g, k]) * over)
            for j in range(k + 2, 8):
                one, two = spread(cols[p, k], j), spread(cols[p, k + 1], j)
                for g in range(p, 8):
                    cols[g, j] = cols[g, j] - (left[g - p] * one + right[g - p] * two)
            first = lax.rsqrt(a)
            ratio = b * first * first
            second = lax.rsqrt(c - b * ratio)
            line, below = spread(groups[p], k), spread(groups[p], k + 1)
            top = line * thrice(first)
            low = (below - thrice(ratio) * line) * thrice(second)
            rest = groups[p] - (thrice(left[0]) * line + thrice(right[0]) * below)
            groups[p] = jnp.where(wide == k, top, jnp.where(wide == k + 1, low, jnp.where(wide > k + 1, rest, groups[p])))
            for g in range(p, 8):
                cols[g, k + 1] = (cols[g, k + 1] - ratio * cols[g, k]) * second
                cols[g, k] = cols[g, k] * first
        for g in range(p + 1, 8):
            acc = groups[g]
            for k in range(8):
                acc = acc - thrice(cols[g, k]) * spread(groups[p], k)
            groups[g] = acc
    for g in range(4 * (piece % 2), 8):
        u[base + 8 * g:base + 8 * g + 8, :] = groups[g]
    if piece % 2 and piece < 7:
        block = u[base:base + 64, :]
        first = 0 if base == 0 else 128
        update = jnp.dot(block[:, first:256].T, block, precision=HIGH, preferred_element_type=F32)
        rest = base + 64
        u[rest:256, :] = u[rest:256, :] - update[rest - first:256 - first, :]


def gather_kernel(
    tokens_hbm, gate_hbm, up_hbm, rows_out, cols_out, lead_out, own_out,
    held, weights, total, rows, cols, leads,
    load_sem, send_sem, recv_sem, send2, recv2, side_send, side_recv, lead_send, lead_recv, local_sem,
):
    tok, row, col = lax.axis_index("tok"), lax.axis_index("row"), lax.axis_index("col")
    x, z_lo, z_hi, y = lax.div(row, 2), lax.rem(row, 2), lax.div(col, 4), lax.rem(col, 4)

    def around(at):
        return {0: at, 1: lax.rem(at + 1, 4), 2: lax.rem(at + 2, 4), -1: lax.rem(at + 3, 4)}

    xs, zs, ys = around(x), around(z_hi), around(y)
    places = {(h, j): zs[h] * 4 + ys[j] for h in OFFSETS for j in OFFSETS}
    quarters = {d: xs[d] * QUARTER for d in OFFSETS}
    groups = {(d, z): xs[d] * 2 + z for d in OFFSETS for z in (0, 1)}
    firsts = {h: zs[h] * 4 for h in OFFSETS}
    spots = {d: lax.rem(xs[d], 2) * 2 for d in OFFSETS}
    keeps = {d: lax.div(xs[d], 2) == tok for d in OFFSETS}
    partner_row = x * 2 + 1 - z_lo

    devices = {"zl": (tok, partner_row, col)}
    for sign, d in (("+", 1), ("-", -1)):
        devices["x" + sign] = (tok, xs[d] * 2 + z_lo, col)
        devices["y" + sign] = (tok, row, places[0, d])
        devices["z" + sign] = (tok, row, places[d, 0])
    sibling = (1 - tok, row, col)
    step = {
        ("u", 0): devices["zl"], ("u", 1): (tok, partner_row, places[1, 0]),
        ("d", 0): (tok, partner_row, places[-1, 0]), ("d", 1): devices["zl"],
    }
    low = y < 2
    at_z = {k: jnp.logical_and(low, z_hi == k) for k in range(4)}
    past_first = jnp.logical_and(low, z_hi > 0)
    at_y = {k: y == k for k in range(4)}

    first = pltpu.make_async_copy(tokens_hbm, held.at[col], load_sem.at[2])
    first.start()
    loads = [
        pltpu.make_async_copy(gate_hbm, weights.at[:, 0:128], load_sem.at[0]),
        pltpu.make_async_copy(up_hbm, weights.at[:, 128:256], load_sem.at[1]),
    ]
    for load in loads:
        load.start()

    barrier = pltpu.get_barrier_semaphore()
    far = (tok, partner_row, places[1, 0] * z_lo + places[-1, 0] * (1 - z_lo))
    near = [devices[k] for k in ("x+", "x-", "y+", "y-", "z+", "z-", "zl")] + [far, sibling]
    for device in near:
        pl.semaphore_signal(barrier, inc=1, device_id=device, device_id_type=MESH)
    pl.semaphore_wait(barrier, len(near))
    first.wait()

    tokens, ready = token_moves()
    hiddens, row_groups, pairs = hidden_moves()
    number = {name: at for at, name in enumerate(tokens)}
    number.update({name: at for at, name in enumerate(n for n in hiddens if hiddens[n].role[0] in ("rows", "cols"))})

    def span(at_rows):
        if at_rows[0] is None:
            return pl.ds(at_rows[1], at_rows[2])
        return pl.ds(pl.multiple_of(quarters[at_rows[0]] + at_rows[1], 16), at_rows[2])

    def remote(semaphores, index, source, target, device):
        return pltpu.make_async_remote_copy(
            src_ref=source, dst_ref=target, send_sem=semaphores[0].at[index], recv_sem=semaphores[1].at[index],
            device_id=device, device_id_type=MESH,
        )

    def held_ref(spot, at_rows):
        return held.at[places[spot], span(at_rows), :]

    def block_ref(move, at, parity):
        kind, which = move.role[0], move.role[4]
        if kind == "rows":
            return rows.at[places[at]] if which is None else rows.at[places[at], pl.ds(64 * which, 64), :]
        z = {"mine": parity, "other": 1 - parity}.get(at[1], at[1])
        if which is None:
            return cols.at[groups[at[0], z]]
        size = 128 // PIECES
        return cols.at[groups[at[0], z], pl.ds(size * which, size), :]

    def outgoing(move, name, parity):
        if move.role is not None:
            place = block_ref(move, move.role[1], parity)
            return remote((send2, recv2), number[name], place, place, devices[move.role[3]])
        place = held_ref(move.source[parity], move.rows)
        device = step[move.link, parity] if move.link in "ud" else devices[move.link]
        return remote((send_sem, recv_sem), number[name], place, place, device)

    def incoming(move, name, parity):
        if move.role is not None:
            place = block_ref(move, move.role[2], parity)
            return remote((send2, recv2), number[name], place, place, sibling)
        place = held_ref(move.target, move.target_rows)
        return remote((send_sem, recv_sem), number[name], place, place, sibling)

    def lead(b, p):
        size = 128 // PIECES
        return leads.at[b, pl.ds(size * p, size), :]

    def lead_copy(kind, b, p, device, from_cols=False):
        size = 128 // PIECES
        return pltpu.make_async_remote_copy(
            src_ref=cols.at[0, pl.ds(size * p, size), :] if from_cols else lead(b, p), dst_ref=lead(b, p),
            send_sem=lead_send.at[kind * PIECES + p],
            recv_sem=lead_recv.at[b * PIECES + p],
            device_id=device, device_id_type=MESH,
        )

    def lead_arrive(b, p):
        lead_copy(0, b, p, sibling).wait_recv()

    def chain_role(hop, parity):
        if hop == 1:
            return at_z[0], step["u" if parity == 1 else "d", parity]
        upward = (hop == 2) == (parity == 0)
        return at_z[1 if upward else 3], step["u" if upward else "d", parity]

    relays = ((3, 0, "y-"), (2, 1, "y+"))

    def lead_start(role, parity):
        if role[0] == "chain":
            hop, p = role[1:]
            here, device = chain_role(hop, parity)

            @pl.when(here)
            def _():
                if hop > 1:
                    lead_arrive(y, p)
                lead_copy(0, y, p, device, hop == 1).start()
        elif role[0] == "spread":
            p = role[1]

            @pl.when(at_z[0])
            def _():
                lead_copy(1, y, p, devices["y+"], True).start()
                lead_copy(2, y, p, devices["y-"], True).start()

            @pl.when(at_z[2])
            def _():
                lead_arrive(y, p)

            @pl.when(past_first)
            def _():
                lead_copy(1, y, p, devices["y+"]).start()
                lead_copy(2, y, p, devices["y-"]).start()
        else:
            p = role[1]
            for k, b, way in relays:
                @pl.when(at_y[k])
                def _():
                    lead_arrive(b, p)
                    lead_copy(3, b, p, devices[way]).start()

    def lead_end(parity):
        for p in range(PIECES):
            for hop in (1, 2, 3):
                here, device = chain_role(hop, parity)

                @pl.when(here)
                def _():
                    lead_copy(0, y, p, device).wait_send()

            @pl.when(low)
            def _():
                lead_copy(1, y, p, devices["y+"]).wait_send()
                lead_copy(2, y, p, devices["y-"]).wait_send()

            for k, b, way in relays:
                @pl.when(at_y[k])
                def _():
                    lead_copy(3, b, p, devices[way]).wait_send()

    def side(index, source, target):
        return pltpu.make_async_remote_copy(
            src_ref=source, dst_ref=target, send_sem=side_send.at[index], recv_sem=side_recv.at[index],
            device_id=sibling, device_id_type=MESH,
        )

    def keep(index, source, target):
        return pltpu.make_async_copy(source, target, local_sem.at[index])

    shared = {}
    for k, h in enumerate(OFFSETS):
        shared["r", h] = (row_groups[h], k)
        shared["c", h] = (pairs[h], 4 + k)

    def side_refs(kind, d):
        if kind == "r":
            at = pl.ds(firsts[d], 4)
            return rows.at[at], (lambda t: rows_out.at[t, at])
        if kind == "c":
            return cols.at[pl.ds(groups[d, 0], 2)], (lambda t: cols_out.at[t, pl.ds(spots[d], 2)])
        if kind == "l":
            return leads, (lambda t: lead_out.at[t])
        return rows.at[col], (lambda t: own_out.at[t])

    def side_start(kind, d, index):
        source, target = side_refs(kind, d)
        if kind != "c":
            side(index, source, target(tok)).start()
            keep(index, source, target(tok)).start()
            return

        @pl.when(keeps[d])
        def _():
            keep(index, source, target(tok)).start()

        @pl.when(jnp.logical_not(keeps[d]))
        def _():
            side(index, source, target(tok)).start()

    def side_end(kind, d, index):
        source, target = side_refs(kind, d)
        if kind != "c":
            side(index, target(1 - tok), target(1 - tok)).wait_recv()
            side(index, source, target(tok)).wait_send()
            keep(index, source, target(tok)).wait()
            return

        @pl.when(keeps[d])
        def _():
            keep(index, source, target(tok)).wait()
            side(index, target(1 - tok), target(1 - tok)).wait_recv()

        @pl.when(jnp.logical_not(keeps[d]))
        def _():
            side(index, source, target(tok)).wait_send()

    def both(act):
        for parity in (0, 1):
            pl.when(z_lo == parity)(functools.partial(act, parity))

    def in_order(begun):
        return [sorted((begun[parity][name], name) for name in begun[parity]) for parity in (0, 1)]

    begun, landed = schedule(tokens)
    order = in_order(begun)
    seen, at = (set(), set()), [0, 0]

    def arrive(moves, name, parity):
        if name not in seen[parity]:
            seen[parity].add(name)
            if name in number:
                incoming(moves[name], name, parity).wait_recv()

    def stretch(until, batch, parity):
        while at[parity] < len(order[parity]) and order[parity][at[parity]][0] <= until:
            name = order[parity][at[parity]][1]
            at[parity] += 1
            for need in tokens[name].needs[parity]:
                arrive(tokens, need, parity)
            outgoing(tokens[name], name, parity).start()
        for chunk in batch:
            for need in ready[chunk]:
                arrive(tokens, need, parity)

    finished = {c: max(landed[p][name] for p in (0, 1) for name in ready[c]) for c in ready}
    queue = sorted(ready, key=lambda c: (finished[c], c))
    start = 0
    for k, size in enumerate(BATCHES):
        batch = queue[start:start + size]
        start += size
        until = max(finished[c] for c in batch) + AHEAD if start < len(queue) else 1e9
        both(functools.partial(stretch, until, batch))
        if k == 0:
            for load in loads:
                load.wait()
            total[...] = jnp.zeros_like(total)
        for here in ([col] if k == 0 else []) + [places[chunk] for chunk in batch]:
            total[...] += jnp.dot(held[here], weights[pl.ds(pl.multiple_of(here * 512, 512), 512), :], preferred_element_type=F32)

    def tokens_end(parity):
        for name in tokens:
            arrive(tokens, name, parity)

    both(tokens_end)
    gate = total[:, 0:128]
    hidden = gate / (1.0 + jnp.exp(-gate)) * total[:, 128:256]
    hidden = hidden.T.astype(jnp.bfloat16)
    rows[col] = hidden
    cols[row] = hidden

    begun, landed = schedule(hiddens)
    order = in_order(begun)
    left = (dict(shared), dict(shared))

    def hidden_stage(parity):
        waited = False
        for _, name in order[parity]:
            move = hiddens[name]
            if move.needs[parity] and not waited:
                waited = True
                side_start("o", 0, 8)
                for sent in tokens:
                    outgoing(tokens[sent], sent, parity).wait_send()
            for need in move.needs[parity]:
                arrive(hiddens, need, parity)
            if move.role[0] in ("rows", "cols"):
                outgoing(move, name, parity).start()
            else:
                lead_start(move.role, parity)
            for key in list(left[parity]):
                names, index = left[parity][key]
                if seen[parity].issuperset(names):
                    del left[parity][key]
                    side_start(*key, index)
        for key in list(left[parity]):
            names, index = left[parity].pop(key)
            for name in names:
                arrive(hiddens, name, parity)
            side_start(*key, index)
        for name in hiddens:
            arrive(hiddens, name, parity)

    both(hidden_stage)
    held_lead = pltpu.make_async_copy(cols.at[0], leads.at[lax.rem(y, 2)], local_sem.at[10])

    @pl.when(at_z[0])
    def _():
        held_lead.start()

    for p in range(PIECES):
        for k, b in ((0, 1), (1, 0), (2, 0), (3, 1)):
            @pl.when(at_y[k])
            def _():
                lead_arrive(b, p)

    @pl.when(at_z[0])
    def _():
        held_lead.wait()

    side_start("l", 0, 9)

    def hidden_end(parity):
        lead_end(parity)
        for name in hiddens:
            if name in number:
                outgoing(hiddens[name], name, parity).wait_send()

    both(hidden_end)
    for kind, d in shared:
        side_end(kind, d, shared[kind, d][1])
    side_end("o", 0, 8)
    side_end("l", 0, 9)


def gather(tokens, gate_weight, up_weight):
    depth, width = gate_weight.shape
    half = tokens.shape[0]
    bf16 = jnp.bfloat16
    hbm = pl.BlockSpec(memory_space=pl.ANY)
    return pl.pallas_call(
        gather_kernel,
        out_shape=(
            jax.ShapeDtypeStruct((2, 16, width, half), bf16),
            jax.ShapeDtypeStruct((2, 4, width, half), bf16),
            jax.ShapeDtypeStruct((2, 2, width, half), bf16),
            jax.ShapeDtypeStruct((2, width, half), bf16),
        ),
        in_specs=[hbm, hbm, hbm],
        out_specs=(hbm,) * 4,
        scratch_shapes=[
            pltpu.VMEM((16, half, 512), bf16),
            pltpu.VMEM((depth, 2 * width), bf16),
            pltpu.VMEM((half, 2 * width), F32),
            pltpu.VMEM((16, width, half), bf16),
            pltpu.VMEM((8, width, half), bf16),
            pltpu.VMEM((2, width, half), bf16),
            pltpu.SemaphoreType.DMA((3,)),
            pltpu.SemaphoreType.DMA((120,)),
            pltpu.SemaphoreType.DMA((120,)),
            pltpu.SemaphoreType.DMA((55,)),
            pltpu.SemaphoreType.DMA((55,)),
            pltpu.SemaphoreType.DMA((10,)),
            pltpu.SemaphoreType.DMA((10,)),
            pltpu.SemaphoreType.DMA((4 * PIECES,)),
            pltpu.SemaphoreType.DMA((2 * PIECES,)),
            pltpu.SemaphoreType.DMA((11,)),
        ],
        compiler_params=pltpu.CompilerParams(
            collective_id=0, has_side_effects=True, vmem_limit_bytes=60 * 2**20
        ),
        cost_estimate=pl.CostEstimate(flops=2 * half * depth * 2 * width, bytes_accessed=12 * 2**20, transcendentals=half * width),
    )(tokens, gate_weight, up_weight)


def gram_kernel(rows_ref, cols_ref, lead_ref, own_ref, gram_ref, panel_ref, u, out):
    step = pl.program_id(0)

    def tile():
        both = rows_ref[...].reshape(2, 256, 512)
        right = cols_ref[...].reshape(2, 512, 512)
        product = lax.dot_general(both[0], right[0], NT, preferred_element_type=F32)
        product += lax.dot_general(both[1], right[1], NT, preferred_element_type=F32)
        for a in range(4):
            gram_ref[a] = product[:, 128 * a:128 * a + 128]

    @pl.when(step == 0)
    def _():
        lead = lead_ref[...].reshape(2, 256, 512)
        u[:, 0:256] = lax.dot_general(lead[0], lead[0], NT, preferred_element_type=F32) + lax.dot_general(lead[1], lead[1], NT, preferred_element_type=F32)
        u[:, 256:384] = lax.dot_general(lead[0], own_ref[0], NT, preferred_element_type=F32) + lax.dot_general(lead[1], own_ref[1], NT, preferred_element_type=F32)
        balance(u)

    for part_at in range(8):
        @pl.when(step == part_at)
        def _():
            tile()
            eliminate(u, part_at)

    @pl.when(step == 7)
    def _():
        panel_ref[...] = u[pl.ds(pl.multiple_of(lax.axis_index("tok") * 128, 128), 128), 256:384].T


def gram_and_panel(rows, cols, lead, own):
    width, half = rows.shape[2:]
    return pl.pallas_call(
        gram_kernel,
        grid=(8,),
        out_shape=(
            jax.ShapeDtypeStruct((4, 16 * width, width), F32),
            jax.ShapeDtypeStruct((width, width), F32),
        ),
        in_specs=[
            pl.BlockSpec((2, 2, width, half), lambda s: (0, s, 0, 0)),
            pl.BlockSpec((2, 4, width, half), lambda s: (0, 0, 0, 0)),
            pl.BlockSpec((2, 2, width, half), lambda s: (0, 0, 0, 0)),
            pl.BlockSpec((2, width, half), lambda s: (0, 0, 0)),
        ],
        out_specs=(
            pl.BlockSpec((4, 2 * width, width), lambda s: (0, s, 0)),
            pl.BlockSpec((width, width), lambda s: (0, 0)),
        ),
        scratch_shapes=[pltpu.VMEM((PANEL, 384), F32), pltpu.VMEM((8, 128), F32)],
        compiler_params=pltpu.CompilerParams(vmem_limit_bytes=60 * 2**20),
        cost_estimate=pl.CostEstimate(flops=2 * 2048 * 512 * 1024, bytes_accessed=10 * 2**20, transcendentals=0),
    )(rows, cols, lead, own)


def local(tokens, gate_weight, up_weight):
    gram, panel = gram_and_panel(*gather(tokens, gate_weight, up_weight))
    return (gram.reshape(4, 2048, 1, 128), panel)


def solution(mesh):
    placed = (P("tok", "col"), P(None, ("row", "col")), P(None, ("row", "col")))
    return jax.shard_map(
        local,
        mesh=mesh,
        in_specs=placed,
        out_specs=(P("tok", "row", "col", None), P(("row", "col"), "tok")),
        check_vma=False,
    )
```

```python
import functools

import jax
import jax.numpy as jnp
from jax import lax
from jax.experimental import pallas as pl
from jax.experimental.pallas import tpu as pltpu
from jax.sharding import PartitionSpec as P

PANEL = 256
HIGH = lax.Precision.HIGHEST
MESH = pl.DeviceIdType.MESH
OFFSETS = (0, -1, 1, 2)
NT = (((1,), (1,)), ((), ()))
F32 = jnp.float32

ROWS = 512
QUARTER = 64
FIRST_Y = (256, 96)
FIRST_Z = (352, 160)
PIECES = 4
BATCHES = (2, 2, 2, 2, 2, 2, 1, 1, 1)
RATE, HOP, ISSUE, AHEAD = 49.0, 2.0, 0.12, 0.5


class Move:
    def __init__(self, link, size, needs, source=None, target=None, rows=None, target_rows=None, role=None):
        self.link, self.size, self.needs = link, size, needs
        self.source, self.target, self.rows, self.target_rows, self.role = source, target, rows, target_rows, role


def part(rows, which):
    first = (rows[2] // 2 + 15) // 16 * 16
    return (rows[0], rows[1] + first, rows[2] - first) if which == "b" else (rows[0], rows[1], first)


def token_moves():
    moves, arrivals = {}, {}

    def add(name, link, needs0, needs1, source, target, rows, target_rows=None):
        moves[name] = Move(link, rows[2], (tuple(needs0), tuple(needs1)), source, target, rows, target_rows or rows)

    def along_z(tag, rows, j, have):
        up, far_up, down, far_down = [tag + k for k in ("u1", "u2", "d1", "d2")]
        at = {h: (h, j) for h in OFFSETS}
        add(up, "u", [up], have, (at[-1], at[0]), at[-1], rows)
        add(far_up, "u", [far_up], [up], (at[2], at[-1]), at[2], part(rows, "a"))
        add(down, "d", have, [down], (at[0], at[1]), at[1], rows)
        add(far_down, "d", [down], [far_down], (at[1], at[2]), at[2], part(rows, "b"))
        return {0: list(have), -1: [up], 1: [down], 2: [far_up, far_down]}

    def along_y(tag, rows, h, have):
        right, left, far_right, far_left = [tag + k for k in ("y+1", "y-1", "y+2", "y-2")]
        at = {j: (h, j) for j in OFFSETS}
        add(right, "y+", have, have, (at[0],) * 2, at[-1], rows)
        add(left, "y-", have, have, (at[0],) * 2, at[1], rows)
        add(far_right, "y+", [right], [right], (at[-1],) * 2, at[2], part(rows, "a"))
        add(far_left, "y-", [left], [left], (at[1],) * 2, at[2], part(rows, "b"))
        return {0: list(have), -1: [right], 1: [left], 2: [far_right, far_left]}

    for tag, rows in (("q", (0, 0, QUARTER)), ("f", (None,) + FIRST_Y)):
        near = along_y(tag, rows, 0, [])
        for j in OFFSETS:
            for h, names in along_z(tag + "%d" % j, rows, j, near[j]).items():
                arrivals[tag, h, j] = names
    near = along_z("s", (None,) + FIRST_Z, 0, [])
    for h in OFFSETS:
        for j, names in along_y("s%d" % h, (None,) + FIRST_Z, h, near[h]).items():
            arrivals["s", h, j] = names
    ready = {}
    own, before, after, across = [(d, 0, QUARTER) for d in (0, -1, 1, 2)]
    for spot in [(h, j) for h in OFFSETS for j in OFFSETS][1:]:
        have = arrivals[("q",) + spot]
        right, left, far_right, far_left = ["x%d,%d" % spot + k for k in ("x+1", "x-1", "x+2", "x-2")]
        add(right, "x+", have, have, (spot,) * 2, spot, own, before)
        add(left, "x-", have, have, (spot,) * 2, spot, own, after)
        add(far_right, "x+", [right], [right], (spot,) * 2, spot, part(before, "a"), part(across, "a"))
        add(far_left, "x-", [left], [left], (spot,) * 2, spot, part(after, "b"), part(across, "b"))
        ready[spot] = [n for kind in "qfs" for n in arrivals[(kind,) + spot]] + [right, left, far_right, far_left]
    return moves, ready


def hidden_moves():
    moves, piece, block = {}, 128 // PIECES, 128
    every = range(PIECES)

    def add(name, link, size, needs, role):
        moves[name] = Move(link, size, (tuple(needs),) * 2, role=role)

    for p in every:
        add("zl%d" % p, "zl", piece, [], ("cols", (0, "mine"), (0, "other"), "zl", p))
        for sign, d in (("+", 1), ("-", -1)):
            add("xo%s%d" % (sign, p), "x" + sign, piece, [], ("cols", (0, "mine"), (-d, "mine"), "x" + sign, p))
            add("xp%s%d" % (sign, p), "x" + sign, piece, ["zl%d" % p], ("cols", (0, "other"), (-d, "other"), "x" + sign, p))
        add("xr+%d" % p, "x+", piece, ["xo+%d" % p, "xp+%d" % p], ("cols", (-1, 0), (2, 0), "x+", p))
    add("xr-", "x-", block, ["x%s-%d" % (k, p) for k in "op" for p in every], ("cols", (1, 1), (2, 1), "x-", None))
    gone = {0: ([], []), -1: (["za+"], ["zb+"]), 1: (["za-"], ["zb-"]), 2: (["zr+"], ["zr-"])}
    for relayed, (sign, d) in enumerate((("+", 1), ("-", -1))):
        link = "u" if d == 1 else "d"
        for which, half in enumerate("ab"):
            add("z" + half + sign, link, block, [], ("rows", (0, 0), (-d, 0), "z" + sign, which))
            for h in OFFSETS:
                add("y%d" % h + half + sign, "y" + sign, block // 2, gone[h][which], ("rows", (h, 0), (h, -d), "y" + sign, which))
        add("zr" + sign, link, block, ["z" + "ab"[relayed] + sign], ("rows", (-d, 0), (2, 0), "z" + sign, relayed))
        for h in OFFSETS:
            need = ["y%d" % h + "ab"[relayed] + sign]
            add("y%dr" % h + sign, "y" + sign, block // 2, need, ("rows", (h, -d), (h, 2), "y" + sign, relayed))
    for p in every:
        first = [name % p for name in ("zl%d", "xo+%d", "xo-%d", "xp+%d", "xp-%d", "xr+%d")]
        for hop in (1, 2, 3):
            add("c%d%d" % (hop, p), "c%d" % hop, piece, first if hop == 1 else ["c%d%d" % (hop - 1, p)], ("chain", hop, p))
        add("l%d" % p, "l", piece, ["c3%d" % p], ("spread", p))
        add("m%d" % p, "m", piece, ["l%d" % p], ("relay", p))
    row_groups = {h: gone[h][0] + gone[h][1] + ["y%d" % h + k + sign for k in "abr" for sign in "+-"] for h in OFFSETS}
    pairs = {0: ["zl%d" % p for p in every], 2: ["xr-"] + ["xr+%d" % p for p in every]}
    for sign, d in (("+", -1), ("-", 1)):
        pairs[d] = ["x%s%s%d" % (k, sign, p) for k in "op" for p in every]
    return moves, row_groups, pairs


def schedule(moves):
    followers = {name: set() for name in moves}
    for name, move in moves.items():
        for parity in (0, 1):
            for need in move.needs[parity]:
                followers[need].add((name, parity))

    def there(name, parity):
        return 1 - parity if moves[name].role is None and moves[name].link in "ud" else parity

    @functools.lru_cache(None)
    def rest(name, parity):
        after = [moves[m].size / RATE + HOP + rest(m, there(m, q)) for m, q in followers[name] if q == parity]
        return max(after, default=0.0)

    landed, begun, free = ({}, {}), ({}, {}), {}
    waiting = {(name, parity) for name in moves for parity in (0, 1)}
    while waiting:
        best = None
        for name, parity in waiting:
            move, have = moves[name], landed[parity]
            when = max(free.get((move.link, parity), 0.0), free.get(parity, 0.0))
            for need in move.needs[parity]:
                if need not in have:
                    break
                when = max(when, have[need])
            else:
                key = (when, -(rest(name, there(name, parity)) + move.size / RATE), name, parity)
                if best is None or key < best:
                    best = key
        when, _, name, parity = best
        done = when + moves[name].size / RATE
        free[moves[name].link, parity] = done
        free[parity] = when + ISSUE
        begun[parity][name] = when
        landed[there(name, parity)][name] = done + HOP
        waiting.discard((name, parity))
    return begun, landed


def balance(u):
    rows = lax.broadcasted_iota(jnp.int32, (PANEL, PANEL), 0)
    lanes = lax.broadcasted_iota(jnp.int32, (PANEL, PANEL), 1)
    corner = u[:, 0:PANEL]
    only = jnp.where(rows == lanes, corner, 0.0)
    down, across = lax.rsqrt(jnp.sum(only, axis=1, keepdims=True)), lax.rsqrt(jnp.sum(only, axis=0, keepdims=True))
    u[:, 0:PANEL] = corner * down * across
    u[:, PANEL:] = u[:, PANEL:] * down


def eliminate(u, piece):
    wide = lax.broadcasted_iota(jnp.int32, (8, 384), 0)
    base = 64 * (piece // 2)
    groups = [u[base + 8 * g:base + 8 * g + 8, :] for g in range(8)]

    def spread(row, at):
        return jnp.broadcast_to(row[at:at + 1, :], (8, row.shape[1]))

    def thrice(tile):
        return jnp.concatenate([tile] * 3, axis=1)

    for p in range(4 * (piece % 2), 4 * (piece % 2) + 4):
        cols = {
            (g, k): jnp.broadcast_to(groups[g][:, base + 8 * p + k:base + 8 * p + k + 1], (8, 128))
            for g in range(p, 8) for k in range(8)
        }
        for k in range(0, 8, 2):
            a, b, c = spread(cols[p, k], k), spread(cols[p, k + 1], k), spread(cols[p, k + 1], k + 1)
            over = 1.0 / (a * c - b * b)
            left, right = [], []
            for g in range(p, 8):
                left.append((c * cols[g, k] - b * cols[g, k + 1]) * over)
                right.append((a * cols[g, k + 1] - b * cols[g, k]) * over)
            for j in range(k + 2, 8):
                one, two = spread(cols[p, k], j), spread(cols[p, k + 1], j)
                for g in range(p, 8):
                    cols[g, j] = cols[g, j] - (left[g - p] * one + right[g - p] * two)
            first = lax.rsqrt(a)
            ratio = b * first * first
            second = lax.rsqrt(c - b * ratio)
            line, below = spread(groups[p], k), spread(groups[p], k + 1)
            top = line * thrice(first)
            low = (below - thrice(ratio) * line) * thrice(second)
            rest = groups[p] - (thrice(left[0]) * line + thrice(right[0]) * below)
            groups[p] = jnp.where(wide == k, top, jnp.where(wide == k + 1, low, jnp.where(wide > k + 1, rest, groups[p])))
            for g in range(p, 8):
                cols[g, k + 1] = (cols[g, k + 1] - ratio * cols[g, k]) * second
                cols[g, k] = cols[g, k] * first
        lines = [spread(groups[p], k) for k in range(8)]
        for g in range(p + 1, 8):
            acc = groups[g]
            for k in range(8):
                acc = acc - thrice(cols[g, k]) * lines[k]
            groups[g] = acc
    for g in range(4 * (piece % 2), 8):
        u[base + 8 * g:base + 8 * g + 8, :] = groups[g]
    if piece % 2 and piece < 7:
        block = u[base:base + 64, :]
        first = 0 if base == 0 else 128
        update = jnp.dot(block[:, first:256].T, block, precision=HIGH, preferred_element_type=F32)
        rest = base + 64
        u[rest:256, :] = u[rest:256, :] - update[rest - first:256 - first, :]


def gather_kernel(
    tokens_hbm, gate_hbm, up_hbm, rows_out, cols_out, lead_out, own_out,
    held, weights, total, rows, cols, leads,
    load_sem, send_sem, recv_sem, send2, recv2, side_send, side_recv, lead_send, lead_recv, local_sem,
):
    tok, row, col = lax.axis_index("tok"), lax.axis_index("row"), lax.axis_index("col")
    x, z_lo, z_hi, y = lax.div(row, 2), lax.rem(row, 2), lax.div(col, 4), lax.rem(col, 4)

    def around(at):
        return {0: at, 1: lax.rem(at + 1, 4), 2: lax.rem(at + 2, 4), -1: lax.rem(at + 3, 4)}

    xs, zs, ys = around(x), around(z_hi), around(y)
    places = {(h, j): zs[h] * 4 + ys[j] for h in OFFSETS for j in OFFSETS}
    quarters = {d: xs[d] * QUARTER for d in OFFSETS}
    groups = {(d, z): xs[d] * 2 + z for d in OFFSETS for z in (0, 1)}
    firsts = {h: zs[h] * 4 for h in OFFSETS}
    spots = {d: lax.rem(xs[d], 2) * 2 for d in OFFSETS}
    keeps = {d: lax.div(xs[d], 2) == tok for d in OFFSETS}
    partner_row = x * 2 + 1 - z_lo

    devices = {"zl": (tok, partner_row, col)}
    for sign, d in (("+", 1), ("-", -1)):
        devices["x" + sign] = (tok, xs[d] * 2 + z_lo, col)
        devices["y" + sign] = (tok, row, places[0, d])
        devices["z" + sign] = (tok, row, places[d, 0])
    sibling = (1 - tok, row, col)
    step = {
        ("u", 0): devices["zl"], ("u", 1): (tok, partner_row, places[1, 0]),
        ("d", 0): (tok, partner_row, places[-1, 0]), ("d", 1): devices["zl"],
    }
    low = y < 2
    at_z = {k: jnp.logical_and(low, z_hi == k) for k in range(4)}
    past_first = jnp.logical_and(low, z_hi > 0)
    at_y = {k: y == k for k in range(4)}

    first = pltpu.make_async_copy(tokens_hbm, held.at[col], load_sem.at[2])
    first.start()
    loads = [
        pltpu.make_async_copy(gate_hbm, weights.at[:, 0:128], load_sem.at[0]),
        pltpu.make_async_copy(up_hbm, weights.at[:, 128:256], load_sem.at[1]),
    ]
    for load in loads:
        load.start()

    barrier = pltpu.get_barrier_semaphore()
    far = (tok, partner_row, places[1, 0] * z_lo + places[-1, 0] * (1 - z_lo))
    near = [devices[k] for k in ("x+", "x-", "y+", "y-", "z+", "z-", "zl")] + [far, sibling]
    for device in near:
        pl.semaphore_signal(barrier, inc=1, device_id=device, device_id_type=MESH)
    pl.semaphore_wait(barrier, len(near))
    first.wait()

    tokens, ready = token_moves()
    hiddens, row_groups, pairs = hidden_moves()
    number = {name: at for at, name in enumerate(tokens)}
    number.update({name: at for at, name in enumerate(n for n in hiddens if hiddens[n].role[0] in ("rows", "cols"))})

    def span(at_rows):
        if at_rows[0] is None:
            return pl.ds(at_rows[1], at_rows[2])
        return pl.ds(pl.multiple_of(quarters[at_rows[0]] + at_rows[1], 16), at_rows[2])

    def remote(semaphores, index, source, target, device):
        return pltpu.make_async_remote_copy(
            src_ref=source, dst_ref=target, send_sem=semaphores[0].at[0], recv_sem=semaphores[1].at[index],
            device_id=device, device_id_type=MESH,
        )

    def held_ref(spot, at_rows):
        return held.at[places[spot], span(at_rows), :]

    def block_ref(move, at, parity):
        kind, which = move.role[0], move.role[4]
        if kind == "rows":
            return rows.at[places[at]] if which is None else rows.at[places[at], pl.ds(64 * which, 64), :]
        z = {"mine": parity, "other": 1 - parity}.get(at[1], at[1])
        if which is None:
            return cols.at[groups[at[0], z]]
        size = 128 // PIECES
        return cols.at[groups[at[0], z], pl.ds(size * which, size), :]

    def outgoing(move, name, parity):
        if move.role is not None:
            place = block_ref(move, move.role[1], parity)
            return remote((send2, recv2), number[name], place, place, devices[move.role[3]])
        place = held_ref(move.source[parity], move.rows)
        device = step[move.link, parity] if move.link in "ud" else devices[move.link]
        return remote((send_sem, recv_sem), number[name], place, place, device)

    def incoming(move, name, parity):
        if move.role is not None:
            place = block_ref(move, move.role[2], parity)
            return remote((send2, recv2), number[name], place, place, sibling)
        place = held_ref(move.target, move.target_rows)
        return remote((send_sem, recv_sem), number[name], place, place, sibling)

    def lead(b, p):
        size = 128 // PIECES
        return leads.at[b, pl.ds(size * p, size), :]

    def lead_copy(kind, b, p, device, from_cols=False):
        size = 128 // PIECES
        return pltpu.make_async_remote_copy(
            src_ref=cols.at[0, pl.ds(size * p, size), :] if from_cols else lead(b, p), dst_ref=lead(b, p),
            send_sem=lead_send.at[kind * PIECES + p],
            recv_sem=lead_recv.at[b * PIECES + p],
            device_id=device, device_id_type=MESH,
        )

    def lead_arrive(b, p):
        lead_copy(0, b, p, sibling).wait_recv()

    def chain_role(hop, parity):
        if hop == 1:
            return at_z[0], step["u" if parity == 1 else "d", parity]
        upward = (hop == 2) == (parity == 0)
        return at_z[1 if upward else 3], step["u" if upward else "d", parity]

    relays = ((3, 0, "y-"), (2, 1, "y+"))

    def lead_start(role, parity):
        if role[0] == "chain":
            hop, p = role[1:]
            here, device = chain_role(hop, parity)

            @pl.when(here)
            def _():
                if hop > 1:
                    lead_arrive(y, p)
                lead_copy(0, y, p, device, hop == 1).start()
        elif role[0] == "spread":
            p = role[1]

            @pl.when(at_z[0])
            def _():
                lead_copy(1, y, p, devices["y+"], True).start()
                lead_copy(2, y, p, devices["y-"], True).start()

            @pl.when(at_z[2])
            def _():
                lead_arrive(y, p)

            @pl.when(past_first)
            def _():
                lead_copy(1, y, p, devices["y+"]).start()
                lead_copy(2, y, p, devices["y-"]).start()
        else:
            p = role[1]
            for k, b, way in relays:
                @pl.when(at_y[k])
                def _():
                    lead_arrive(b, p)
                    lead_copy(3, b, p, devices[way]).start()

    def lead_end(parity):
        for p in range(PIECES):
            for hop in (1, 2, 3):
                here, device = chain_role(hop, parity)

                @pl.when(here)
                def _():
                    lead_copy(0, y, p, device).wait_send()

            @pl.when(low)
            def _():
                lead_copy(1, y, p, devices["y+"]).wait_send()
                lead_copy(2, y, p, devices["y-"]).wait_send()

            for k, b, way in relays:
                @pl.when(at_y[k])
                def _():
                    lead_copy(3, b, p, devices[way]).wait_send()

    def side(index, source, target):
        return pltpu.make_async_remote_copy(
            src_ref=source, dst_ref=target, send_sem=side_send.at[index], recv_sem=side_recv.at[index],
            device_id=sibling, device_id_type=MESH,
        )

    def keep(index, source, target):
        return pltpu.make_async_copy(source, target, local_sem.at[index])

    shared = {}
    for k, h in enumerate(OFFSETS):
        shared["r", h] = (row_groups[h], k)
        shared["c", h] = (pairs[h], 4 + k)

    def side_refs(kind, d):
        if kind == "r":
            at = pl.ds(firsts[d], 4)
            return rows.at[at], (lambda t: rows_out.at[t, at])
        if kind == "c":
            return cols.at[pl.ds(groups[d, 0], 2)], (lambda t: cols_out.at[t, pl.ds(spots[d], 2)])
        if kind == "l":
            return leads, (lambda t: lead_out.at[t])
        return rows.at[col], (lambda t: own_out.at[t])

    def side_start(kind, d, index):
        source, target = side_refs(kind, d)
        if kind != "c":
            side(index, source, target(tok)).start()
            keep(index, source, target(tok)).start()
            return

        @pl.when(keeps[d])
        def _():
            keep(index, source, target(tok)).start()

        @pl.when(jnp.logical_not(keeps[d]))
        def _():
            side(index, source, target(tok)).start()

    def side_end(kind, d, index):
        source, target = side_refs(kind, d)
        if kind != "c":
            side(index, target(1 - tok), target(1 - tok)).wait_recv()
            side(index, source, target(tok)).wait_send()
            keep(index, source, target(tok)).wait()
            return

        @pl.when(keeps[d])
        def _():
            keep(index, source, target(tok)).wait()
            side(index, target(1 - tok), target(1 - tok)).wait_recv()

        @pl.when(jnp.logical_not(keeps[d]))
        def _():
            side(index, source, target(tok)).wait_send()

    def both(act):
        for parity in (0, 1):
            pl.when(z_lo == parity)(functools.partial(act, parity))

    def in_order(begun):
        return [sorted((begun[parity][name], name) for name in begun[parity]) for parity in (0, 1)]

    begun, landed = schedule(tokens)
    order = in_order(begun)
    seen, at = (set(), set()), [0, 0]

    def arrive(moves, name, parity):
        if name not in seen[parity]:
            seen[parity].add(name)
            if name in number:
                incoming(moves[name], name, parity).wait_recv()

    def stretch(until, batch, parity):
        while at[parity] < len(order[parity]) and order[parity][at[parity]][0] <= until:
            name = order[parity][at[parity]][1]
            at[parity] += 1
            for need in tokens[name].needs[parity]:
                arrive(tokens, need, parity)
            outgoing(tokens[name], name, parity).start()
        for chunk in batch:
            for need in ready[chunk]:
                arrive(tokens, need, parity)

    finished = {c: max(landed[p][name] for p in (0, 1) for name in ready[c]) for c in ready}
    queue = sorted(ready, key=lambda c: (finished[c], c))
    start = 0
    for k, size in enumerate(BATCHES):
        batch = queue[start:start + size]
        start += size
        until = max(finished[c] for c in batch) + AHEAD if start < len(queue) else 1e9
        both(functools.partial(stretch, until, batch))
        if k == 0:
            for load in loads:
                load.wait()
            total[...] = jnp.zeros_like(total)
        for here in ([col] if k == 0 else []) + [places[chunk] for chunk in batch]:
            total[...] += jnp.dot(held[here], weights[pl.ds(pl.multiple_of(here * 512, 512), 512), :], preferred_element_type=F32)

    def tokens_end(parity):
        for name in tokens:
            arrive(tokens, name, parity)

    both(tokens_end)
    gate = total[:, 0:128]
    hidden = gate / (1.0 + jnp.exp(-gate)) * total[:, 128:256]
    hidden = hidden.T.astype(jnp.bfloat16)
    rows[col] = hidden
    cols[row] = hidden

    begun, landed = schedule(hiddens)
    order = in_order(begun)
    left = (dict(shared), dict(shared))

    def hidden_stage(parity):
        waited = False
        for _, name in order[parity]:
            move = hiddens[name]
            if move.needs[parity] and not waited:
                waited = True
                side_start("o", 0, 8)
            for need in move.needs[parity]:
                arrive(hiddens, need, parity)
            if move.role[0] in ("rows", "cols"):
                outgoing(move, name, parity).start()
            else:
                lead_start(move.role, parity)
            for key in list(left[parity]):
                names, index = left[parity][key]
                if seen[parity].issuperset(names):
                    del left[parity][key]
                    side_start(*key, index)
        for key in list(left[parity]):
            names, index = left[parity].pop(key)
            for name in names:
                arrive(hiddens, name, parity)
            side_start(*key, index)
        for name in hiddens:
            arrive(hiddens, name, parity)

    both(hidden_stage)
    held_lead = pltpu.make_async_copy(cols.at[0], leads.at[lax.rem(y, 2)], local_sem.at[10])

    @pl.when(at_z[0])
    def _():
        held_lead.start()

    for p in range(PIECES):
        for k, b in ((0, 1), (1, 0), (2, 0), (3, 1)):
            @pl.when(at_y[k])
            def _():
                lead_arrive(b, p)

    @pl.when(at_z[0])
    def _():
        held_lead.wait()

    side_start("l", 0, 9)

    remote((send_sem, recv_sem), 0, held.at[pl.ds(0, 15)], held.at[pl.ds(0, 15)], sibling).wait_send()
    gone = weights.at[pl.ds(0, 5632), :]
    remote((send2, recv2), 0, gone, gone, sibling).wait_send()
    both(lead_end)
    for kind, d in shared:
        side_end(kind, d, shared[kind, d][1])
    side_end("o", 0, 8)
    side_end("l", 0, 9)


def gather(tokens, gate_weight, up_weight):
    depth, width = gate_weight.shape
    half = tokens.shape[0]
    bf16 = jnp.bfloat16
    hbm = pl.BlockSpec(memory_space=pl.ANY)
    return pl.pallas_call(
        gather_kernel,
        out_shape=(
            jax.ShapeDtypeStruct((2, 16, width, half), bf16),
            jax.ShapeDtypeStruct((2, 4, width, half), bf16),
            jax.ShapeDtypeStruct((2, 2, width, half), bf16),
            jax.ShapeDtypeStruct((2, width, half), bf16),
        ),
        in_specs=[hbm, hbm, hbm],
        out_specs=(hbm,) * 4,
        scratch_shapes=[
            pltpu.VMEM((16, half, 512), bf16),
            pltpu.VMEM((depth, 2 * width), bf16),
            pltpu.VMEM((half, 2 * width), F32),
            pltpu.VMEM((16, width, half), bf16),
            pltpu.VMEM((8, width, half), bf16),
            pltpu.VMEM((2, width, half), bf16),
            pltpu.SemaphoreType.DMA((3,)),
            pltpu.SemaphoreType.DMA((1,)),
            pltpu.SemaphoreType.DMA((120,)),
            pltpu.SemaphoreType.DMA((1,)),
            pltpu.SemaphoreType.DMA((55,)),
            pltpu.SemaphoreType.DMA((10,)),
            pltpu.SemaphoreType.DMA((10,)),
            pltpu.SemaphoreType.DMA((4 * PIECES,)),
            pltpu.SemaphoreType.DMA((2 * PIECES,)),
            pltpu.SemaphoreType.DMA((11,)),
        ],
        compiler_params=pltpu.CompilerParams(
            collective_id=0, has_side_effects=True, vmem_limit_bytes=60 * 2**20
        ),
        cost_estimate=pl.CostEstimate(flops=2 * half * depth * 2 * width, bytes_accessed=12 * 2**20, transcendentals=half * width),
    )(tokens, gate_weight, up_weight)


def gram_kernel(rows_hbm, cols_hbm, lead_ref, own_ref, gram_ref, panel_ref, u, rows, cols, sems):
    step = pl.program_id(0)

    def fetch(k):
        if k == 8:
            return pltpu.make_async_copy(cols_hbm, cols, sems.at[8])
        pair = pl.ds(2 * k, 2)
        return pltpu.make_async_copy(rows_hbm.at[:, pair], rows.at[:, pair], sems.at[k])

    def product(left, right):
        return sum(lax.dot_general(left(t), right(t), NT, preferred_element_type=F32) for t in (0, 1))

    def tile(k):
        fetch(k).wait()
        whole = product(lambda t: rows[t, 2 * k:2 * k + 2].reshape(256, 512), lambda t: cols[t].reshape(512, 512))
        for a in range(4):
            gram_ref[a] = whole[:, 128 * a:128 * a + 128]

    @pl.when(step == 0)
    def _():
        for k in (8, 0, 1, 2, 3, 4, 5, 6, 7):
            fetch(k).start()

        def lead(t):
            return lead_ref[t].reshape(256, 512)

        u[:, 0:256] = product(lead, lead)
        u[:, 256:384] = product(lead, lambda t: own_ref[t])
        balance(u)
        eliminate(u, 0)
        fetch(8).wait()
        tile(0)

    for k in range(1, 8):
        @pl.when(step == k)
        def _():
            tile(k)
            eliminate(u, k)

    @pl.when(step == 7)
    def _():
        panel_ref[...] = u[pl.ds(pl.multiple_of(lax.axis_index("tok") * 128, 128), 128), 256:384].T


def gram_and_panel(rows, cols, lead, own):
    width, half = rows.shape[2:]
    hbm = pl.BlockSpec(memory_space=pl.ANY)
    return pl.pallas_call(
        gram_kernel,
        grid=(8,),
        out_shape=(
            jax.ShapeDtypeStruct((4, 16 * width, width), F32),
            jax.ShapeDtypeStruct((width, width), F32),
        ),
        in_specs=[
            hbm,
            hbm,
            pl.BlockSpec((2, 2, width, half), lambda s: (0, 0, 0, 0)),
            pl.BlockSpec((2, width, half), lambda s: (0, 0, 0)),
        ],
        out_specs=(
            pl.BlockSpec((4, 2 * width, width), lambda s: (0, s, 0)),
            pl.BlockSpec((width, width), lambda s: (0, 0)),
        ),
        scratch_shapes=[
            pltpu.VMEM((PANEL, 384), F32),
            pltpu.VMEM((2, 16, width, half), jnp.bfloat16),
            pltpu.VMEM((2, 4, width, half), jnp.bfloat16),
            pltpu.SemaphoreType.DMA((9,)),
        ],
        compiler_params=pltpu.CompilerParams(vmem_limit_bytes=60 * 2**20),
        cost_estimate=pl.CostEstimate(flops=2 * 2048 * 512 * 1024, bytes_accessed=10 * 2**20, transcendentals=0),
    )(rows, cols, lead, own)


def local(tokens, gate_weight, up_weight):
    gram, panel = gram_and_panel(*gather(tokens, gate_weight, up_weight))
    return (gram.reshape(4, 2048, 1, 128), panel)


def solution(mesh):
    placed = (P("tok", "col"), P(None, ("row", "col")), P(None, ("row", "col")))
    return jax.shard_map(
        local,
        mesh=mesh,
        in_specs=placed,
        out_specs=(P("tok", "row", "col", None), P(("row", "col"), "tok")),
        check_vma=False,
    )
```

```python
import functools

import jax
import jax.numpy as jnp
from jax import lax
from jax.experimental import pallas as pl
from jax.experimental.pallas import tpu as pltpu
from jax.sharding import PartitionSpec as P

PANEL = 256
HIGH = lax.Precision.HIGHEST
MESH = pl.DeviceIdType.MESH
OFFSETS = (0, -1, 1, 2)
NT = (((1,), (1,)), ((), ()))
F32 = jnp.float32

ROWS = 512
QUARTER = 64
FIRST_Y = (256, 96)
FIRST_Z = (352, 160)
PIECES = 4
BATCHES = (2, 2, 2, 2, 2, 2, 1, 1, 1)
RATE, HOP, ISSUE, AHEAD = 49.0, 2.0, 0.14, 0.5


class Move:
    def __init__(self, link, size, needs, source=None, target=None, rows=None, target_rows=None, role=None):
        self.link, self.size, self.needs = link, size, needs
        self.source, self.target, self.rows, self.target_rows, self.role = source, target, rows, target_rows, role


def part(rows, which):
    first = (rows[2] // 2 + 15) // 16 * 16
    return (rows[0], rows[1] + first, rows[2] - first) if which == "b" else (rows[0], rows[1], first)


def token_moves():
    moves, arrivals = {}, {}

    def add(name, link, needs0, needs1, source, target, rows, target_rows=None):
        moves[name] = Move(link, rows[2], (tuple(needs0), tuple(needs1)), source, target, rows, target_rows or rows)

    def along_z(tag, rows, j, have):
        up, far_up, down, far_down = [tag + k for k in ("u1", "u2", "d1", "d2")]
        at = {h: (h, j) for h in OFFSETS}
        add(up, "u", [up], have, (at[-1], at[0]), at[-1], rows)
        add(far_up, "u", [far_up], [up], (at[2], at[-1]), at[2], part(rows, "a"))
        add(down, "d", have, [down], (at[0], at[1]), at[1], rows)
        add(far_down, "d", [down], [far_down], (at[1], at[2]), at[2], part(rows, "b"))
        return {0: list(have), -1: [up], 1: [down], 2: [far_up, far_down]}

    def along_y(tag, rows, h, have):
        right, left, far_right, far_left = [tag + k for k in ("y+1", "y-1", "y+2", "y-2")]
        at = {j: (h, j) for j in OFFSETS}
        add(right, "y+", have, have, (at[0],) * 2, at[-1], rows)
        add(left, "y-", have, have, (at[0],) * 2, at[1], rows)
        add(far_right, "y+", [right], [right], (at[-1],) * 2, at[2], part(rows, "a"))
        add(far_left, "y-", [left], [left], (at[1],) * 2, at[2], part(rows, "b"))
        return {0: list(have), -1: [right], 1: [left], 2: [far_right, far_left]}

    for tag, rows in (("q", (0, 0, QUARTER)), ("f", (None,) + FIRST_Y)):
        near = along_y(tag, rows, 0, [])
        for j in OFFSETS:
            for h, names in along_z(tag + "%d" % j, rows, j, near[j]).items():
                arrivals[tag, h, j] = names
    near = along_z("s", (None,) + FIRST_Z, 0, [])
    for h in OFFSETS:
        for j, names in along_y("s%d" % h, (None,) + FIRST_Z, h, near[h]).items():
            arrivals["s", h, j] = names
    ready = {}
    own, before, after, across = [(d, 0, QUARTER) for d in (0, -1, 1, 2)]
    for spot in [(h, j) for h in OFFSETS for j in OFFSETS][1:]:
        have = arrivals[("q",) + spot]
        right, left, far_right, far_left = ["x%d,%d" % spot + k for k in ("x+1", "x-1", "x+2", "x-2")]
        add(right, "x+", have, have, (spot,) * 2, spot, own, before)
        add(left, "x-", have, have, (spot,) * 2, spot, own, after)
        add(far_right, "x+", [right], [right], (spot,) * 2, spot, part(before, "a"), part(across, "a"))
        add(far_left, "x-", [left], [left], (spot,) * 2, spot, part(after, "b"), part(across, "b"))
        ready[spot] = [n for kind in "qfs" for n in arrivals[(kind,) + spot]] + [right, left, far_right, far_left]
    return moves, ready


def hidden_moves():
    moves, piece, block = {}, 128 // PIECES, 128
    every = range(PIECES)

    def add(name, link, size, needs, role):
        moves[name] = Move(link, size, (tuple(needs),) * 2, role=role)

    for p in every:
        add("zl%d" % p, "zl", piece, [], ("cols", (0, "mine"), (0, "other"), "zl", p))
        for sign, d in (("+", 1), ("-", -1)):
            add("xo%s%d" % (sign, p), "x" + sign, piece, [], ("cols", (0, "mine"), (-d, "mine"), "x" + sign, p))
            add("xp%s%d" % (sign, p), "x" + sign, piece, ["zl%d" % p], ("cols", (0, "other"), (-d, "other"), "x" + sign, p))
        add("xr+%d" % p, "x+", piece, ["xo+%d" % p, "xp+%d" % p], ("cols", (-1, 0), (2, 0), "x+", p))
    add("xr-", "x-", block, ["x%s-%d" % (k, p) for k in "op" for p in every], ("cols", (1, 1), (2, 1), "x-", None))
    gone = {0: [], -1: ["z+"], 1: ["z-"], 2: ["zr+", "zr-"]}
    for relayed, (sign, d) in enumerate((("+", 1), ("-", -1))):
        link = "u" if d == 1 else "d"
        add("z" + sign, link, 2 * block, [], ("rows", (0, 0), (-d, 0), "z" + sign, None))
        add("zr" + sign, link, block, ["z" + sign], ("rows", (-d, 0), (2, 0), "z" + sign, relayed))
        for h in OFFSETS:
            add("y%d" % h + sign, "y" + sign, block, gone[h], ("rows", (h, 0), (h, -d), "y" + sign, None))
            add("y%dr" % h + sign, "y" + sign, block // 2, ["y%d" % h + sign], ("rows", (h, -d), (h, 2), "y" + sign, relayed))
    for p in every:
        first = [name % p for name in ("zl%d", "xo+%d", "xo-%d", "xp+%d", "xp-%d", "xr+%d")]
        for hop in (1, 2, 3):
            add("c%d%d" % (hop, p), "c%d" % hop, piece, first if hop == 1 else ["c%d%d" % (hop - 1, p)], ("chain", hop, p))
        add("l%d" % p, "l", piece, ["c3%d" % p], ("spread", p))
        add("m%d" % p, "m", piece, ["l%d" % p], ("relay", p))
    row_groups = {h: gone[h] + ["y%d" % h + k + sign for k in ("", "r") for sign in "+-"] for h in OFFSETS}
    pairs = {0: ["zl%d" % p for p in every], 2: ["xr-"] + ["xr+%d" % p for p in every]}
    for sign, d in (("+", -1), ("-", 1)):
        pairs[d] = ["x%s%s%d" % (k, sign, p) for k in "op" for p in every]
    return moves, row_groups, pairs


def schedule(moves):
    followers = {name: set() for name in moves}
    for name, move in moves.items():
        for parity in (0, 1):
            for need in move.needs[parity]:
                followers[need].add((name, parity))

    def there(name, parity):
        return 1 - parity if moves[name].role is None and moves[name].link in "ud" else parity

    @functools.lru_cache(None)
    def rest(name, parity):
        after = [moves[m].size / RATE + HOP + rest(m, there(m, q)) for m, q in followers[name] if q == parity]
        return max(after, default=0.0)

    landed, begun, free = ({}, {}), ({}, {}), {}
    waiting = {(name, parity) for name in moves for parity in (0, 1)}
    while waiting:
        best = None
        for name, parity in waiting:
            move, have = moves[name], landed[parity]
            when = max(free.get((move.link, parity), 0.0), free.get(parity, 0.0))
            for need in move.needs[parity]:
                if need not in have:
                    break
                when = max(when, have[need])
            else:
                key = (when, -(rest(name, there(name, parity)) + move.size / RATE), name, parity)
                if best is None or key < best:
                    best = key
        when, _, name, parity = best
        done = when + moves[name].size / RATE
        free[moves[name].link, parity] = done
        free[parity] = when + ISSUE
        begun[parity][name] = when
        landed[there(name, parity)][name] = done + HOP
        waiting.discard((name, parity))
    return begun, landed


def balance(u):
    rows = lax.broadcasted_iota(jnp.int32, (PANEL, PANEL), 0)
    lanes = lax.broadcasted_iota(jnp.int32, (PANEL, PANEL), 1)
    corner = u[:, 0:PANEL]
    only = jnp.where(rows == lanes, corner, 0.0)
    down, across = lax.rsqrt(jnp.sum(only, axis=1, keepdims=True)), lax.rsqrt(jnp.sum(only, axis=0, keepdims=True))
    u[:, 0:PANEL] = corner * down * across
    u[:, PANEL:] = u[:, PANEL:] * down


def eliminate(u, piece, beside):
    wide = lax.broadcasted_iota(jnp.int32, (8, 384), 0)
    base = 64 * (piece // 2)
    groups = [u[base + 8 * g:base + 8 * g + 8, :] for g in range(8)]

    def spread(row, at):
        return jnp.broadcast_to(row[at:at + 1, :], (8, row.shape[1]))

    def thrice(tile):
        return jnp.concatenate([tile] * 3, axis=1)

    for p in range(4 * (piece % 2), 4 * (piece % 2) + 4):
        cols = {
            (g, k): jnp.broadcast_to(groups[g][:, base + 8 * p + k:base + 8 * p + k + 1], (8, 128))
            for g in range(p, 8) for k in range(8)
        }
        for k in range(0, 8, 2):
            a, b, c = spread(cols[p, k], k), spread(cols[p, k + 1], k), spread(cols[p, k + 1], k + 1)
            over = 1.0 / (a * c - b * b)
            left, right = [], []
            for g in range(p, 8):
                left.append((c * cols[g, k] - b * cols[g, k + 1]) * over)
                right.append((a * cols[g, k + 1] - b * cols[g, k]) * over)
            for j in range(k + 2, 8):
                one, two = spread(cols[p, k], j), spread(cols[p, k + 1], j)
                for g in range(p, 8):
                    cols[g, j] = cols[g, j] - (left[g - p] * one + right[g - p] * two)
            first = lax.rsqrt(a)
            ratio = b * first * first
            second = lax.rsqrt(c - b * ratio)
            line, below = spread(groups[p], k), spread(groups[p], k + 1)
            top = line * thrice(first)
            low = (below - thrice(ratio) * line) * thrice(second)
            rest = groups[p] - (thrice(left[0]) * line + thrice(right[0]) * below)
            groups[p] = jnp.where(wide == k, top, jnp.where(wide == k + 1, low, jnp.where(wide > k + 1, rest, groups[p])))
            for g in range(p, 8):
                cols[g, k + 1] = (cols[g, k + 1] - ratio * cols[g, k]) * second
                cols[g, k] = cols[g, k] * first
        lines = [spread(groups[p], k) for k in range(8)]
        for g in range(p + 1, 8):
            acc = groups[g]
            for k in range(8):
                acc = acc - thrice(cols[g, k]) * lines[k]
            groups[g] = acc
        beside(p % 4)
    for g in range(4 * (piece % 2), 8):
        u[base + 8 * g:base + 8 * g + 8, :] = groups[g]
    if piece % 2 and piece < 7:
        block = u[base:base + 64, :]
        first = 0 if base == 0 else 128
        update = jnp.dot(block[:, first:256].T, block, precision=HIGH, preferred_element_type=F32)
        rest = base + 64
        u[rest:256, :] = u[rest:256, :] - update[rest - first:256 - first, :]


def gather_kernel(
    tokens_hbm, gate_hbm, up_hbm, rows_out, cols_out, lead_out, own_out,
    held, weights, total, rows, cols, leads,
    load_sem, send_sem, recv_sem, send2, recv2, side_send, side_recv, lead_send, lead_recv, local_sem,
):
    tok, row, col = lax.axis_index("tok"), lax.axis_index("row"), lax.axis_index("col")
    x, z_lo, z_hi, y = lax.div(row, 2), lax.rem(row, 2), lax.div(col, 4), lax.rem(col, 4)

    def around(at):
        return {0: at, 1: lax.rem(at + 1, 4), 2: lax.rem(at + 2, 4), -1: lax.rem(at + 3, 4)}

    xs, zs, ys = around(x), around(z_hi), around(y)
    places = {(h, j): zs[h] * 4 + ys[j] for h in OFFSETS for j in OFFSETS}
    quarters = {d: xs[d] * QUARTER for d in OFFSETS}
    groups = {(d, z): xs[d] * 2 + z for d in OFFSETS for z in (0, 1)}
    firsts = {h: zs[h] * 4 for h in OFFSETS}
    spots = {d: lax.rem(xs[d], 2) * 2 for d in OFFSETS}
    keeps = {d: lax.div(xs[d], 2) == tok for d in OFFSETS}
    partner_row = x * 2 + 1 - z_lo

    devices = {"zl": (tok, partner_row, col)}
    for sign, d in (("+", 1), ("-", -1)):
        devices["x" + sign] = (tok, xs[d] * 2 + z_lo, col)
        devices["y" + sign] = (tok, row, places[0, d])
        devices["z" + sign] = (tok, row, places[d, 0])
    sibling = (1 - tok, row, col)
    step = {
        ("u", 0): devices["zl"], ("u", 1): (tok, partner_row, places[1, 0]),
        ("d", 0): (tok, partner_row, places[-1, 0]), ("d", 1): devices["zl"],
    }
    low = y < 2
    at_z = {k: jnp.logical_and(low, z_hi == k) for k in range(4)}
    past_first = jnp.logical_and(low, z_hi > 0)
    at_y = {k: y == k for k in range(4)}

    first = pltpu.make_async_copy(tokens_hbm, held.at[col], load_sem.at[2])
    first.start()
    loads = [
        pltpu.make_async_copy(gate_hbm, weights.at[:, 0:128], load_sem.at[0]),
        pltpu.make_async_copy(up_hbm, weights.at[:, 128:256], load_sem.at[1]),
    ]
    for load in loads:
        load.start()

    barrier = pltpu.get_barrier_semaphore()
    far = (tok, partner_row, places[1, 0] * z_lo + places[-1, 0] * (1 - z_lo))
    near = [devices[k] for k in ("x+", "x-", "y+", "y-", "z+", "z-", "zl")] + [far, sibling]
    for device in near:
        pl.semaphore_signal(barrier, inc=1, device_id=device, device_id_type=MESH)
    pl.semaphore_wait(barrier, len(near))
    first.wait()

    tokens, ready = token_moves()
    hiddens, row_groups, pairs = hidden_moves()
    number = {name: at for at, name in enumerate(tokens)}
    number.update({name: at for at, name in enumerate(n for n in hiddens if hiddens[n].role[0] in ("rows", "cols"))})

    def span(at_rows):
        if at_rows[0] is None:
            return pl.ds(at_rows[1], at_rows[2])
        return pl.ds(pl.multiple_of(quarters[at_rows[0]] + at_rows[1], 16), at_rows[2])

    def remote(semaphores, index, source, target, device):
        return pltpu.make_async_remote_copy(
            src_ref=source, dst_ref=target, send_sem=semaphores[0].at[0], recv_sem=semaphores[1].at[index],
            device_id=device, device_id_type=MESH,
        )

    def held_ref(spot, at_rows):
        return held.at[places[spot], span(at_rows), :]

    def block_ref(move, at, parity):
        kind, which = move.role[0], move.role[4]
        if kind == "rows":
            return rows.at[places[at]] if which is None else rows.at[places[at], pl.ds(64 * which, 64), :]
        z = {"mine": parity, "other": 1 - parity}.get(at[1], at[1])
        if which is None:
            return cols.at[groups[at[0], z]]
        size = 128 // PIECES
        return cols.at[groups[at[0], z], pl.ds(size * which, size), :]

    def outgoing(move, name, parity):
        if move.role is not None:
            place = block_ref(move, move.role[1], parity)
            return remote((send2, recv2), number[name], place, place, devices[move.role[3]])
        place = held_ref(move.source[parity], move.rows)
        device = step[move.link, parity] if move.link in "ud" else devices[move.link]
        return remote((send_sem, recv_sem), number[name], place, place, device)

    def incoming(move, name, parity):
        if move.role is not None:
            place = block_ref(move, move.role[2], parity)
            return remote((send2, recv2), number[name], place, place, sibling)
        place = held_ref(move.target, move.target_rows)
        return remote((send_sem, recv_sem), number[name], place, place, sibling)

    def lead(b, p):
        size = 128 // PIECES
        return leads.at[b, pl.ds(size * p, size), :]

    def lead_copy(kind, b, p, device, from_cols=False):
        size = 128 // PIECES
        return pltpu.make_async_remote_copy(
            src_ref=cols.at[0, pl.ds(size * p, size), :] if from_cols else lead(b, p), dst_ref=lead(b, p),
            send_sem=lead_send.at[kind * PIECES + p],
            recv_sem=lead_recv.at[b * PIECES + p],
            device_id=device, device_id_type=MESH,
        )

    def lead_arrive(b, p):
        lead_copy(0, b, p, sibling).wait_recv()

    def chain_role(hop, parity):
        if hop == 1:
            return at_z[0], step["u" if parity == 1 else "d", parity]
        upward = (hop == 2) == (parity == 0)
        return at_z[1 if upward else 3], step["u" if upward else "d", parity]

    relays = ((3, 0, "y-"), (2, 1, "y+"))

    def lead_start(role, parity):
        if role[0] == "chain":
            hop, p = role[1:]
            here, device = chain_role(hop, parity)

            @pl.when(here)
            def _():
                if hop > 1:
                    lead_arrive(y, p)
                lead_copy(0, y, p, device, hop == 1).start()
        elif role[0] == "spread":
            p = role[1]

            @pl.when(at_z[0])
            def _():
                lead_copy(1, y, p, devices["y+"], True).start()
                lead_copy(2, y, p, devices["y-"], True).start()

            @pl.when(at_z[2])
            def _():
                lead_arrive(y, p)

            @pl.when(past_first)
            def _():
                lead_copy(1, y, p, devices["y+"]).start()
                lead_copy(2, y, p, devices["y-"]).start()
        else:
            p = role[1]
            for k, b, way in relays:
                @pl.when(at_y[k])
                def _():
                    lead_arrive(b, p)
                    lead_copy(3, b, p, devices[way]).start()

    def lead_end(parity):
        for p in range(PIECES):
            for hop in (1, 2, 3):
                here, device = chain_role(hop, parity)

                @pl.when(here)
                def _():
                    lead_copy(0, y, p, device).wait_send()

            @pl.when(low)
            def _():
                lead_copy(1, y, p, devices["y+"]).wait_send()
                lead_copy(2, y, p, devices["y-"]).wait_send()

            for k, b, way in relays:
                @pl.when(at_y[k])
                def _():
                    lead_copy(3, b, p, devices[way]).wait_send()

    def side(index, source, target):
        return pltpu.make_async_remote_copy(
            src_ref=source, dst_ref=target, send_sem=side_send.at[index], recv_sem=side_recv.at[index],
            device_id=sibling, device_id_type=MESH,
        )

    def keep(index, source, target):
        return pltpu.make_async_copy(source, target, local_sem.at[index])

    shared = {}
    for k, h in enumerate(OFFSETS):
        shared["r", h] = (row_groups[h], k)
        shared["c", h] = (pairs[h], 4 + k)

    def side_refs(kind, d):
        if kind == "r":
            at = pl.ds(firsts[d], 4)
            return rows.at[at], (lambda t: rows_out.at[t, at])
        if kind == "c":
            return cols.at[pl.ds(groups[d, 0], 2)], (lambda t: cols_out.at[t, pl.ds(spots[d], 2)])
        if kind == "l":
            return leads, (lambda t: lead_out.at[t])
        return rows.at[col], (lambda t: own_out.at[t])

    def side_start(kind, d, index):
        source, target = side_refs(kind, d)
        if kind != "c":
            side(index, source, target(tok)).start()
            keep(index, source, target(tok)).start()
            return

        @pl.when(keeps[d])
        def _():
            keep(index, source, target(tok)).start()

        @pl.when(jnp.logical_not(keeps[d]))
        def _():
            side(index, source, target(tok)).start()

    def side_end(kind, d, index):
        source, target = side_refs(kind, d)
        if kind != "c":
            side(index, target(1 - tok), target(1 - tok)).wait_recv()
            side(index, source, target(tok)).wait_send()
            keep(index, source, target(tok)).wait()
            return

        @pl.when(keeps[d])
        def _():
            keep(index, source, target(tok)).wait()
            side(index, target(1 - tok), target(1 - tok)).wait_recv()

        @pl.when(jnp.logical_not(keeps[d]))
        def _():
            side(index, source, target(tok)).wait_send()

    def both(act):
        for parity in (0, 1):
            pl.when(z_lo == parity)(functools.partial(act, parity))

    def in_order(begun):
        return [sorted((begun[parity][name], name) for name in begun[parity]) for parity in (0, 1)]

    begun, landed = schedule(tokens)
    order = in_order(begun)
    seen, at = (set(), set()), [0, 0]

    def arrive(moves, name, parity):
        if name not in seen[parity]:
            seen[parity].add(name)
            if name in number:
                incoming(moves[name], name, parity).wait_recv()

    def stretch(until, batch, parity):
        while at[parity] < len(order[parity]) and order[parity][at[parity]][0] <= until:
            name = order[parity][at[parity]][1]
            at[parity] += 1
            for need in tokens[name].needs[parity]:
                arrive(tokens, need, parity)
            outgoing(tokens[name], name, parity).start()
        for chunk in batch:
            for need in ready[chunk]:
                arrive(tokens, need, parity)

    finished = {c: max(landed[p][name] for p in (0, 1) for name in ready[c]) for c in ready}
    queue = sorted(ready, key=lambda c: (finished[c], c))
    start = 0
    for k, size in enumerate(BATCHES):
        batch = queue[start:start + size]
        start += size
        until = max(finished[c] for c in batch) + AHEAD if start < len(queue) else 1e9
        both(functools.partial(stretch, until, batch))
        if k == 0:
            for load in loads:
                load.wait()
            total[...] = jnp.zeros_like(total)
        for here in ([col] if k == 0 else []) + [places[chunk] for chunk in batch]:
            total[...] += jnp.dot(held[here], weights[pl.ds(pl.multiple_of(here * 512, 512), 512), :], preferred_element_type=F32)

    def tokens_end(parity):
        for name in tokens:
            arrive(tokens, name, parity)

    both(tokens_end)
    gate = total[:, 0:128]
    hidden = gate / (1.0 + jnp.exp(-gate)) * total[:, 128:256]
    hidden = hidden.T.astype(jnp.bfloat16)
    rows[col] = hidden
    cols[row] = hidden

    begun, landed = schedule(hiddens)
    order = in_order(begun)
    left = (dict(shared), dict(shared))

    def hidden_stage(parity):
        waited = False
        for _, name in order[parity]:
            move = hiddens[name]
            if move.needs[parity] and not waited:
                waited = True
                side_start("o", 0, 8)
            for need in move.needs[parity]:
                arrive(hiddens, need, parity)
            if move.role[0] in ("rows", "cols"):
                outgoing(move, name, parity).start()
            else:
                lead_start(move.role, parity)
            for key in list(left[parity]):
                names, index = left[parity][key]
                if seen[parity].issuperset(names):
                    del left[parity][key]
                    side_start(*key, index)
        for key in list(left[parity]):
            names, index = left[parity].pop(key)
            for name in names:
                arrive(hiddens, name, parity)
            side_start(*key, index)
        for name in hiddens:
            arrive(hiddens, name, parity)

    both(hidden_stage)
    held_lead = pltpu.make_async_copy(cols.at[0], leads.at[lax.rem(y, 2)], local_sem.at[10])

    @pl.when(at_z[0])
    def _():
        held_lead.start()

    for p in range(PIECES):
        for k, b in ((0, 1), (1, 0), (2, 0), (3, 1)):
            @pl.when(at_y[k])
            def _():
                lead_arrive(b, p)

    @pl.when(at_z[0])
    def _():
        held_lead.wait()

    side_start("l", 0, 9)

    remote((send_sem, recv_sem), 0, held.at[pl.ds(0, 15)], held.at[pl.ds(0, 15)], sibling).wait_send()
    gone = weights.at[pl.ds(0, 5632), :]
    remote((send2, recv2), 0, gone, gone, sibling).wait_send()
    both(lead_end)
    for kind, d in shared:
        side_end(kind, d, shared[kind, d][1])
    side_end("o", 0, 8)
    side_end("l", 0, 9)


def gather(tokens, gate_weight, up_weight):
    depth, width = gate_weight.shape
    half = tokens.shape[0]
    bf16 = jnp.bfloat16
    hbm = pl.BlockSpec(memory_space=pl.ANY)
    return pl.pallas_call(
        gather_kernel,
        out_shape=(
            jax.ShapeDtypeStruct((2, 16, width, half), bf16),
            jax.ShapeDtypeStruct((2, 4, width, half), bf16),
            jax.ShapeDtypeStruct((2, 2, width, half), bf16),
            jax.ShapeDtypeStruct((2, width, half), bf16),
        ),
        in_specs=[hbm, hbm, hbm],
        out_specs=(hbm,) * 4,
        scratch_shapes=[
            pltpu.VMEM((16, half, 512), bf16),
            pltpu.VMEM((depth, 2 * width), bf16),
            pltpu.VMEM((half, 2 * width), F32),
            pltpu.VMEM((16, width, half), bf16),
            pltpu.VMEM((8, width, half), bf16),
            pltpu.VMEM((2, width, half), bf16),
            pltpu.SemaphoreType.DMA((3,)),
            pltpu.SemaphoreType.DMA((1,)),
            pltpu.SemaphoreType.DMA((120,)),
            pltpu.SemaphoreType.DMA((1,)),
            pltpu.SemaphoreType.DMA((45,)),
            pltpu.SemaphoreType.DMA((10,)),
            pltpu.SemaphoreType.DMA((10,)),
            pltpu.SemaphoreType.DMA((4 * PIECES,)),
            pltpu.SemaphoreType.DMA((2 * PIECES,)),
            pltpu.SemaphoreType.DMA((11,)),
        ],
        compiler_params=pltpu.CompilerParams(
            collective_id=0, has_side_effects=True, vmem_limit_bytes=60 * 2**20
        ),
        cost_estimate=pl.CostEstimate(flops=2 * half * depth * 2 * width, bytes_accessed=12 * 2**20, transcendentals=half * width),
    )(tokens, gate_weight, up_weight)


def gram_kernel(rows_ref, cols_ref, lead_ref, own_ref, gram_ref, panel_ref, u):
    step = pl.program_id(0)

    def product(left, right):
        return sum(lax.dot_general(left(t), right(t), NT, preferred_element_type=F32) for t in (0, 1))

    def tile(panel):
        if panel % 2:
            return
        whole = product(
            lambda t: rows_ref[t].reshape(256, 512), lambda t: cols_ref[t, panel:panel + 2].reshape(256, 512)
        )
        for a in (0, 1):
            gram_ref[panel + a] = whole[:, 128 * a:128 * a + 128]

    @pl.when(step == 0)
    def _():
        def lead(t):
            return lead_ref[t].reshape(256, 512)

        u[:, 0:256] = product(lead, lead)
        u[:, 256:384] = product(lead, lambda t: own_ref[t])
        balance(u)

    for k in range(8):
        @pl.when(step == k)
        def _():
            eliminate(u, k, tile)

    @pl.when(step == 7)
    def _():
        panel_ref[...] = u[pl.ds(pl.multiple_of(lax.axis_index("tok") * 128, 128), 128), 256:384].T


def gram_and_panel(rows, cols, lead, own):
    width, half = rows.shape[2:]
    return pl.pallas_call(
        gram_kernel,
        grid=(8,),
        out_shape=(
            jax.ShapeDtypeStruct((4, 16 * width, width), F32),
            jax.ShapeDtypeStruct((width, width), F32),
        ),
        in_specs=[
            pl.BlockSpec((2, 2, width, half), lambda s: (0, s, 0, 0)),
            pl.BlockSpec((2, 4, width, half), lambda s: (0, 0, 0, 0)),
            pl.BlockSpec((2, 2, width, half), lambda s: (0, 0, 0, 0)),
            pl.BlockSpec((2, width, half), lambda s: (0, 0, 0)),
        ],
        out_specs=(
            pl.BlockSpec((4, 2 * width, width), lambda s: (0, s, 0)),
            pl.BlockSpec((width, width), lambda s: (0, 0)),
        ),
        scratch_shapes=[pltpu.VMEM((PANEL, 384), F32)],
        compiler_params=pltpu.CompilerParams(vmem_limit_bytes=60 * 2**20),
        cost_estimate=pl.CostEstimate(flops=2 * 2048 * 512 * 1024, bytes_accessed=10 * 2**20, transcendentals=0),
    )(rows, cols, lead, own)


def local(tokens, gate_weight, up_weight):
    gram, panel = gram_and_panel(*gather(tokens, gate_weight, up_weight))
    return (gram.reshape(4, 2048, 1, 128), panel)


def solution(mesh):
    placed = (P("tok", "col"), P(None, ("row", "col")), P(None, ("row", "col")))
    return jax.shard_map(
        local,
        mesh=mesh,
        in_specs=placed,
        out_specs=(P("tok", "row", "col", None), P(("row", "col"), "tok")),
        check_vma=False,
    )
```

```python
import functools

import jax
import jax.numpy as jnp
from jax import lax
from jax.experimental import pallas as pl
from jax.experimental.pallas import tpu as pltpu
from jax.sharding import PartitionSpec as P

PANEL = 256
HIGH = lax.Precision.HIGHEST
MESH = pl.DeviceIdType.MESH
OFFSETS = (0, -1, 1, 2)
NT = (((1,), (1,)), ((), ()))
F32 = jnp.float32

ROWS = 512
QUARTER = 64
FIRST_Y = (256, 96)
FIRST_Z = (352, 160)
PIECES = 4
BATCHES = (2, 2, 2, 2, 2, 2, 1, 1, 1)
RATE, HOP, ISSUE, AHEAD = 49.0, 2.0, 0.12, 0.5


class Move:
    def __init__(self, link, size, needs, source=None, target=None, rows=None, target_rows=None, role=None):
        self.link, self.size, self.needs = link, size, needs
        self.source, self.target, self.rows, self.target_rows, self.role = source, target, rows, target_rows, role


def part(rows, which):
    first = (rows[2] // 2 + 15) // 16 * 16
    return (rows[0], rows[1] + first, rows[2] - first) if which == "b" else (rows[0], rows[1], first)


def token_moves():
    moves, arrivals = {}, {}

    def add(name, link, needs0, needs1, source, target, rows, target_rows=None):
        moves[name] = Move(link, rows[2], (tuple(needs0), tuple(needs1)), source, target, rows, target_rows or rows)

    def along_z(tag, rows, j, have):
        up, far_up, down, far_down = [tag + k for k in ("u1", "u2", "d1", "d2")]
        at = {h: (h, j) for h in OFFSETS}
        add(up, "u", [up], have, (at[-1], at[0]), at[-1], rows)
        add(far_up, "u", [far_up], [up], (at[2], at[-1]), at[2], part(rows, "a"))
        add(down, "d", have, [down], (at[0], at[1]), at[1], rows)
        add(far_down, "d", [down], [far_down], (at[1], at[2]), at[2], part(rows, "b"))
        return {0: list(have), -1: [up], 1: [down], 2: [far_up, far_down]}

    def along_y(tag, rows, h, have):
        right, left, far_right, far_left = [tag + k for k in ("y+1", "y-1", "y+2", "y-2")]
        at = {j: (h, j) for j in OFFSETS}
        add(right, "y+", have, have, (at[0],) * 2, at[-1], rows)
        add(left, "y-", have, have, (at[0],) * 2, at[1], rows)
        add(far_right, "y+", [right], [right], (at[-1],) * 2, at[2], part(rows, "a"))
        add(far_left, "y-", [left], [left], (at[1],) * 2, at[2], part(rows, "b"))
        return {0: list(have), -1: [right], 1: [left], 2: [far_right, far_left]}

    for tag, rows in (("q", (0, 0, QUARTER)), ("f", (None,) + FIRST_Y)):
        near = along_y(tag, rows, 0, [])
        for j in OFFSETS:
            for h, names in along_z(tag + "%d" % j, rows, j, near[j]).items():
                arrivals[tag, h, j] = names
    near = along_z("s", (None,) + FIRST_Z, 0, [])
    for h in OFFSETS:
        for j, names in along_y("s%d" % h, (None,) + FIRST_Z, h, near[h]).items():
            arrivals["s", h, j] = names
    ready = {}
    own, before, after, across = [(d, 0, QUARTER) for d in (0, -1, 1, 2)]
    for spot in [(h, j) for h in OFFSETS for j in OFFSETS][1:]:
        have = arrivals[("q",) + spot]
        right, left, far_right, far_left = ["x%d,%d" % spot + k for k in ("x+1", "x-1", "x+2", "x-2")]
        add(right, "x+", have, have, (spot,) * 2, spot, own, before)
        add(left, "x-", have, have, (spot,) * 2, spot, own, after)
        add(far_right, "x+", [right], [right], (spot,) * 2, spot, part(before, "a"), part(across, "a"))
        add(far_left, "x-", [left], [left], (spot,) * 2, spot, part(after, "b"), part(across, "b"))
        ready[spot] = [n for kind in "qfs" for n in arrivals[(kind,) + spot]] + [right, left, far_right, far_left]
    return moves, ready


def hidden_moves():
    moves, piece, block = {}, 128 // PIECES, 128
    every = range(PIECES)

    def add(name, link, size, needs, role):
        moves[name] = Move(link, size, (tuple(needs),) * 2, role=role)

    for p in every:
        add("zl%d" % p, "zl", piece, [], ("cols", (0, "mine"), (0, "other"), "zl", p))
        for sign, d in (("+", 1), ("-", -1)):
            add("xo%s%d" % (sign, p), "x" + sign, piece, [], ("cols", (0, "mine"), (-d, "mine"), "x" + sign, p))
            add("xp%s%d" % (sign, p), "x" + sign, piece, ["zl%d" % p], ("cols", (0, "other"), (-d, "other"), "x" + sign, p))
        add("xr+%d" % p, "x+", piece, ["xo+%d" % p, "xp+%d" % p], ("cols", (-1, 0), (2, 0), "x+", p))
    add("xr-", "x-", block, ["x%s-%d" % (k, p) for k in "op" for p in every], ("cols", (1, 1), (2, 1), "x-", None))
    gone = {0: ([], []), -1: (["za+"], ["zb+"]), 1: (["za-"], ["zb-"]), 2: (["zr+"], ["zr-"])}
    for relayed, (sign, d) in enumerate((("+", 1), ("-", -1))):
        link = "u" if d == 1 else "d"
        for which, half in enumerate("ab"):
            add("z" + half + sign, link, block, [], ("rows", (0, 0), (-d, 0), "z" + sign, which))
            for h in OFFSETS:
                add("y%d" % h + half + sign, "y" + sign, block // 2, gone[h][which], ("rows", (h, 0), (h, -d), "y" + sign, which))
        add("zr" + sign, link, block, ["z" + "ab"[relayed] + sign], ("rows", (-d, 0), (2, 0), "z" + sign, relayed))
        for h in OFFSETS:
            need = ["y%d" % h + "ab"[relayed] + sign]
            add("y%dr" % h + sign, "y" + sign, block // 2, need, ("rows", (h, -d), (h, 2), "y" + sign, relayed))
    for p in every:
        first = [name % p for name in ("zl%d", "xo+%d", "xo-%d", "xp+%d", "xp-%d", "xr+%d")]
        for hop in (1, 2, 3):
            add("c%d%d" % (hop, p), "c%d" % hop, piece, first if hop == 1 else ["c%d%d" % (hop - 1, p)], ("chain", hop, p))
        add("l%d" % p, "l", piece, ["c3%d" % p], ("spread", p))
        add("m%d" % p, "m", piece, ["l%d" % p], ("relay", p))
    row_groups = {h: gone[h][0] + gone[h][1] + ["y%d" % h + k + sign for k in "abr" for sign in "+-"] for h in OFFSETS}
    pairs = {0: ["zl%d" % p for p in every], 2: ["xr-"] + ["xr+%d" % p for p in every]}
    for sign, d in (("+", -1), ("-", 1)):
        pairs[d] = ["x%s%s%d" % (k, sign, p) for k in "op" for p in every]
    return moves, row_groups, pairs


def schedule(moves):
    followers = {name: set() for name in moves}
    for name, move in moves.items():
        for parity in (0, 1):
            for need in move.needs[parity]:
                followers[need].add((name, parity))

    def there(name, parity):
        return 1 - parity if moves[name].role is None and moves[name].link in "ud" else parity

    @functools.lru_cache(None)
    def rest(name, parity):
        after = [moves[m].size / RATE + HOP + rest(m, there(m, q)) for m, q in followers[name] if q == parity]
        return max(after, default=0.0)

    landed, begun, free = ({}, {}), ({}, {}), {}
    waiting = {(name, parity) for name in moves for parity in (0, 1)}
    while waiting:
        best = None
        for name, parity in waiting:
            move, have = moves[name], landed[parity]
            when = max(free.get((move.link, parity), 0.0), free.get(parity, 0.0))
            for need in move.needs[parity]:
                if need not in have:
                    break
                when = max(when, have[need])
            else:
                key = (when, -(rest(name, there(name, parity)) + move.size / RATE), name, parity)
                if best is None or key < best:
                    best = key
        when, _, name, parity = best
        done = when + moves[name].size / RATE
        free[moves[name].link, parity] = done
        free[parity] = when + ISSUE
        begun[parity][name] = when
        landed[there(name, parity)][name] = done + HOP
        waiting.discard((name, parity))
    return begun, landed


def balance(u):
    rows = lax.broadcasted_iota(jnp.int32, (PANEL, PANEL), 0)
    lanes = lax.broadcasted_iota(jnp.int32, (PANEL, PANEL), 1)
    corner = u[:, 0:PANEL]
    only = jnp.where(rows == lanes, corner, 0.0)
    down, across = lax.rsqrt(jnp.sum(only, axis=1, keepdims=True)), lax.rsqrt(jnp.sum(only, axis=0, keepdims=True))
    u[:, 0:PANEL] = corner * down * across
    u[:, PANEL:] = u[:, PANEL:] * down


def eliminate(u, piece):
    wide = lax.broadcasted_iota(jnp.int32, (8, 384), 0)
    base = 64 * (piece // 2)
    groups = [u[base + 8 * g:base + 8 * g + 8, :] for g in range(8)]

    def spread(row, at):
        return jnp.broadcast_to(row[at:at + 1, :], (8, row.shape[1]))

    def thrice(tile):
        return jnp.concatenate([tile] * 3, axis=1)

    for p in range(4 * (piece % 2), 4 * (piece % 2) + 4):
        cols = {
            (g, k): jnp.broadcast_to(groups[g][:, base + 8 * p + k:base + 8 * p + k + 1], (8, 128))
            for g in range(p, 8) for k in range(8)
        }
        for k in range(0, 8, 2):
            a, b, c = spread(cols[p, k], k), spread(cols[p, k + 1], k), spread(cols[p, k + 1], k + 1)
            root = lax.rsqrt(a * c - b * b)
            over = root * root
            left, right = [], []
            for g in range(p, 8):
                left.append((c * cols[g, k] - b * cols[g, k + 1]) * over)
                right.append((a * cols[g, k + 1] - b * cols[g, k]) * over)
            for j in range(k + 2, 8):
                one, two = spread(cols[p, k], j), spread(cols[p, k + 1], j)
                for g in range(p, 8):
                    cols[g, j] = cols[g, j] - (left[g - p] * one + right[g - p] * two)
            first = lax.rsqrt(a)
            ratio = b * first * first
            second = lax.rsqrt(c - b * ratio)
            line, below = spread(groups[p], k), spread(groups[p], k + 1)
            top = line * thrice(first)
            low = (below - thrice(ratio) * line) * thrice(second)
            rest = groups[p] - (thrice(left[0]) * line + thrice(right[0]) * below)
            groups[p] = jnp.where(wide == k, top, jnp.where(wide == k + 1, low, jnp.where(wide > k + 1, rest, groups[p])))
            for g in range(p, 8):
                cols[g, k + 1] = (cols[g, k + 1] - ratio * cols[g, k]) * second
                cols[g, k] = cols[g, k] * first
        lines = [spread(groups[p], k) for k in range(8)]
        for g in range(p + 1, 8):
            acc = groups[g]
            for k in range(8):
                acc = acc - thrice(cols[g, k]) * lines[k]
            groups[g] = acc
    for g in range(4 * (piece % 2), 8):
        u[base + 8 * g:base + 8 * g + 8, :] = groups[g]
    if piece % 2 and piece < 7:
        block = u[base:base + 64, :]
        first = 0 if base == 0 else 128
        update = jnp.dot(block[:, first:256].T, block, precision=HIGH, preferred_element_type=F32)
        rest = base + 64
        u[rest:256, :] = u[rest:256, :] - update[rest - first:256 - first, :]


def gather_kernel(
    tokens_hbm, gate_hbm, up_hbm, rows_out, cols_out, lead_out, own_out,
    held, weights, total, rows, cols, leads,
    load_sem, send_sem, recv_sem, send2, recv2, side_send, side_recv, lead_send, lead_recv, local_sem,
):
    tok, row, col = lax.axis_index("tok"), lax.axis_index("row"), lax.axis_index("col")
    x, z_lo, z_hi, y = lax.div(row, 2), lax.rem(row, 2), lax.div(col, 4), lax.rem(col, 4)

    def around(at):
        return {0: at, 1: lax.rem(at + 1, 4), 2: lax.rem(at + 2, 4), -1: lax.rem(at + 3, 4)}

    xs, zs, ys = around(x), around(z_hi), around(y)
    places = {(h, j): zs[h] * 4 + ys[j] for h in OFFSETS for j in OFFSETS}
    quarters = {d: xs[d] * QUARTER for d in OFFSETS}
    groups = {(d, z): xs[d] * 2 + z for d in OFFSETS for z in (0, 1)}
    firsts = {h: zs[h] * 4 for h in OFFSETS}
    spots = {d: lax.rem(xs[d], 2) * 2 for d in OFFSETS}
    keeps = {d: lax.div(xs[d], 2) == tok for d in OFFSETS}
    partner_row = x * 2 + 1 - z_lo

    devices = {"zl": (tok, partner_row, col)}
    for sign, d in (("+", 1), ("-", -1)):
        devices["x" + sign] = (tok, xs[d] * 2 + z_lo, col)
        devices["y" + sign] = (tok, row, places[0, d])
        devices["z" + sign] = (tok, row, places[d, 0])
    sibling = (1 - tok, row, col)
    step = {
        ("u", 0): devices["zl"], ("u", 1): (tok, partner_row, places[1, 0]),
        ("d", 0): (tok, partner_row, places[-1, 0]), ("d", 1): devices["zl"],
    }
    low = y < 2
    at_z = {k: jnp.logical_and(low, z_hi == k) for k in range(4)}
    past_first = jnp.logical_and(low, z_hi > 0)
    at_y = {k: y == k for k in range(4)}

    first = pltpu.make_async_copy(tokens_hbm, held.at[col], load_sem.at[2])
    first.start()
    loads = [
        pltpu.make_async_copy(gate_hbm, weights.at[:, 0:128], load_sem.at[0]),
        pltpu.make_async_copy(up_hbm, weights.at[:, 128:256], load_sem.at[1]),
    ]
    for load in loads:
        load.start()

    barrier = pltpu.get_barrier_semaphore()
    far = (tok, partner_row, places[1, 0] * z_lo + places[-1, 0] * (1 - z_lo))
    near = [devices[k] for k in ("x+", "x-", "y+", "y-", "z+", "z-", "zl")] + [far, sibling]
    for device in near:
        pl.semaphore_signal(barrier, inc=1, device_id=device, device_id_type=MESH)
    pl.semaphore_wait(barrier, len(near))
    first.wait()

    tokens, ready = token_moves()
    hiddens, row_groups, pairs = hidden_moves()
    number = {name: at for at, name in enumerate(tokens)}
    number.update({name: at for at, name in enumerate(n for n in hiddens if hiddens[n].role[0] in ("rows", "cols"))})

    def span(at_rows):
        if at_rows[0] is None:
            return pl.ds(at_rows[1], at_rows[2])
        return pl.ds(pl.multiple_of(quarters[at_rows[0]] + at_rows[1], 16), at_rows[2])

    def remote(semaphores, index, source, target, device):
        return pltpu.make_async_remote_copy(
            src_ref=source, dst_ref=target, send_sem=semaphores[0].at[0], recv_sem=semaphores[1].at[index],
            device_id=device, device_id_type=MESH,
        )

    def held_ref(spot, at_rows):
        return held.at[places[spot], span(at_rows), :]

    def block_ref(move, at, parity):
        kind, which = move.role[0], move.role[4]
        if kind == "rows":
            return rows.at[places[at]] if which is None else rows.at[places[at], pl.ds(64 * which, 64), :]
        z = {"mine": parity, "other": 1 - parity}.get(at[1], at[1])
        if which is None:
            return cols.at[groups[at[0], z]]
        size = 128 // PIECES
        return cols.at[groups[at[0], z], pl.ds(size * which, size), :]

    def outgoing(move, name, parity):
        if move.role is not None:
            place = block_ref(move, move.role[1], parity)
            return remote((send2, recv2), number[name], place, place, devices[move.role[3]])
        place = held_ref(move.source[parity], move.rows)
        device = step[move.link, parity] if move.link in "ud" else devices[move.link]
        return remote((send_sem, recv_sem), number[name], place, place, device)

    def incoming(move, name, parity):
        if move.role is not None:
            place = block_ref(move, move.role[2], parity)
            return remote((send2, recv2), number[name], place, place, sibling)
        place = held_ref(move.target, move.target_rows)
        return remote((send_sem, recv_sem), number[name], place, place, sibling)

    def lead(b, p):
        size = 128 // PIECES
        return leads.at[b, pl.ds(size * p, size), :]

    def lead_copy(kind, b, p, device, from_cols=False):
        size = 128 // PIECES
        return pltpu.make_async_remote_copy(
            src_ref=cols.at[0, pl.ds(size * p, size), :] if from_cols else lead(b, p), dst_ref=lead(b, p),
            send_sem=lead_send.at[kind * PIECES + p],
            recv_sem=lead_recv.at[b * PIECES + p],
            device_id=device, device_id_type=MESH,
        )

    def lead_arrive(b, p):
        lead_copy(0, b, p, sibling).wait_recv()

    def chain_role(hop, parity):
        if hop == 1:
            return at_z[0], step["u" if parity == 1 else "d", parity]
        upward = (hop == 2) == (parity == 0)
        return at_z[1 if upward else 3], step["u" if upward else "d", parity]

    relays = ((3, 0, "y-"), (2, 1, "y+"))

    def lead_start(role, parity):
        if role[0] == "chain":
            hop, p = role[1:]
            here, device = chain_role(hop, parity)

            @pl.when(here)
            def _():
                if hop > 1:
                    lead_arrive(y, p)
                lead_copy(0, y, p, device, hop == 1).start()
        elif role[0] == "spread":
            p = role[1]

            @pl.when(at_z[0])
            def _():
                lead_copy(1, y, p, devices["y+"], True).start()
                lead_copy(2, y, p, devices["y-"], True).start()

            @pl.when(at_z[2])
            def _():
                lead_arrive(y, p)

            @pl.when(past_first)
            def _():
                lead_copy(1, y, p, devices["y+"]).start()
                lead_copy(2, y, p, devices["y-"]).start()
        else:
            p = role[1]
            for k, b, way in relays:
                @pl.when(at_y[k])
                def _():
                    lead_arrive(b, p)
                    lead_copy(3, b, p, devices[way]).start()

    def lead_end(parity):
        for p in range(PIECES):
            for hop in (1, 2, 3):
                here, device = chain_role(hop, parity)

                @pl.when(here)
                def _():
                    lead_copy(0, y, p, device).wait_send()

            @pl.when(low)
            def _():
                lead_copy(1, y, p, devices["y+"]).wait_send()
                lead_copy(2, y, p, devices["y-"]).wait_send()

            for k, b, way in relays:
                @pl.when(at_y[k])
                def _():
                    lead_copy(3, b, p, devices[way]).wait_send()

    def side(index, source, target):
        return pltpu.make_async_remote_copy(
            src_ref=source, dst_ref=target, send_sem=side_send.at[index], recv_sem=side_recv.at[index],
            device_id=sibling, device_id_type=MESH,
        )

    def keep(index, source, target):
        return pltpu.make_async_copy(source, target, local_sem.at[index])

    shared = {}
    for k, h in enumerate(OFFSETS):
        shared["r", h] = (row_groups[h], k)
        shared["c", h] = (pairs[h], 4 + k)

    def side_refs(kind, d):
        if kind == "r":
            at = pl.ds(firsts[d], 4)
            return rows.at[at], (lambda t: rows_out.at[t, at])
        if kind == "c":
            return cols.at[pl.ds(groups[d, 0], 2)], (lambda t: cols_out.at[t, pl.ds(spots[d], 2)])
        if kind == "l":
            return leads, (lambda t: lead_out.at[t])
        return rows.at[col], (lambda t: own_out.at[t])

    def side_start(kind, d, index):
        source, target = side_refs(kind, d)
        if kind != "c":
            side(index, source, target(tok)).start()
            if kind != "r":
                keep(index, source, target(tok)).start()
            return

        @pl.when(keeps[d])
        def _():
            keep(index, source, target(tok)).start()

        @pl.when(jnp.logical_not(keeps[d]))
        def _():
            side(index, source, target(tok)).start()

    def side_end(kind, d, index):
        source, target = side_refs(kind, d)
        if kind != "c":
            side(index, target(1 - tok), target(1 - tok)).wait_recv()
            side(index, source, target(tok)).wait_send()
            if kind != "r":
                keep(index, source, target(tok)).wait()
            return

        @pl.when(keeps[d])
        def _():
            keep(index, source, target(tok)).wait()
            side(index, target(1 - tok), target(1 - tok)).wait_recv()

        @pl.when(jnp.logical_not(keeps[d]))
        def _():
            side(index, source, target(tok)).wait_send()

    def both(act):
        for parity in (0, 1):
            pl.when(z_lo == parity)(functools.partial(act, parity))

    def in_order(begun):
        return [sorted((begun[parity][name], name) for name in begun[parity]) for parity in (0, 1)]

    begun, landed = schedule(tokens)
    order = in_order(begun)
    seen, at = (set(), set()), [0, 0]

    def arrive(moves, name, parity):
        if name not in seen[parity]:
            seen[parity].add(name)
            if name in number:
                incoming(moves[name], name, parity).wait_recv()

    def stretch(until, batch, parity):
        while at[parity] < len(order[parity]) and order[parity][at[parity]][0] <= until:
            name = order[parity][at[parity]][1]
            at[parity] += 1
            for need in tokens[name].needs[parity]:
                arrive(tokens, need, parity)
            outgoing(tokens[name], name, parity).start()
        for chunk in batch:
            for need in ready[chunk]:
                arrive(tokens, need, parity)

    finished = {c: max(landed[p][name] for p in (0, 1) for name in ready[c]) for c in ready}
    queue = sorted(ready, key=lambda c: (finished[c], c))
    start = 0
    for k, size in enumerate(BATCHES):
        batch = queue[start:start + size]
        start += size
        until = max(finished[c] for c in batch) + AHEAD if start < len(queue) else 1e9
        both(functools.partial(stretch, until, batch))
        if k == 0:
            for load in loads:
                load.wait()
            total[...] = jnp.zeros_like(total)
        for here in ([col] if k == 0 else []) + [places[chunk] for chunk in batch]:
            total[...] += jnp.dot(held[here], weights[pl.ds(pl.multiple_of(here * 512, 512), 512), :], preferred_element_type=F32)

    def tokens_end(parity):
        for name in tokens:
            arrive(tokens, name, parity)

    both(tokens_end)
    gate = total[:, 0:128]
    hidden = gate / (1.0 + jnp.exp(-gate)) * total[:, 128:256]
    hidden = hidden.T.astype(jnp.bfloat16)
    rows[col] = hidden
    cols[row] = hidden

    begun, landed = schedule(hiddens)
    order = in_order(begun)
    left = (dict(shared), dict(shared))

    def hidden_stage(parity):
        waited = False
        for _, name in order[parity]:
            move = hiddens[name]
            if move.needs[parity] and not waited:
                waited = True
                side_start("o", 0, 8)
            for need in move.needs[parity]:
                arrive(hiddens, need, parity)
            if move.role[0] in ("rows", "cols"):
                outgoing(move, name, parity).start()
            else:
                lead_start(move.role, parity)
            for key in list(left[parity]):
                names, index = left[parity][key]
                if seen[parity].issuperset(names):
                    del left[parity][key]
                    side_start(*key, index)
        for key in list(left[parity]):
            names, index = left[parity].pop(key)
            for name in names:
                arrive(hiddens, name, parity)
            side_start(*key, index)
        for name in hiddens:
            arrive(hiddens, name, parity)

    both(hidden_stage)
    keep_rows = keep(0, rows, rows_out.at[tok])
    keep_rows.start()
    held_lead = pltpu.make_async_copy(cols.at[0], leads.at[lax.rem(y, 2)], local_sem.at[10])

    @pl.when(at_z[0])
    def _():
        held_lead.start()

    for p in range(PIECES):
        for k, b in ((0, 1), (1, 0), (2, 0), (3, 1)):
            @pl.when(at_y[k])
            def _():
                lead_arrive(b, p)

    @pl.when(at_z[0])
    def _():
        held_lead.wait()

    side_start("l", 0, 9)

    remote((send_sem, recv_sem), 0, held.at[pl.ds(0, 15)], held.at[pl.ds(0, 15)], sibling).wait_send()
    gone = weights.at[pl.ds(0, 5632), :]
    remote((send2, recv2), 0, gone, gone, sibling).wait_send()
    both(lead_end)
    keep_rows.wait()
    for kind, d in shared:
        side_end(kind, d, shared[kind, d][1])
    side_end("o", 0, 8)
    side_end("l", 0, 9)


def gather(tokens, gate_weight, up_weight):
    depth, width = gate_weight.shape
    half = tokens.shape[0]
    bf16 = jnp.bfloat16
    hbm = pl.BlockSpec(memory_space=pl.ANY)
    return pl.pallas_call(
        gather_kernel,
        out_shape=(
            jax.ShapeDtypeStruct((2, 16, width, half), bf16),
            jax.ShapeDtypeStruct((2, 4, width, half), bf16),
            jax.ShapeDtypeStruct((2, 2, width, half), bf16),
            jax.ShapeDtypeStruct((2, width, half), bf16),
        ),
        in_specs=[hbm, hbm, hbm],
        out_specs=(hbm,) * 4,
        scratch_shapes=[
            pltpu.VMEM((16, half, 512), bf16),
            pltpu.VMEM((depth, 2 * width), bf16),
            pltpu.VMEM((half, 2 * width), F32),
            pltpu.VMEM((16, width, half), bf16),
            pltpu.VMEM((8, width, half), bf16),
            pltpu.VMEM((2, width, half), bf16),
            pltpu.SemaphoreType.DMA((3,)),
            pltpu.SemaphoreType.DMA((1,)),
            pltpu.SemaphoreType.DMA((120,)),
            pltpu.SemaphoreType.DMA((1,)),
            pltpu.SemaphoreType.DMA((55,)),
            pltpu.SemaphoreType.DMA((10,)),
            pltpu.SemaphoreType.DMA((10,)),
            pltpu.SemaphoreType.DMA((4 * PIECES,)),
            pltpu.SemaphoreType.DMA((2 * PIECES,)),
            pltpu.SemaphoreType.DMA((11,)),
        ],
        compiler_params=pltpu.CompilerParams(
            collective_id=0, has_side_effects=True, vmem_limit_bytes=60 * 2**20
        ),
        cost_estimate=pl.CostEstimate(flops=2 * half * depth * 2 * width, bytes_accessed=12 * 2**20, transcendentals=half * width),
    )(tokens, gate_weight, up_weight)


def gram_kernel(rows_ref, cols_ref, lead_ref, own_ref, gram_ref, panel_ref, u):
    step = pl.program_id(0)

    def product(left, right):
        return sum(lax.dot_general(left(t), right(t), NT, preferred_element_type=F32) for t in (0, 1))

    def tile():
        whole = product(lambda t: rows_ref[t].reshape(256, 512), lambda t: cols_ref[t].reshape(512, 512))
        for a in range(4):
            gram_ref[a] = whole[:, 128 * a:128 * a + 128]

    @pl.when(step == 0)
    def _():
        def lead(t):
            return lead_ref[t].reshape(256, 512)

        u[:, 0:256] = product(lead, lead)
        u[:, 256:384] = product(lead, lambda t: own_ref[t])
        balance(u)

    for k in range(8):
        @pl.when(step == k)
        def _():
            tile()
            eliminate(u, k)

    @pl.when(step == 7)
    def _():
        panel_ref[...] = u[pl.ds(pl.multiple_of(lax.axis_index("tok") * 128, 128), 128), 256:384].T


def gram_and_panel(rows, cols, lead, own):
    width, half = rows.shape[2:]
    return pl.pallas_call(
        gram_kernel,
        grid=(8,),
        out_shape=(
            jax.ShapeDtypeStruct((4, 16 * width, width), F32),
            jax.ShapeDtypeStruct((width, width), F32),
        ),
        in_specs=[
            pl.BlockSpec((2, 2, width, half), lambda s: (0, s, 0, 0)),
            pl.BlockSpec((2, 4, width, half), lambda s: (0, 0, 0, 0)),
            pl.BlockSpec((2, 2, width, half), lambda s: (0, 0, 0, 0)),
            pl.BlockSpec((2, width, half), lambda s: (0, 0, 0)),
        ],
        out_specs=(
            pl.BlockSpec((4, 2 * width, width), lambda s: (0, s, 0)),
            pl.BlockSpec((width, width), lambda s: (0, 0)),
        ),
        scratch_shapes=[pltpu.VMEM((PANEL, 384), F32)],
        compiler_params=pltpu.CompilerParams(vmem_limit_bytes=60 * 2**20),
        cost_estimate=pl.CostEstimate(flops=2 * 2048 * 512 * 1024, bytes_accessed=10 * 2**20, transcendentals=0),
    )(rows, cols, lead, own)


def local(tokens, gate_weight, up_weight):
    gram, panel = gram_and_panel(*gather(tokens, gate_weight, up_weight))
    return (gram.reshape(4, 2048, 1, 128), panel)


def solution(mesh):
    placed = (P("tok", "col"), P(None, ("row", "col")), P(None, ("row", "col")))
    return jax.shard_map(
        local,
        mesh=mesh,
        in_specs=placed,
        out_specs=(P("tok", "row", "col", None), P(("row", "col"), "tok")),
        check_vma=False,
    )
```

```python
import functools

import jax
import jax.numpy as jnp
from jax import lax
from jax.experimental import pallas as pl
from jax.experimental.pallas import tpu as pltpu
from jax.sharding import PartitionSpec as P

PANEL = 256
HIGH = lax.Precision.HIGHEST
MESH = pl.DeviceIdType.MESH
OFFSETS = (0, -1, 1, 2)
NT = (((1,), (1,)), ((), ()))
F32 = jnp.float32

ROWS = 512
QUARTER = 64
FIRST_Y = (256, 96)
FIRST_Z = (352, 160)
PIECES = 4
BATCHES = (2, 2, 2, 2, 2, 2, 1, 1, 1)
RATE, HOP, ISSUE, AHEAD = 49.0, 2.3, 0.14, 1.5


class Move:
    def __init__(self, link, size, needs, source=None, target=None, rows=None, target_rows=None, role=None):
        self.link, self.size, self.needs = link, size, needs
        self.source, self.target, self.rows, self.target_rows, self.role = source, target, rows, target_rows, role


def part(rows, which):
    first = (rows[2] // 2 + 15) // 16 * 16
    return (rows[0], rows[1] + first, rows[2] - first) if which == "b" else (rows[0], rows[1], first)


def token_moves():
    moves, arrivals = {}, {}

    def add(name, link, needs0, needs1, source, target, rows, target_rows=None):
        moves[name] = Move(link, rows[2], (tuple(needs0), tuple(needs1)), source, target, rows, target_rows or rows)

    def along_z(tag, rows, j, have):
        up, far_up, down, far_down = [tag + k for k in ("u1", "u2", "d1", "d2")]
        at = {h: (h, j) for h in OFFSETS}
        add(up, "u", [up], have, (at[-1], at[0]), at[-1], rows)
        add(far_up, "u", [far_up], [up], (at[2], at[-1]), at[2], part(rows, "a"))
        add(down, "d", have, [down], (at[0], at[1]), at[1], rows)
        add(far_down, "d", [down], [far_down], (at[1], at[2]), at[2], part(rows, "b"))
        return {0: list(have), -1: [up], 1: [down], 2: [far_up, far_down]}

    def along_y(tag, rows, h, have):
        right, left, far_right, far_left = [tag + k for k in ("y+1", "y-1", "y+2", "y-2")]
        at = {j: (h, j) for j in OFFSETS}
        add(right, "y+", have, have, (at[0],) * 2, at[-1], rows)
        add(left, "y-", have, have, (at[0],) * 2, at[1], rows)
        add(far_right, "y+", [right], [right], (at[-1],) * 2, at[2], part(rows, "a"))
        add(far_left, "y-", [left], [left], (at[1],) * 2, at[2], part(rows, "b"))
        return {0: list(have), -1: [right], 1: [left], 2: [far_right, far_left]}

    for tag, rows in (("q", (0, 0, QUARTER)), ("f", (None,) + FIRST_Y)):
        near = along_y(tag, rows, 0, [])
        for j in OFFSETS:
            for h, names in along_z(tag + "%d" % j, rows, j, near[j]).items():
                arrivals[tag, h, j] = names
    near = along_z("s", (None,) + FIRST_Z, 0, [])
    for h in OFFSETS:
        for j, names in along_y("s%d" % h, (None,) + FIRST_Z, h, near[h]).items():
            arrivals["s", h, j] = names
    ready = {}
    own, before, after, across = [(d, 0, QUARTER) for d in (0, -1, 1, 2)]
    for spot in [(h, j) for h in OFFSETS for j in OFFSETS][1:]:
        have = arrivals[("q",) + spot]
        right, left, far_right, far_left = ["x%d,%d" % spot + k for k in ("x+1", "x-1", "x+2", "x-2")]
        add(right, "x+", have, have, (spot,) * 2, spot, own, before)
        add(left, "x-", have, have, (spot,) * 2, spot, own, after)
        add(far_right, "x+", [right], [right], (spot,) * 2, spot, part(before, "a"), part(across, "a"))
        add(far_left, "x-", [left], [left], (spot,) * 2, spot, part(after, "b"), part(across, "b"))
        ready[spot] = [n for kind in "qfs" for n in arrivals[(kind,) + spot]] + [right, left, far_right, far_left]
    return moves, ready


def hidden_moves():
    moves, piece, block = {}, 128 // PIECES, 128
    every = range(PIECES)

    def add(name, link, size, needs, role):
        moves[name] = Move(link, size, (tuple(needs),) * 2, role=role)

    for p in every:
        add("zl%d" % p, "zl", piece, [], ("cols", (0, "mine"), (0, "other"), "zl", p))
        for sign, d in (("+", 1), ("-", -1)):
            add("xo%s%d" % (sign, p), "x" + sign, piece, [], ("cols", (0, "mine"), (-d, "mine"), "x" + sign, p))
            add("xp%s%d" % (sign, p), "x" + sign, piece, ["zl%d" % p], ("cols", (0, "other"), (-d, "other"), "x" + sign, p))
        add("xr+%d" % p, "x+", piece, ["xo+%d" % p, "xp+%d" % p], ("cols", (-1, 0), (2, 0), "x+", p))
    add("xr-", "x-", block, ["x%s-%d" % (k, p) for k in "op" for p in every], ("cols", (1, 1), (2, 1), "x-", None))
    gone = {0: ([], []), -1: (["za+"], ["zb+"]), 1: (["za-"], ["zb-"]), 2: (["zr+"], ["zr-"])}
    for relayed, (sign, d) in enumerate((("+", 1), ("-", -1))):
        link = "u" if d == 1 else "d"
        for which, half in enumerate("ab"):
            add("z" + half + sign, link, block, [], ("rows", (0, 0), (-d, 0), "z" + sign, which))
            for h in OFFSETS:
                add("y%d" % h + half + sign, "y" + sign, block // 2, gone[h][which], ("rows", (h, 0), (h, -d), "y" + sign, which))
        add("zr" + sign, link, block, ["z" + "ab"[relayed] + sign], ("rows", (-d, 0), (2, 0), "z" + sign, relayed))
        for h in OFFSETS:
            need = ["y%d" % h + "ab"[relayed] + sign]
            add("y%dr" % h + sign, "y" + sign, block // 2, need, ("rows", (h, -d), (h, 2), "y" + sign, relayed))
    for p in every:
        first = [name % p for name in ("zl%d", "xo+%d", "xo-%d", "xp+%d", "xp-%d", "xr+%d")]
        for hop in (1, 2, 3):
            add("c%d%d" % (hop, p), "c%d" % hop, piece, first if hop == 1 else ["c%d%d" % (hop - 1, p)], ("chain", hop, p))
        add("l%d" % p, "l", piece, ["c3%d" % p], ("spread", p))
        add("m%d" % p, "m", piece, ["l%d" % p], ("relay", p))
    row_groups = {h: gone[h][0] + gone[h][1] + ["y%d" % h + k + sign for k in "abr" for sign in "+-"] for h in OFFSETS}
    pairs = {0: ["zl%d" % p for p in every], 2: ["xr-"] + ["xr+%d" % p for p in every]}
    for sign, d in (("+", -1), ("-", 1)):
        pairs[d] = ["x%s%s%d" % (k, sign, p) for k in "op" for p in every]
    return moves, row_groups, pairs


def schedule(moves):
    followers = {name: set() for name in moves}
    for name, move in moves.items():
        for parity in (0, 1):
            for need in move.needs[parity]:
                followers[need].add((name, parity))

    def there(name, parity):
        return 1 - parity if moves[name].role is None and moves[name].link in "ud" else parity

    @functools.lru_cache(None)
    def rest(name, parity):
        after = [moves[m].size / RATE + HOP + rest(m, there(m, q)) for m, q in followers[name] if q == parity]
        return max(after, default=0.0)

    landed, begun, free = ({}, {}), ({}, {}), {}
    waiting = {(name, parity) for name in moves for parity in (0, 1)}
    while waiting:
        best = None
        for name, parity in waiting:
            move, have = moves[name], landed[parity]
            when = max(free.get((move.link, parity), 0.0), free.get(parity, 0.0))
            for need in move.needs[parity]:
                if need not in have:
                    break
                when = max(when, have[need])
            else:
                key = (when, -(rest(name, there(name, parity)) + move.size / RATE), name, parity)
                if best is None or key < best:
                    best = key
        when, _, name, parity = best
        done = when + moves[name].size / RATE
        free[moves[name].link, parity] = done
        free[parity] = when + ISSUE
        begun[parity][name] = when
        landed[there(name, parity)][name] = done + HOP
        waiting.discard((name, parity))
    return begun, landed


def balance(u):
    rows = lax.broadcasted_iota(jnp.int32, (PANEL, PANEL), 0)
    lanes = lax.broadcasted_iota(jnp.int32, (PANEL, PANEL), 1)
    corner = u[:, 0:PANEL]
    only = jnp.where(rows == lanes, corner, 0.0)
    down, across = lax.rsqrt(jnp.sum(only, axis=1, keepdims=True)), lax.rsqrt(jnp.sum(only, axis=0, keepdims=True))
    u[:, 0:PANEL] = corner * down * across
    u[:, PANEL:] = u[:, PANEL:] * down


def eliminate(u, piece):
    wide = lax.broadcasted_iota(jnp.int32, (8, 384), 0)
    base = 32 * piece
    groups = [u[base + 8 * g:base + 8 * g + 8, :] for g in range(4)]

    def spread(row, at):
        return jnp.broadcast_to(row[at:at + 1, :], (8, row.shape[1]))

    def thrice(tile):
        return jnp.concatenate([tile] * 3, axis=1)

    for p in range(4):
        cols = {
            (g, k): jnp.broadcast_to(groups[g][:, base + 8 * p + k:base + 8 * p + k + 1], (8, 128))
            for g in range(p, 4) for k in range(8)
        }
        for k in range(0, 8, 2):
            a, b, c = spread(cols[p, k], k), spread(cols[p, k + 1], k), spread(cols[p, k + 1], k + 1)
            root = lax.rsqrt(a * c - b * b)
            over = root * root
            left, right = [], []
            for g in range(p, 4):
                left.append((c * cols[g, k] - b * cols[g, k + 1]) * over)
                right.append((a * cols[g, k + 1] - b * cols[g, k]) * over)
            for j in range(k + 2, 8):
                one, two = spread(cols[p, k], j), spread(cols[p, k + 1], j)
                for g in range(p, 4):
                    cols[g, j] = cols[g, j] - (left[g - p] * one + right[g - p] * two)
            first = lax.rsqrt(a)
            ratio = b * first * first
            second = lax.rsqrt(c - b * ratio)
            line, below = spread(groups[p], k), spread(groups[p], k + 1)
            top = line * thrice(first)
            low = (below - thrice(ratio) * line) * thrice(second)
            rest = groups[p] - (thrice(left[0]) * line + thrice(right[0]) * below)
            groups[p] = jnp.where(wide == k, top, jnp.where(wide == k + 1, low, jnp.where(wide > k + 1, rest, groups[p])))
            for g in range(p, 4):
                cols[g, k + 1] = (cols[g, k + 1] - ratio * cols[g, k]) * second
                cols[g, k] = cols[g, k] * first
        lines = [spread(groups[p], k) for k in range(8)]
        for g in range(p + 1, 4):
            acc = groups[g]
            for k in range(8):
                acc = acc - thrice(cols[g, k]) * lines[k]
            groups[g] = acc
    for g in range(4):
        u[base + 8 * g:base + 8 * g + 8, :] = groups[g]
    if piece < 7:
        block = u[base:base + 32, :]
        first = 0 if piece < 3 else 128
        update = jnp.dot(block[:, first:256].T, block, precision=HIGH, preferred_element_type=F32)
        rest = base + 32
        u[rest:256, :] = u[rest:256, :] - update[rest - first:256 - first, :]


def gather_kernel(
    tokens_hbm, gate_hbm, up_hbm, rows_out, cols_out, lead_out, own_out,
    held, weights, total, rows, cols, leads,
    load_sem, send_sem, recv_sem, send2, recv2, side_send, side_recv, lead_send, lead_recv, local_sem,
):
    tok, row, col = lax.axis_index("tok"), lax.axis_index("row"), lax.axis_index("col")
    x, z_lo, z_hi, y = lax.div(row, 2), lax.rem(row, 2), lax.div(col, 4), lax.rem(col, 4)

    def around(at):
        return {0: at, 1: lax.rem(at + 1, 4), 2: lax.rem(at + 2, 4), -1: lax.rem(at + 3, 4)}

    xs, zs, ys = around(x), around(z_hi), around(y)
    places = {(h, j): zs[h] * 4 + ys[j] for h in OFFSETS for j in OFFSETS}
    quarters = {d: xs[d] * QUARTER for d in OFFSETS}
    groups = {(d, z): xs[d] * 2 + z for d in OFFSETS for z in (0, 1)}
    firsts = {h: zs[h] * 4 for h in OFFSETS}
    spots = {d: lax.rem(xs[d], 2) * 2 for d in OFFSETS}
    keeps = {d: lax.div(xs[d], 2) == tok for d in OFFSETS}
    partner_row = x * 2 + 1 - z_lo

    devices = {"zl": (tok, partner_row, col)}
    for sign, d in (("+", 1), ("-", -1)):
        devices["x" + sign] = (tok, xs[d] * 2 + z_lo, col)
        devices["y" + sign] = (tok, row, places[0, d])
        devices["z" + sign] = (tok, row, places[d, 0])
    sibling = (1 - tok, row, col)
    step = {
        ("u", 0): devices["zl"], ("u", 1): (tok, partner_row, places[1, 0]),
        ("d", 0): (tok, partner_row, places[-1, 0]), ("d", 1): devices["zl"],
    }
    low = y < 2
    at_z = {k: jnp.logical_and(low, z_hi == k) for k in range(4)}
    past_first = jnp.logical_and(low, z_hi > 0)
    at_y = {k: y == k for k in range(4)}

    first = pltpu.make_async_copy(tokens_hbm, held.at[col], load_sem.at[2])
    first.start()
    loads = [
        pltpu.make_async_copy(gate_hbm, weights.at[:, 0:128], load_sem.at[0]),
        pltpu.make_async_copy(up_hbm, weights.at[:, 128:256], load_sem.at[1]),
    ]
    for load in loads:
        load.start()

    barrier = pltpu.get_barrier_semaphore()
    far = (tok, partner_row, places[1, 0] * z_lo + places[-1, 0] * (1 - z_lo))
    near = [devices[k] for k in ("x+", "x-", "y+", "y-", "z+", "z-", "zl")] + [far, sibling]
    for device in near:
        pl.semaphore_signal(barrier, inc=1, device_id=device, device_id_type=MESH)
    pl.semaphore_wait(barrier, len(near))
    first.wait()

    tokens, ready = token_moves()
    hiddens, row_groups, pairs = hidden_moves()
    number = {name: at for at, name in enumerate(tokens)}
    number.update({name: at for at, name in enumerate(n for n in hiddens if hiddens[n].role[0] in ("rows", "cols"))})

    def span(at_rows):
        if at_rows[0] is None:
            return pl.ds(at_rows[1], at_rows[2])
        return pl.ds(pl.multiple_of(quarters[at_rows[0]] + at_rows[1], 16), at_rows[2])

    def remote(semaphores, index, source, target, device):
        return pltpu.make_async_remote_copy(
            src_ref=source, dst_ref=target, send_sem=semaphores[0].at[0], recv_sem=semaphores[1].at[index],
            device_id=device, device_id_type=MESH,
        )

    def held_ref(spot, at_rows):
        return held.at[places[spot], span(at_rows), :]

    def block_ref(move, at, parity):
        kind, which = move.role[0], move.role[4]
        if kind == "rows":
            return rows.at[places[at]] if which is None else rows.at[places[at], pl.ds(64 * which, 64), :]
        z = {"mine": parity, "other": 1 - parity}.get(at[1], at[1])
        if which is None:
            return cols.at[groups[at[0], z]]
        size = 128 // PIECES
        return cols.at[groups[at[0], z], pl.ds(size * which, size), :]

    def outgoing(move, name, parity):
        if move.role is not None:
            place = block_ref(move, move.role[1], parity)
            return remote((send2, recv2), number[name], place, place, devices[move.role[3]])
        place = held_ref(move.source[parity], move.rows)
        device = step[move.link, parity] if move.link in "ud" else devices[move.link]
        return remote((send_sem, recv_sem), number[name], place, place, device)

    def incoming(move, name, parity):
        if move.role is not None:
            place = block_ref(move, move.role[2], parity)
            return remote((send2, recv2), number[name], place, place, sibling)
        place = held_ref(move.target, move.target_rows)
        return remote((send_sem, recv_sem), number[name], place, place, sibling)

    def lead(b, p):
        size = 128 // PIECES
        return leads.at[b, pl.ds(size * p, size), :]

    def lead_copy(kind, b, p, device, from_cols=False):
        size = 128 // PIECES
        return pltpu.make_async_remote_copy(
            src_ref=cols.at[0, pl.ds(size * p, size), :] if from_cols else lead(b, p), dst_ref=lead(b, p),
            send_sem=lead_send.at[kind * PIECES + p],
            recv_sem=lead_recv.at[b * PIECES + p],
            device_id=device, device_id_type=MESH,
        )

    def lead_arrive(b, p):
        lead_copy(0, b, p, sibling).wait_recv()

    def chain_role(hop, parity):
        if hop == 1:
            return at_z[0], step["u" if parity == 1 else "d", parity]
        upward = (hop == 2) == (parity == 0)
        return at_z[1 if upward else 3], step["u" if upward else "d", parity]

    relays = ((3, 0, "y-"), (2, 1, "y+"))

    def lead_start(role, parity):
        if role[0] == "chain":
            hop, p = role[1:]
            here, device = chain_role(hop, parity)

            @pl.when(here)
            def _():
                if hop > 1:
                    lead_arrive(y, p)
                lead_copy(0, y, p, device, hop == 1).start()
        elif role[0] == "spread":
            p = role[1]

            @pl.when(at_z[0])
            def _():
                lead_copy(1, y, p, devices["y+"], True).start()
                lead_copy(2, y, p, devices["y-"], True).start()

            @pl.when(at_z[2])
            def _():
                lead_arrive(y, p)

            @pl.when(past_first)
            def _():
                lead_copy(1, y, p, devices["y+"]).start()
                lead_copy(2, y, p, devices["y-"]).start()
        else:
            p = role[1]
            for k, b, way in relays:
                @pl.when(at_y[k])
                def _():
                    lead_arrive(b, p)
                    lead_copy(3, b, p, devices[way]).start()

    def lead_end(parity):
        for p in range(PIECES):
            for hop in (1, 2, 3):
                here, device = chain_role(hop, parity)

                @pl.when(here)
                def _():
                    lead_copy(0, y, p, device).wait_send()

            @pl.when(low)
            def _():
                lead_copy(1, y, p, devices["y+"]).wait_send()
                lead_copy(2, y, p, devices["y-"]).wait_send()

            for k, b, way in relays:
                @pl.when(at_y[k])
                def _():
                    lead_copy(3, b, p, devices[way]).wait_send()

    def side(index, source, target):
        return pltpu.make_async_remote_copy(
            src_ref=source, dst_ref=target, send_sem=side_send.at[index], recv_sem=side_recv.at[index],
            device_id=sibling, device_id_type=MESH,
        )

    def keep(index, source, target):
        return pltpu.make_async_copy(source, target, local_sem.at[index])

    shared = {}
    for k, h in enumerate(OFFSETS):
        shared["r", h] = (row_groups[h], k)
        shared["c", h] = (pairs[h], 4 + k)

    def side_refs(kind, d):
        if kind == "r":
            at = pl.ds(firsts[d], 4)
            return rows.at[at], (lambda t: rows_out.at[t, at])
        if kind == "c":
            return cols.at[pl.ds(groups[d, 0], 2)], (lambda t: cols_out.at[t, pl.ds(spots[d], 2)])
        if kind == "l":
            return leads, (lambda t: lead_out.at[t])
        return rows.at[col], (lambda t: own_out.at[t])

    def side_start(kind, d, index):
        source, target = side_refs(kind, d)
        if kind != "c":
            side(index, source, target(tok)).start()
            if kind != "r":
                keep(index, source, target(tok)).start()
            return

        @pl.when(keeps[d])
        def _():
            keep(index, source, target(tok)).start()

        @pl.when(jnp.logical_not(keeps[d]))
        def _():
            side(index, source, target(tok)).start()

    def side_end(kind, d, index):
        source, target = side_refs(kind, d)
        if kind != "c":
            side(index, target(1 - tok), target(1 - tok)).wait_recv()
            side(index, source, target(tok)).wait_send()
            if kind != "r":
                keep(index, source, target(tok)).wait()
            return

        @pl.when(keeps[d])
        def _():
            keep(index, source, target(tok)).wait()
            side(index, target(1 - tok), target(1 - tok)).wait_recv()

        @pl.when(jnp.logical_not(keeps[d]))
        def _():
            side(index, source, target(tok)).wait_send()

    def both(act):
        for parity in (0, 1):
            pl.when(z_lo == parity)(functools.partial(act, parity))

    def in_order(begun):
        return [sorted((begun[parity][name], name) for name in begun[parity]) for parity in (0, 1)]

    begun, landed = schedule(tokens)
    order = in_order(begun)
    seen, at = (set(), set()), [0, 0]

    def arrive(moves, name, parity):
        if name not in seen[parity]:
            seen[parity].add(name)
            if name in number:
                incoming(moves[name], name, parity).wait_recv()

    def stretch(until, batch, parity):
        while at[parity] < len(order[parity]) and order[parity][at[parity]][0] <= until:
            name = order[parity][at[parity]][1]
            at[parity] += 1
            for need in tokens[name].needs[parity]:
                arrive(tokens, need, parity)
            outgoing(tokens[name], name, parity).start()
        for chunk in batch:
            for need in ready[chunk]:
                arrive(tokens, need, parity)

    finished = {c: max(landed[p][name] for p in (0, 1) for name in ready[c]) for c in ready}
    queue = sorted(ready, key=lambda c: (finished[c], c))
    start = 0
    for k, size in enumerate(BATCHES):
        batch = queue[start:start + size]
        start += size
        until = max(finished[c] for c in batch) + AHEAD if start < len(queue) else 1e9
        both(functools.partial(stretch, until, batch))
        if k == 0:
            for load in loads:
                load.wait()
            total[...] = jnp.zeros_like(total)
        for here in ([col] if k == 0 else []) + [places[chunk] for chunk in batch]:
            total[...] += jnp.dot(held[here], weights[pl.ds(pl.multiple_of(here * 512, 512), 512), :], preferred_element_type=F32)

    def tokens_end(parity):
        for name in tokens:
            arrive(tokens, name, parity)

    both(tokens_end)
    gate = total[:, 0:128]
    hidden = gate / (1.0 + jnp.exp(-gate)) * total[:, 128:256]
    hidden = hidden.T.astype(jnp.bfloat16)
    rows[col] = hidden
    cols[row] = hidden

    begun, landed = schedule(hiddens)
    order = in_order(begun)
    left = (dict(shared), dict(shared))

    def hidden_stage(parity):
        waited = False
        for _, name in order[parity]:
            move = hiddens[name]
            if move.needs[parity] and not waited:
                waited = True
                side_start("o", 0, 8)
            for need in move.needs[parity]:
                arrive(hiddens, need, parity)
            if move.role[0] in ("rows", "cols"):
                outgoing(move, name, parity).start()
            else:
                lead_start(move.role, parity)
            for key in list(left[parity]):
                names, index = left[parity][key]
                if seen[parity].issuperset(names):
                    del left[parity][key]
                    side_start(*key, index)
        for key in list(left[parity]):
            names, index = left[parity].pop(key)
            for name in names:
                arrive(hiddens, name, parity)
            side_start(*key, index)
        for name in hiddens:
            arrive(hiddens, name, parity)

    both(hidden_stage)
    keep_rows = keep(0, rows, rows_out.at[tok])
    keep_rows.start()
    held_lead = pltpu.make_async_copy(cols.at[0], leads.at[lax.rem(y, 2)], local_sem.at[10])

    @pl.when(at_z[0])
    def _():
        held_lead.start()

    for p in range(PIECES):
        for k, b in ((0, 1), (1, 0), (2, 0), (3, 1)):
            @pl.when(at_y[k])
            def _():
                lead_arrive(b, p)

    @pl.when(at_z[0])
    def _():
        held_lead.wait()

    side_start("l", 0, 9)

    remote((send_sem, recv_sem), 0, held.at[pl.ds(0, 15)], held.at[pl.ds(0, 15)], sibling).wait_send()
    gone = weights.at[pl.ds(0, 5632), :]
    remote((send2, recv2), 0, gone, gone, sibling).wait_send()
    both(lead_end)
    keep_rows.wait()
    for kind, d in shared:
        side_end(kind, d, shared[kind, d][1])
    side_end("o", 0, 8)
    side_end("l", 0, 9)


def gather(tokens, gate_weight, up_weight):
    depth, width = gate_weight.shape
    half = tokens.shape[0]
    bf16 = jnp.bfloat16
    hbm = pl.BlockSpec(memory_space=pl.ANY)
    return pl.pallas_call(
        gather_kernel,
        out_shape=(
            jax.ShapeDtypeStruct((2, 16, width, half), bf16),
            jax.ShapeDtypeStruct((2, 4, width, half), bf16),
            jax.ShapeDtypeStruct((2, 2, width, half), bf16),
            jax.ShapeDtypeStruct((2, width, half), bf16),
        ),
        in_specs=[hbm, hbm, hbm],
        out_specs=(hbm,) * 4,
        scratch_shapes=[
            pltpu.VMEM((16, half, 512), bf16),
            pltpu.VMEM((depth, 2 * width), bf16),
            pltpu.VMEM((half, 2 * width), F32),
            pltpu.VMEM((16, width, half), bf16),
            pltpu.VMEM((8, width, half), bf16),
            pltpu.VMEM((2, width, half), bf16),
            pltpu.SemaphoreType.DMA((3,)),
            pltpu.SemaphoreType.DMA((1,)),
            pltpu.SemaphoreType.DMA((120,)),
            pltpu.SemaphoreType.DMA((1,)),
            pltpu.SemaphoreType.DMA((55,)),
            pltpu.SemaphoreType.DMA((10,)),
            pltpu.SemaphoreType.DMA((10,)),
            pltpu.SemaphoreType.DMA((4 * PIECES,)),
            pltpu.SemaphoreType.DMA((2 * PIECES,)),
            pltpu.SemaphoreType.DMA((11,)),
        ],
        compiler_params=pltpu.CompilerParams(
            collective_id=0, has_side_effects=True, vmem_limit_bytes=60 * 2**20
        ),
        cost_estimate=pl.CostEstimate(flops=2 * half * depth * 2 * width, bytes_accessed=12 * 2**20, transcendentals=half * width),
    )(tokens, gate_weight, up_weight)


def gram_kernel(rows_ref, cols_ref, lead_ref, own_ref, gram_ref, panel_ref, u):
    step = pl.program_id(0)

    def product(left, right):
        return sum(lax.dot_general(left(t), right(t), NT, preferred_element_type=F32) for t in (0, 1))

    def tile():
        whole = product(lambda t: rows_ref[t].reshape(256, 512), lambda t: cols_ref[t].reshape(512, 512))
        for a in range(4):
            gram_ref[a] = whole[:, 128 * a:128 * a + 128]

    @pl.when(step == 0)
    def _():
        def lead(t):
            return lead_ref[t].reshape(256, 512)

        u[:, 0:256] = product(lead, lead)
        u[:, 256:384] = product(lead, lambda t: own_ref[t])
        balance(u)

    for k in range(8):
        @pl.when(step == k)
        def _():
            tile()
            eliminate(u, k)

    @pl.when(step == 7)
    def _():
        panel_ref[...] = u[pl.ds(pl.multiple_of(lax.axis_index("tok") * 128, 128), 128), 256:384].T


def gram_and_panel(rows, cols, lead, own):
    width, half = rows.shape[2:]
    return pl.pallas_call(
        gram_kernel,
        grid=(8,),
        out_shape=(
            jax.ShapeDtypeStruct((4, 16 * width, width), F32),
            jax.ShapeDtypeStruct((width, width), F32),
        ),
        in_specs=[
            pl.BlockSpec((2, 2, width, half), lambda s: (0, s, 0, 0)),
            pl.BlockSpec((2, 4, width, half), lambda s: (0, 0, 0, 0)),
            pl.BlockSpec((2, 2, width, half), lambda s: (0, 0, 0, 0)),
            pl.BlockSpec((2, width, half), lambda s: (0, 0, 0)),
        ],
        out_specs=(
            pl.BlockSpec((4, 2 * width, width), lambda s: (0, s, 0)),
            pl.BlockSpec((width, width), lambda s: (0, 0)),
        ),
        scratch_shapes=[pltpu.VMEM((PANEL, 384), F32)],
        compiler_params=pltpu.CompilerParams(vmem_limit_bytes=60 * 2**20),
        cost_estimate=pl.CostEstimate(flops=2 * 2048 * 512 * 1024, bytes_accessed=10 * 2**20, transcendentals=0),
    )(rows, cols, lead, own)


def local(tokens, gate_weight, up_weight):
    gram, panel = gram_and_panel(*gather(tokens, gate_weight, up_weight))
    return (gram.reshape(4, 2048, 1, 128), panel)


def solution(mesh):
    placed = (P("tok", "col"), P(None, ("row", "col")), P(None, ("row", "col")))
    return jax.shard_map(
        local,
        mesh=mesh,
        in_specs=placed,
        out_specs=(P("tok", "row", "col", None), P(("row", "col"), "tok")),
        check_vma=False,
    )
```

```python
import functools

import jax
import jax.numpy as jnp
from jax import lax
from jax.experimental import pallas as pl
from jax.experimental.pallas import tpu as pltpu
from jax.sharding import PartitionSpec as P

PANEL = 256
HIGH = lax.Precision.HIGHEST
MESH = pl.DeviceIdType.MESH
OFFSETS = (0, -1, 1, 2)
NT = (((1,), (1,)), ((), ()))
F32 = jnp.float32

ROWS = 512
QUARTER = 64
FIRST_Y = (256, 96)
FIRST_Z = (352, 160)
PIECES = 4
BATCHES = (2, 2, 2, 2, 2, 2, 1, 1, 1)
RATE, HOP, ISSUE, AHEAD = 49.0, 2.3, 0.14, 1.5


class Move:
    def __init__(self, link, size, needs, source=None, target=None, rows=None, target_rows=None, role=None):
        self.link, self.size, self.needs = link, size, needs
        self.source, self.target, self.rows, self.target_rows, self.role = source, target, rows, target_rows, role


def part(rows, which):
    first = (rows[2] // 2 + 15) // 16 * 16
    return (rows[0], rows[1] + first, rows[2] - first) if which == "b" else (rows[0], rows[1], first)


def token_moves():
    moves, arrivals = {}, {}

    def add(name, link, needs0, needs1, source, target, rows, target_rows=None):
        moves[name] = Move(link, rows[2], (tuple(needs0), tuple(needs1)), source, target, rows, target_rows or rows)

    def along_z(tag, rows, j, have):
        up, far_up, down, far_down = [tag + k for k in ("u1", "u2", "d1", "d2")]
        at = {h: (h, j) for h in OFFSETS}
        add(up, "u", [up], have, (at[-1], at[0]), at[-1], rows)
        add(far_up, "u", [far_up], [up], (at[2], at[-1]), at[2], part(rows, "a"))
        add(down, "d", have, [down], (at[0], at[1]), at[1], rows)
        add(far_down, "d", [down], [far_down], (at[1], at[2]), at[2], part(rows, "b"))
        return {0: list(have), -1: [up], 1: [down], 2: [far_up, far_down]}

    def along_y(tag, rows, h, have):
        right, left, far_right, far_left = [tag + k for k in ("y+1", "y-1", "y+2", "y-2")]
        at = {j: (h, j) for j in OFFSETS}
        add(right, "y+", have, have, (at[0],) * 2, at[-1], rows)
        add(left, "y-", have, have, (at[0],) * 2, at[1], rows)
        add(far_right, "y+", [right], [right], (at[-1],) * 2, at[2], part(rows, "a"))
        add(far_left, "y-", [left], [left], (at[1],) * 2, at[2], part(rows, "b"))
        return {0: list(have), -1: [right], 1: [left], 2: [far_right, far_left]}

    for tag, rows in (("q", (0, 0, QUARTER)), ("f", (None,) + FIRST_Y)):
        near = along_y(tag, rows, 0, [])
        for j in OFFSETS:
            for h, names in along_z(tag + "%d" % j, rows, j, near[j]).items():
                arrivals[tag, h, j] = names
    near = along_z("s", (None,) + FIRST_Z, 0, [])
    for h in OFFSETS:
        for j, names in along_y("s%d" % h, (None,) + FIRST_Z, h, near[h]).items():
            arrivals["s", h, j] = names
    ready = {}
    own, before, after, across = [(d, 0, QUARTER) for d in (0, -1, 1, 2)]
    for spot in [(h, j) for h in OFFSETS for j in OFFSETS][1:]:
        have = arrivals[("q",) + spot]
        right, left, far_right, far_left = ["x%d,%d" % spot + k for k in ("x+1", "x-1", "x+2", "x-2")]
        add(right, "x+", have, have, (spot,) * 2, spot, own, before)
        add(left, "x-", have, have, (spot,) * 2, spot, own, after)
        add(far_right, "x+", [right], [right], (spot,) * 2, spot, part(before, "a"), part(across, "a"))
        add(far_left, "x-", [left], [left], (spot,) * 2, spot, part(after, "b"), part(across, "b"))
        ready[spot] = [n for kind in "qfs" for n in arrivals[(kind,) + spot]] + [right, left, far_right, far_left]
    return moves, ready


def hidden_moves():
    moves, piece, block = {}, 128 // PIECES, 128
    every = range(PIECES)

    def add(name, link, size, needs, role):
        moves[name] = Move(link, size, (tuple(needs),) * 2, role=role)

    for p in every:
        add("zl%d" % p, "zl", piece, [], ("cols", (0, "mine"), (0, "other"), "zl", p))
        for sign, d in (("+", 1), ("-", -1)):
            add("xo%s%d" % (sign, p), "x" + sign, piece, [], ("cols", (0, "mine"), (-d, "mine"), "x" + sign, p))
            add("xp%s%d" % (sign, p), "x" + sign, piece, ["zl%d" % p], ("cols", (0, "other"), (-d, "other"), "x" + sign, p))
        add("xr+%d" % p, "x+", piece, ["xo+%d" % p, "xp+%d" % p], ("cols", (-1, 0), (2, 0), "x+", p))
    add("xr-", "x-", block, ["x%s-%d" % (k, p) for k in "op" for p in every], ("cols", (1, 1), (2, 1), "x-", None))
    gone = {0: ([], []), -1: (["za+"], ["zb+"]), 1: (["za-"], ["zb-"]), 2: (["zr+"], ["zr-"])}
    for relayed, (sign, d) in enumerate((("+", 1), ("-", -1))):
        link = "u" if d == 1 else "d"
        for which, half in enumerate("ab"):
            add("z" + half + sign, link, block, [], ("rows", (0, 0), (-d, 0), "z" + sign, which))
            for h in OFFSETS:
                add("y%d" % h + half + sign, "y" + sign, block // 2, gone[h][which], ("rows", (h, 0), (h, -d), "y" + sign, which))
        add("zr" + sign, link, block, ["z" + "ab"[relayed] + sign], ("rows", (-d, 0), (2, 0), "z" + sign, relayed))
        for h in OFFSETS:
            need = ["y%d" % h + "ab"[relayed] + sign]
            add("y%dr" % h + sign, "y" + sign, block // 2, need, ("rows", (h, -d), (h, 2), "y" + sign, relayed))
    for p in every:
        first = [name % p for name in ("zl%d", "xo+%d", "xo-%d", "xp+%d", "xp-%d", "xr+%d")]
        for hop in (1, 2, 3):
            add("c%d%d" % (hop, p), "c%d" % hop, piece, first if hop == 1 else ["c%d%d" % (hop - 1, p)], ("chain", hop, p))
        add("l%d" % p, "l", piece, ["c3%d" % p], ("spread", p))
        add("m%d" % p, "m", piece, ["l%d" % p], ("relay", p))
    row_groups = {h: gone[h][0] + gone[h][1] + ["y%d" % h + k + sign for k in "abr" for sign in "+-"] for h in OFFSETS}
    pairs = {0: ["zl%d" % p for p in every], 2: ["xr-"] + ["xr+%d" % p for p in every]}
    for sign, d in (("+", -1), ("-", 1)):
        pairs[d] = ["x%s%s%d" % (k, sign, p) for k in "op" for p in every]
    return moves, row_groups, pairs


def schedule(moves):
    followers = {name: set() for name in moves}
    for name, move in moves.items():
        for parity in (0, 1):
            for need in move.needs[parity]:
                followers[need].add((name, parity))

    def there(name, parity):
        return 1 - parity if moves[name].role is None and moves[name].link in "ud" else parity

    @functools.lru_cache(None)
    def rest(name, parity):
        after = [moves[m].size / RATE + HOP + rest(m, there(m, q)) for m, q in followers[name] if q == parity]
        return max(after, default=0.0)

    landed, begun, free = ({}, {}), ({}, {}), {}
    waiting = {(name, parity) for name in moves for parity in (0, 1)}
    while waiting:
        best = None
        for name, parity in waiting:
            move, have = moves[name], landed[parity]
            when = max(free.get((move.link, parity), 0.0), free.get(parity, 0.0))
            for need in move.needs[parity]:
                if need not in have:
                    break
                when = max(when, have[need])
            else:
                key = (when, -(rest(name, there(name, parity)) + move.size / RATE), name, parity)
                if best is None or key < best:
                    best = key
        when, _, name, parity = best
        done = when + moves[name].size / RATE
        free[moves[name].link, parity] = done
        free[parity] = when + ISSUE
        begun[parity][name] = when
        landed[there(name, parity)][name] = done + HOP
        waiting.discard((name, parity))
    return begun, landed


def balance(u):
    rows = lax.broadcasted_iota(jnp.int32, (PANEL, PANEL), 0)
    lanes = lax.broadcasted_iota(jnp.int32, (PANEL, PANEL), 1)
    corner = u[:, 0:PANEL]
    only = jnp.where(rows == lanes, corner, 0.0)
    down, across = lax.rsqrt(jnp.sum(only, axis=1, keepdims=True)), lax.rsqrt(jnp.sum(only, axis=0, keepdims=True))
    u[:, 0:PANEL] = corner * down * across
    u[:, PANEL:] = u[:, PANEL:] * down


def eliminate(u, piece):
    wide = lax.broadcasted_iota(jnp.int32, (8, 384), 0)
    base = 64 * (piece // 2)
    groups = [u[base + 8 * g:base + 8 * g + 8, :] for g in range(8)]

    def spread(row, at):
        return jnp.broadcast_to(row[at:at + 1, :], (8, row.shape[1]))

    def thrice(tile):
        return jnp.concatenate([tile] * 3, axis=1)

    for p in range(4 * (piece % 2), 4 * (piece % 2) + 4):
        cols = {
            (g, k): jnp.broadcast_to(groups[g][:, base + 8 * p + k:base + 8 * p + k + 1], (8, 128))
            for g in range(p, 8) for k in range(8)
        }
        for k in range(0, 8, 2):
            a, b, c = spread(cols[p, k], k), spread(cols[p, k + 1], k), spread(cols[p, k + 1], k + 1)
            root = lax.rsqrt(a * c - b * b)
            over = root * root
            left, right = [], []
            for g in range(p, 8):
                left.append((c * cols[g, k] - b * cols[g, k + 1]) * over)
                right.append((a * cols[g, k + 1] - b * cols[g, k]) * over)
            for j in range(k + 2, 8):
                one, two = spread(cols[p, k], j), spread(cols[p, k + 1], j)
                for g in range(p, 8):
                    cols[g, j] = cols[g, j] - (left[g - p] * one + right[g - p] * two)
            first = lax.rsqrt(a)
            ratio = b * first * first
            second = lax.rsqrt(c - b * ratio)
            line, below = spread(groups[p], k), spread(groups[p], k + 1)
            top = line * thrice(first)
            low = (below - thrice(ratio) * line) * thrice(second)
            rest = groups[p] - (thrice(left[0]) * line + thrice(right[0]) * below)
            groups[p] = jnp.where(wide == k, top, jnp.where(wide == k + 1, low, jnp.where(wide > k + 1, rest, groups[p])))
            for g in range(p, 8):
                cols[g, k + 1] = (cols[g, k + 1] - ratio * cols[g, k]) * second
                cols[g, k] = cols[g, k] * first
        lines = [spread(groups[p], k) for k in range(8)]
        for g in range(p + 1, 8):
            acc = groups[g]
            for k in range(8):
                acc = acc - thrice(cols[g, k]) * lines[k]
            groups[g] = acc
    for g in range(4 * (piece % 2), 8):
        u[base + 8 * g:base + 8 * g + 8, :] = groups[g]
    if piece % 2 and piece < 7:
        block = u[base:base + 64, :]
        first = 0 if base == 0 else 128
        update = jnp.dot(block[:, first:256].T, block, precision=HIGH, preferred_element_type=F32)
        rest = base + 64
        u[rest:256, :] = u[rest:256, :] - update[rest - first:256 - first, :]


def gather_kernel(
    tokens_hbm, gate_hbm, up_hbm, rows_out, cols_out, lead_out, own_out,
    held, weights, total, rows, cols, leads,
    load_sem, send_sem, recv_sem, send2, recv2, side_send, side_recv, lead_send, lead_recv, local_sem,
):
    tok, row, col = lax.axis_index("tok"), lax.axis_index("row"), lax.axis_index("col")
    x, z_lo, z_hi, y = lax.div(row, 2), lax.rem(row, 2), lax.div(col, 4), lax.rem(col, 4)

    def around(at):
        return {0: at, 1: lax.rem(at + 1, 4), 2: lax.rem(at + 2, 4), -1: lax.rem(at + 3, 4)}

    xs, zs, ys = around(x), around(z_hi), around(y)
    places = {(h, j): zs[h] * 4 + ys[j] for h in OFFSETS for j in OFFSETS}
    quarters = {d: xs[d] * QUARTER for d in OFFSETS}
    groups = {(d, z): xs[d] * 2 + z for d in OFFSETS for z in (0, 1)}
    firsts = {h: zs[h] * 4 for h in OFFSETS}
    spots = {d: lax.rem(xs[d], 2) * 2 for d in OFFSETS}
    keeps = {d: lax.div(xs[d], 2) == tok for d in OFFSETS}
    partner_row = x * 2 + 1 - z_lo

    devices = {"zl": (tok, partner_row, col)}
    for sign, d in (("+", 1), ("-", -1)):
        devices["x" + sign] = (tok, xs[d] * 2 + z_lo, col)
        devices["y" + sign] = (tok, row, places[0, d])
        devices["z" + sign] = (tok, row, places[d, 0])
    sibling = (1 - tok, row, col)
    step = {
        ("u", 0): devices["zl"], ("u", 1): (tok, partner_row, places[1, 0]),
        ("d", 0): (tok, partner_row, places[-1, 0]), ("d", 1): devices["zl"],
    }
    low = y < 2
    at_z = {k: jnp.logical_and(low, z_hi == k) for k in range(4)}
    past_first = jnp.logical_and(low, z_hi > 0)
    at_y = {k: y == k for k in range(4)}

    first = pltpu.make_async_copy(tokens_hbm, held.at[col], load_sem.at[2])
    first.start()
    loads = [
        pltpu.make_async_copy(gate_hbm, weights.at[:, 0:128], load_sem.at[0]),
        pltpu.make_async_copy(up_hbm, weights.at[:, 128:256], load_sem.at[1]),
    ]
    for load in loads:
        load.start()

    barrier = pltpu.get_barrier_semaphore()
    far = (tok, partner_row, places[1, 0] * z_lo + places[-1, 0] * (1 - z_lo))
    near = [devices[k] for k in ("x+", "x-", "y+", "y-", "z+", "z-", "zl")] + [far, sibling]
    for device in near:
        pl.semaphore_signal(barrier, inc=1, device_id=device, device_id_type=MESH)
    pl.semaphore_wait(barrier, len(near))
    first.wait()

    tokens, ready = token_moves()
    hiddens, row_groups, pairs = hidden_moves()
    number = {name: at for at, name in enumerate(tokens)}
    number.update({name: at for at, name in enumerate(n for n in hiddens if hiddens[n].role[0] in ("rows", "cols"))})

    def span(at_rows):
        if at_rows[0] is None:
            return pl.ds(at_rows[1], at_rows[2])
        return pl.ds(pl.multiple_of(quarters[at_rows[0]] + at_rows[1], 16), at_rows[2])

    def remote(semaphores, index, source, target, device):
        return pltpu.make_async_remote_copy(
            src_ref=source, dst_ref=target, send_sem=semaphores[0].at[0], recv_sem=semaphores[1].at[index],
            device_id=device, device_id_type=MESH,
        )

    def held_ref(spot, at_rows):
        return held.at[places[spot], span(at_rows), :]

    def block_ref(move, at, parity):
        kind, which = move.role[0], move.role[4]
        if kind == "rows":
            return rows.at[places[at]] if which is None else rows.at[places[at], pl.ds(64 * which, 64), :]
        z = {"mine": parity, "other": 1 - parity}.get(at[1], at[1])
        if which is None:
            return cols.at[groups[at[0], z]]
        size = 128 // PIECES
        return cols.at[groups[at[0], z], pl.ds(size * which, size), :]

    def outgoing(move, name, parity):
        if move.role is not None:
            place = block_ref(move, move.role[1], parity)
            return remote((send2, recv2), number[name], place, place, devices[move.role[3]])
        place = held_ref(move.source[parity], move.rows)
        device = step[move.link, parity] if move.link in "ud" else devices[move.link]
        return remote((send_sem, recv_sem), number[name], place, place, device)

    def incoming(move, name, parity):
        if move.role is not None:
            place = block_ref(move, move.role[2], parity)
            return remote((send2, recv2), number[name], place, place, sibling)
        place = held_ref(move.target, move.target_rows)
        return remote((send_sem, recv_sem), number[name], place, place, sibling)

    def lead(b, p):
        size = 128 // PIECES
        return leads.at[b, pl.ds(size * p, size), :]

    def lead_copy(kind, b, p, device, from_cols=False):
        size = 128 // PIECES
        return pltpu.make_async_remote_copy(
            src_ref=cols.at[0, pl.ds(size * p, size), :] if from_cols else lead(b, p), dst_ref=lead(b, p),
            send_sem=lead_send.at[kind * PIECES + p],
            recv_sem=lead_recv.at[b * PIECES + p],
            device_id=device, device_id_type=MESH,
        )

    def lead_arrive(b, p):
        lead_copy(0, b, p, sibling).wait_recv()

    def chain_role(hop, parity):
        if hop == 1:
            return at_z[0], step["u" if parity == 1 else "d", parity]
        upward = (hop == 2) == (parity == 0)
        return at_z[1 if upward else 3], step["u" if upward else "d", parity]

    relays = ((3, 0, "y-"), (2, 1, "y+"))

    def lead_start(role, parity):
        if role[0] == "chain":
            hop, p = role[1:]
            here, device = chain_role(hop, parity)

            @pl.when(here)
            def _():
                if hop > 1:
                    lead_arrive(y, p)
                lead_copy(0, y, p, device, hop == 1).start()
        elif role[0] == "spread":
            p = role[1]

            @pl.when(at_z[0])
            def _():
                lead_copy(1, y, p, devices["y+"], True).start()
                lead_copy(2, y, p, devices["y-"], True).start()

            @pl.when(at_z[2])
            def _():
                lead_arrive(y, p)

            @pl.when(past_first)
            def _():
                lead_copy(1, y, p, devices["y+"]).start()
                lead_copy(2, y, p, devices["y-"]).start()
        else:
            p = role[1]
            for k, b, way in relays:
                @pl.when(at_y[k])
                def _():
                    lead_arrive(b, p)
                    lead_copy(3, b, p, devices[way]).start()

    def lead_end(parity):
        for p in range(PIECES):
            for hop in (1, 2, 3):
                here, device = chain_role(hop, parity)

                @pl.when(here)
                def _():
                    lead_copy(0, y, p, device).wait_send()

            @pl.when(low)
            def _():
                lead_copy(1, y, p, devices["y+"]).wait_send()
                lead_copy(2, y, p, devices["y-"]).wait_send()

            for k, b, way in relays:
                @pl.when(at_y[k])
                def _():
                    lead_copy(3, b, p, devices[way]).wait_send()

    def side(index, source, target):
        return pltpu.make_async_remote_copy(
            src_ref=source, dst_ref=target, send_sem=side_send.at[index], recv_sem=side_recv.at[index],
            device_id=sibling, device_id_type=MESH,
        )

    def keep(index, source, target):
        return pltpu.make_async_copy(source, target, local_sem.at[index])

    shared = {}
    for k, h in enumerate(OFFSETS):
        shared["r", h] = (row_groups[h], k)
        shared["c", h] = (pairs[h], 4 + k)

    def side_refs(kind, d):
        if kind == "r":
            at = pl.ds(firsts[d], 4)
            return rows.at[at], (lambda t: rows_out.at[t, at])
        if kind == "c":
            return cols.at[pl.ds(groups[d, 0], 2)], (lambda t: cols_out.at[t, pl.ds(spots[d], 2)])
        if kind == "l":
            return leads, (lambda t: lead_out.at[t])
        return rows.at[col], (lambda t: own_out.at[t])

    def side_start(kind, d, index):
        source, target = side_refs(kind, d)
        if kind != "c":
            side(index, source, target(tok)).start()
            if kind != "r":
                keep(index, source, target(tok)).start()
            return

        @pl.when(keeps[d])
        def _():
            keep(index, source, target(tok)).start()

        @pl.when(jnp.logical_not(keeps[d]))
        def _():
            side(index, source, target(tok)).start()

    def side_end(kind, d, index):
        source, target = side_refs(kind, d)
        if kind != "c":
            side(index, target(1 - tok), target(1 - tok)).wait_recv()
            side(index, source, target(tok)).wait_send()
            if kind != "r":
                keep(index, source, target(tok)).wait()
            return

        @pl.when(keeps[d])
        def _():
            keep(index, source, target(tok)).wait()
            side(index, target(1 - tok), target(1 - tok)).wait_recv()

        @pl.when(jnp.logical_not(keeps[d]))
        def _():
            side(index, source, target(tok)).wait_send()

    def both(act):
        for parity in (0, 1):
            pl.when(z_lo == parity)(functools.partial(act, parity))

    def in_order(begun):
        return [sorted((begun[parity][name], name) for name in begun[parity]) for parity in (0, 1)]

    begun, landed = schedule(tokens)
    order = in_order(begun)
    seen, at = (set(), set()), [0, 0]

    def arrive(moves, name, parity):
        if name not in seen[parity]:
            seen[parity].add(name)
            if name in number:
                incoming(moves[name], name, parity).wait_recv()

    def stretch(until, batch, parity):
        while at[parity] < len(order[parity]) and order[parity][at[parity]][0] <= until:
            name = order[parity][at[parity]][1]
            at[parity] += 1
            for need in tokens[name].needs[parity]:
                arrive(tokens, need, parity)
            outgoing(tokens[name], name, parity).start()
        for chunk in batch:
            for need in ready[chunk]:
                arrive(tokens, need, parity)

    finished = {c: max(landed[p][name] for p in (0, 1) for name in ready[c]) for c in ready}
    queue = sorted(ready, key=lambda c: (finished[c], c))
    start = 0
    for k, size in enumerate(BATCHES):
        batch = queue[start:start + size]
        start += size
        until = max(finished[c] for c in batch) + AHEAD if start < len(queue) else 1e9
        both(functools.partial(stretch, until, batch))
        if k == 0:
            for load in loads:
                load.wait()
            total[...] = jnp.zeros_like(total)
        for here in ([col] if k == 0 else []) + [places[chunk] for chunk in batch]:
            total[...] += jnp.dot(held[here], weights[pl.ds(pl.multiple_of(here * 512, 512), 512), :], preferred_element_type=F32)

    def tokens_end(parity):
        for name in tokens:
            arrive(tokens, name, parity)

    both(tokens_end)
    gate = total[:, 0:128]
    hidden = gate / (1.0 + jnp.exp(-gate)) * total[:, 128:256]
    hidden = hidden.T.astype(jnp.bfloat16)
    rows[col] = hidden
    cols[row] = hidden

    begun, landed = schedule(hiddens)
    order = in_order(begun)
    left = (dict(shared), dict(shared))

    def hidden_stage(parity):
        waited = False
        for _, name in order[parity]:
            move = hiddens[name]
            if move.needs[parity] and not waited:
                waited = True
                side_start("o", 0, 8)
            for need in move.needs[parity]:
                arrive(hiddens, need, parity)
            if move.role[0] in ("rows", "cols"):
                outgoing(move, name, parity).start()
            else:
                lead_start(move.role, parity)
            for key in list(left[parity]):
                names, index = left[parity][key]
                if seen[parity].issuperset(names):
                    del left[parity][key]
                    side_start(*key, index)
        for key in list(left[parity]):
            names, index = left[parity].pop(key)
            for name in names:
                arrive(hiddens, name, parity)
            side_start(*key, index)
        for name in hiddens:
            arrive(hiddens, name, parity)

    both(hidden_stage)
    keep_rows = keep(0, rows, rows_out.at[tok])
    keep_rows.start()
    held_lead = pltpu.make_async_copy(cols.at[0], leads.at[lax.rem(y, 2)], local_sem.at[10])

    @pl.when(at_z[0])
    def _():
        held_lead.start()

    for p in range(PIECES):
        for k, b in ((0, 1), (1, 0), (2, 0), (3, 1)):
            @pl.when(at_y[k])
            def _():
                lead_arrive(b, p)

    @pl.when(at_z[0])
    def _():
        held_lead.wait()

    side_start("l", 0, 9)

    remote((send_sem, recv_sem), 0, held.at[pl.ds(0, 15)], held.at[pl.ds(0, 15)], sibling).wait_send()
    gone = weights.at[pl.ds(0, 5632), :]
    remote((send2, recv2), 0, gone, gone, sibling).wait_send()
    both(lead_end)
    keep_rows.wait()
    for kind, d in shared:
        side_end(kind, d, shared[kind, d][1])
    side_end("o", 0, 8)
    side_end("l", 0, 9)


def gather(tokens, gate_weight, up_weight):
    depth, width = gate_weight.shape
    half = tokens.shape[0]
    bf16 = jnp.bfloat16
    hbm = pl.BlockSpec(memory_space=pl.ANY)
    return pl.pallas_call(
        gather_kernel,
        out_shape=(
            jax.ShapeDtypeStruct((2, 16, width, half), bf16),
            jax.ShapeDtypeStruct((2, 4, width, half), bf16),
            jax.ShapeDtypeStruct((2, 2, width, half), bf16),
            jax.ShapeDtypeStruct((2, width, half), bf16),
        ),
        in_specs=[hbm, hbm, hbm],
        out_specs=(hbm,) * 4,
        scratch_shapes=[
            pltpu.VMEM((16, half, 512), bf16),
            pltpu.VMEM((depth, 2 * width), bf16),
            pltpu.VMEM((half, 2 * width), F32),
            pltpu.VMEM((16, width, half), bf16),
            pltpu.VMEM((8, width, half), bf16),
            pltpu.VMEM((2, width, half), bf16),
            pltpu.SemaphoreType.DMA((3,)),
            pltpu.SemaphoreType.DMA((1,)),
            pltpu.SemaphoreType.DMA((120,)),
            pltpu.SemaphoreType.DMA((1,)),
            pltpu.SemaphoreType.DMA((55,)),
            pltpu.SemaphoreType.DMA((10,)),
            pltpu.SemaphoreType.DMA((10,)),
            pltpu.SemaphoreType.DMA((4 * PIECES,)),
            pltpu.SemaphoreType.DMA((2 * PIECES,)),
            pltpu.SemaphoreType.DMA((11,)),
        ],
        compiler_params=pltpu.CompilerParams(
            collective_id=0, has_side_effects=True, vmem_limit_bytes=60 * 2**20
        ),
        cost_estimate=pl.CostEstimate(flops=2 * half * depth * 2 * width, bytes_accessed=12 * 2**20, transcendentals=half * width),
    )(tokens, gate_weight, up_weight)


def gram_kernel(rows_ref, cols_ref, lead_ref, own_ref, gram_ref, panel_ref, u):
    step = pl.program_id(0)

    def product(left, right):
        return sum(lax.dot_general(left(t), right(t), NT, preferred_element_type=F32) for t in (0, 1))

    def tile():
        whole = product(lambda t: rows_ref[t].reshape(256, 512), lambda t: cols_ref[t].reshape(512, 512))
        for a in range(4):
            gram_ref[a] = whole[:, 128 * a:128 * a + 128]

    @pl.when(step == 0)
    def _():
        def lead(t):
            return lead_ref[t].reshape(256, 512)

        u[:, 0:256] = product(lead, lead)
        u[:, 256:384] = product(lead, lambda t: own_ref[t])
        balance(u)

    for k in range(8):
        @pl.when(step == k)
        def _():
            tile()
            eliminate(u, k)

    @pl.when(step == 7)
    def _():
        panel_ref[...] = u[pl.ds(pl.multiple_of(lax.axis_index("tok") * 128, 128), 128), 256:384].T


def gram_and_panel(rows, cols, lead, own):
    width, half = rows.shape[2:]
    return pl.pallas_call(
        gram_kernel,
        grid=(8,),
        out_shape=(
            jax.ShapeDtypeStruct((4, 16 * width, width), F32),
            jax.ShapeDtypeStruct((width, width), F32),
        ),
        in_specs=[
            pl.BlockSpec((2, 2, width, half), lambda s: (0, s, 0, 0)),
            pl.BlockSpec((2, 4, width, half), lambda s: (0, 0, 0, 0)),
            pl.BlockSpec((2, 2, width, half), lambda s: (0, 0, 0, 0)),
            pl.BlockSpec((2, width, half), lambda s: (0, 0, 0)),
        ],
        out_specs=(
            pl.BlockSpec((4, 2 * width, width), lambda s: (0, s, 0)),
            pl.BlockSpec((width, width), lambda s: (0, 0)),
        ),
        scratch_shapes=[pltpu.VMEM((PANEL, 384), F32)],
        compiler_params=pltpu.CompilerParams(vmem_limit_bytes=60 * 2**20),
        cost_estimate=pl.CostEstimate(flops=2 * 2048 * 512 * 1024, bytes_accessed=10 * 2**20, transcendentals=0),
    )(rows, cols, lead, own)


def local(tokens, gate_weight, up_weight):
    gram, panel = gram_and_panel(*gather(tokens, gate_weight, up_weight))
    return (gram.reshape(4, 2048, 1, 128), panel)


def solution(mesh):
    placed = (P("tok", "col"), P(None, ("row", "col")), P(None, ("row", "col")))
    return jax.shard_map(
        local,
        mesh=mesh,
        in_specs=placed,
        out_specs=(P("tok", "row", "col", None), P(("row", "col"), "tok")),
        check_vma=False,
    )
```
